32 devices in a mesh: head: 2 (over x), blk: 16 (over z, y, core).
Axes of the slice: x: 2, y: 2, z: 4, core: 2. Of those that a mesh axis runs over, the one named last changes fastest.
Arguments:
- tokens: bfloat16 [2, 2048, 1536], P(None, ('head', 'blk')), may hold values from -10 to 10
- cotangent: bfloat16 [2, 2048, 1536], P(None, ('head', 'blk')), may hold values from -6 to 6
- lengths: int32 [2], replicated, may hold values from 1792 to 2048, as said below
- routes: int32 [2048, 2, 6], P(('head', 'blk')), may hold values from 0 to 15, all different within a row; in each aligned block of 128 rows (0 to 127, 128 to 255, ..., all dimensions but the last counted through in order) at most 96 rows name the same one
- w_qkv: float32 [1536, 2560], P(('head', 'blk')), may hold values from -0.15625 to 0.15625
- m_qkv: float32 [1536, 2560], P(('head', 'blk')), may hold values from -9.1552734e-05 to 9.1552734e-05
- v_qkv: float32 [1536, 2560], P(('head', 'blk')), may hold values from 2.0497503e-11 to 8.199001e-11
- w_out: float32 [1536, 1536], P(('head', 'blk')), may hold values from -1.25 to 1.25
- m_out: float32 [1536, 1536], P(('head', 'blk')), may hold values from -3.0517578e-05 to 3.0517578e-05
- v_out: float32 [1536, 1536], P(('head', 'blk')), may hold values from 1.0248751e-12 to 4.0995003e-12
- w_shgu: float32 [1536, 2048], P(('head', 'blk')), may hold values from -0.15625 to 0.15625
- m_shgu: float32 [1536, 2048], P(('head', 'blk')), may hold values from -9.1552734e-05 to 9.1552734e-05
- v_shgu: float32 [1536, 2048], P(('head', 'blk')), may hold values from 2.0497503e-11 to 8.199001e-11
- w_shdown: float32 [1024, 1536], P(('head', 'blk')), may hold values from -0.1875 to 0.1875
- m_shdown: float32 [1024, 1536], P(('head', 'blk')), may hold values from -9.1552734e-05 to 9.1552734e-05
- v_shdown: float32 [1024, 1536], P(('head', 'blk')), may hold values from 2.0497503e-11 to 8.199001e-11
- w_router: float32 [1536, 16], P(('head', 'blk')), may hold values from -0.078125 to 0.078125
- m_router: float32 [1536, 16], P(('head', 'blk')), may hold values from -0.0014648438 to 0.0014648438
- v_router: float32 [1536, 16], P(('head', 'blk')), may hold values from 2.0497501e-09 to 3.2796002e-08
- w_gains: float32 [2, 1536], P(None, ('head', 'blk')), may hold values from 0.5 to 1.5
- m_gains: float32 [2, 1536], P(None, ('head', 'blk')), may hold values from -9.1552734e-05 to 9.1552734e-05
- v_gains: float32 [2, 1536], P(None, ('head', 'blk')), may hold values from 2.0497503e-11 to 8.199001e-11
- w_expgu: float32 [16, 1536, 1024], P('blk', 'head'), may hold values from -0.15625 to 0.15625
- m_expgu: float32 [16, 1536, 1024], P('blk', 'head'), may hold values from -9.1552734e-05 to 9.1552734e-05
- v_expgu: float32 [16, 1536, 1024], P('blk', 'head'), may hold values from 2.0497503e-11 to 8.199001e-11
- w_expdown: float32 [16, 512, 1536], P('blk', 'head'), may hold values from -0.75 to 0.75
- m_expdown: float32 [16, 512, 1536], P('blk', 'head'), may hold values from -3.0517578e-05 to 3.0517578e-05
- v_expdown: float32 [16, 512, 1536], P('blk', 'head'), may hold values from 8.199001e-13 to 3.2796003e-12
Outputs:
- block_out: bfloat16 [2, 2048, 1536], P(None, ('head', 'blk'))
- token_grad: float32 [2, 2048, 1536], P(None, ('head', 'blk'))
- grad_qkv: float32 [1536, 2560], P(('head', 'blk'))
- mnew_qkv: float32 [1536, 2560], P(('head', 'blk'))
- vnew_qkv: float32 [1536, 2560], P(('head', 'blk'))
- step_qkv: float32 [1536, 2560], P(('head', 'blk'))
- grad_out: float32 [1536, 1536], P(('head', 'blk'))
- mnew_out: float32 [1536, 1536], P(('head', 'blk'))
- vnew_out: float32 [1536, 1536], P(('head', 'blk'))
- step_out: float32 [1536, 1536], P(('head', 'blk'))
- grad_shgu: float32 [1536, 2048], P(('head', 'blk'))
- mnew_shgu: float32 [1536, 2048], P(('head', 'blk'))
- vnew_shgu: float32 [1536, 2048], P(('head', 'blk'))
- step_shgu: float32 [1536, 2048], P(('head', 'blk'))
- grad_shdown: float32 [1024, 1536], P(('head', 'blk'))
- mnew_shdown: float32 [1024, 1536], P(('head', 'blk'))
- vnew_shdown: float32 [1024, 1536], P(('head', 'blk'))
- step_shdown: float32 [1024, 1536], P(('head', 'blk'))
- grad_router: float32 [1536, 16], P(('head', 'blk'))
- mnew_router: float32 [1536, 16], P(('head', 'blk'))
- vnew_router: float32 [1536, 16], P(('head', 'blk'))
- step_router: float32 [1536, 16], P(('head', 'blk'))
- grad_gains: float32 [2, 1536], P(None, ('head', 'blk'))
- mnew_gains: float32 [2, 1536], P(None, ('head', 'blk'))
- vnew_gains: float32 [2, 1536], P(None, ('head', 'blk'))
- step_gains: float32 [2, 1536], P(None, ('head', 'blk'))
- grad_expgu: float32 [16, 1536, 1024], P('blk', 'head')
- mnew_expgu: float32 [16, 1536, 1024], P('blk', 'head')
- vnew_expgu: float32 [16, 1536, 1024], P('blk', 'head')
- step_expgu: float32 [16, 1536, 1024], P('blk', 'head')
- grad_expdown: float32 [16, 512, 1536], P('blk', 'head')
- mnew_expdown: float32 [16, 512, 1536], P('blk', 'head')
- vnew_expdown: float32 [16, 512, 1536], P('blk', 'head')
- step_expdown: float32 [16, 512, 1536], P('blk', 'head')
- grad_norm: float32 [], replicated
- stats: float32 [3], replicated
The draws below stay inside these ranges and needn't reach their ends.
Inputs may be any that keep to these rules, and one draw needn't show every extreme that they name: `lengths`: each slot holds one sequence from its first position, of 1792 positions or more; one slot, drawn from the seed, is full. `routes`: each row names 6 different experts. In the rows of one device (aligned blocks of 128 rows, the first two dimensions taken together in order) no expert is named by more than 96 rows, and in some block one expert is named by exactly 96 rows.
All inputs are finite; a program needn't handle non-finite values.
Results may differ from the reference program's by a relative error of at most 0.024.
Values may be sent and summed in bfloat16 or wider, within the bound.
No kernel may reach another device: no remote copies, remote signals or barrier semaphores. Data moves between devices by JAX's collectives and lax.ppermute only.
A program may use at most 256 MiB of HBM per device.

```python
import math
import jax
import jax.numpy as jnp
import numpy as np
from jax import lax

D = 1536
HEADS = 12
KV_HEADS = 4
HEAD_DIM = 128
EXPERT_FF = 512
SHARED = 1024
TOP = 6
STRETCH = 64
SEQS = 2
ADAM_STEP = 10
GROUP = 3
QDIM = 1536
QKV_COLS = 2560
SLOT = 2048
EXPERTS = 16
CAP = 96
PARAMS = 48786432
DEVICES = 32


def draw_tokens(key, part):
    position_share = jnp.arange(SLOT, dtype=jnp.float32) / SLOT
    base = jnp.clip(jax.random.normal(key, (SEQS, SLOT, D), jnp.float32), -5.0, 5.0)
    scale = 0.6 + 1.4 * position_share
    return (base * scale[None, :, None]).astype(jnp.bfloat16)


def draw_lengths(key, part):
    length_key = jax.random.fold_in(key, 11)
    full_key = jax.random.fold_in(key, 12)
    drawn = jax.random.randint(length_key, (SEQS,), SLOT * 7 // 8, SLOT + 1, dtype=jnp.int32)
    full_slot = jax.random.randint(full_key, (), 0, SEQS, dtype=jnp.int32)
    return jnp.where(jnp.arange(SEQS, dtype=jnp.int32) == full_slot, SLOT, drawn).astype(jnp.int32)


def block_levels(key, shape, shards, least, top_value):
    def one(position, parts):
        steps = jax.random.uniform(jax.random.fold_in(jax.random.fold_in(key, 6), position), (parts,), jnp.float32, least / len(shards), top_value / len(shards))
        return jnp.repeat(jnp.exp(steps), shape[position] // parts).reshape((-1,) + (1,) * (len(shape) - position - 1))

    level = one(*shards[0])
    for cut in shards[1:]:
        level = level * one(*cut)
    return level


def deal_out(key, own, number, rows, number_of, top, most, slope):
    order = jax.random.permutation(key, number_of)
    crowded, ordinary = load_shares(number_of, rows * top, most, slope, True), load_shares(number_of, rows * top, most, slope, False)
    places = jnp.arange(number_of)

    def named(sizes, turn):
        used = int((sizes > 0).sum())
        fixed = max(1, used // 4)
        shifted = fixed + (places - fixed + turn * (used - fixed)) % max(1, number_of - fixed)
        return jnp.zeros((number_of,), jnp.int32).at[order[jnp.where(places < fixed, places, shifted)]].set(jnp.asarray(sizes, jnp.int32))

    sizes = jnp.where(number % 4 == 0, named(crowded, number // 4), named(ordinary, number - number // 4 - 1))
    mixed = jax.random.permutation(jax.random.fold_in(own, 3), number_of)
    giver, receiver = mixed[0:number_of // 2 * 2:2], mixed[1:number_of // 2 * 2:2]
    slack = jnp.minimum(sizes[giver] - 1, most - sizes[receiver]) // 2
    slack = jnp.where((giver == order[0]) | (receiver == order[0]) | (sizes[receiver] == 0), 0, jnp.maximum(slack, 0))
    shifted = jax.random.randint(jax.random.fold_in(own, 4), (number_of // 2,), 0, 1 << 20) % (slack + 1)
    sizes = sizes.at[giver].add(-shifted).at[receiver].add(shifted)
    labels = jnp.searchsorted(jnp.cumsum(sizes), jnp.arange(rows * top), side="right").astype(jnp.int32)
    grid = labels.reshape(top, rows).T
    grid = grid[jax.random.permutation(jax.random.fold_in(own, 1), rows)]
    turn = jax.random.randint(jax.random.fold_in(own, 2), (rows, 1), 0, top)
    return jnp.take_along_axis(grid, (jnp.arange(top)[None, :] + turn) % top, axis=1)


def load_shares(count, total, limit, slope, full):
    portions = [(1 << 20) // math.isqrt(standing ** slope) + 1 for standing in range(1, count + 1)]
    largest = limit if full else min(limit, max(-(-total // count), total * portions[0] // sum(portions)))
    least = 1 if total - largest >= count - 1 else 0
    counts, rest = [largest] + [least] * (count - 1), total - largest - least * (count - 1)
    while rest > 0:
        movable = [i for i in range(1, count) if counts[i] < largest] or [i for i in range(1, count) if counts[i] < limit]
        mass, left = sum([portions[i] for i in movable]), rest
        for i in movable:
            more = min(limit - counts[i], max(1, left * portions[i] // mass), rest)
            counts[i] = counts[i] + more
            rest = rest - more
    return np.array(counts)


def gaussian(stream_key, extent, deviation, most, split=(), kind=jnp.bfloat16):
    values = deviation * jax.random.normal(stream_key, extent, jnp.float32)
    if split:
        values = values * block_levels(stream_key, extent, split, -0.22, 0.18)
    return jnp.clip(values, -most, most).astype(kind)


def setup_inputs(seed: int = 0) -> dict:
    key_of = jax.random.split(jax.random.key(seed), 29)
    tokens = draw_tokens(jax.random.fold_in(key_of[28], 71), 0)
    cotangent = gaussian(key_of[1], (SEQS, SLOT, D), 1.0, 6.0, ((1, 32),))
    lengths = draw_lengths(jax.random.fold_in(key_of[28], 71), 0)
    routes_keys = jax.random.split(jax.random.fold_in(key_of[3], 1), SLOT * SEQS // (STRETCH * SEQS))
    routes_turns = jax.random.permutation(jax.random.fold_in(key_of[3], 3), SLOT * SEQS // (STRETCH * SEQS))
    routes = jax.vmap(lambda own, number: deal_out(jax.random.fold_in(key_of[3], 2), own, number, STRETCH * SEQS, EXPERTS, TOP, CAP, 2))(routes_keys, routes_turns).reshape((SLOT, SEQS, TOP))
    w_qkv = gaussian(key_of[4], (D, QKV_COLS), D ** -0.5, 0.15625, ((0, 32),), jnp.float32)
    m_qkv = gaussian(key_of[5], (D, QKV_COLS), (0.11 * PARAMS ** -0.5), 9.1552734375e-05, ((0, 32),), jnp.float32)
    v_qkv = jnp.clip(jnp.exp(math.log(8.199001200193123e-11) - 1.3862944 * jax.random.uniform(key_of[6], (D, QKV_COLS), jnp.float32) ** block_levels(key_of[6], (D, QKV_COLS), ((0, 32),), -0.2, 0.2)), 2.049750300048281e-11, 8.199001200193123e-11)
    w_out = gaussian(key_of[7], (QDIM, D), (QDIM // 64) ** -0.5, 1.25, ((0, 32),), jnp.float32)
    m_out = gaussian(key_of[8], (QDIM, D), (0.04 * PARAMS ** -0.5), 3.0517578125e-05, ((0, 32),), jnp.float32)
    v_out = jnp.clip(jnp.exp(math.log(4.0995002531518665e-12) - 1.3862944 * jax.random.uniform(key_of[9], (QDIM, D), jnp.float32) ** block_levels(key_of[9], (QDIM, D), ((0, 32),), -0.2, 0.2)), 1.0248750632879666e-12, 4.0995002531518665e-12)
    w_shgu = gaussian(key_of[10], (D, 2 * SHARED), D ** -0.5, 0.15625, ((0, 32),), jnp.float32)
    m_shgu = gaussian(key_of[11], (D, 2 * SHARED), (0.11 * PARAMS ** -0.5), 9.1552734375e-05, ((0, 32),), jnp.float32)
    v_shgu = jnp.clip(jnp.exp(math.log(8.199001200193123e-11) - 1.3862944 * jax.random.uniform(key_of[12], (D, 2 * SHARED), jnp.float32) ** block_levels(key_of[12], (D, 2 * SHARED), ((0, 32),), -0.2, 0.2)), 2.049750300048281e-11, 8.199001200193123e-11)
    w_shdown = gaussian(key_of[13], (SHARED, D), SHARED ** -0.5, 0.1875, ((0, 32),), jnp.float32)
    m_shdown = gaussian(key_of[14], (SHARED, D), (0.11 * PARAMS ** -0.5), 9.1552734375e-05, ((0, 32),), jnp.float32)
    v_shdown = jnp.clip(jnp.exp(math.log(8.199001200193123e-11) - 1.3862944 * jax.random.uniform(key_of[15], (SHARED, D), jnp.float32) ** block_levels(key_of[15], (SHARED, D), ((0, 32),), -0.2, 0.2)), 2.049750300048281e-11, 8.199001200193123e-11)
    w_router = gaussian(key_of[16], (D, EXPERTS), (4 * D) ** -0.5, 0.078125, ((0, 32),), jnp.float32)
    m_router = gaussian(key_of[17], (D, EXPERTS), (1.8 * PARAMS ** -0.5), 0.0014648438, ((0, 32),), jnp.float32)
    v_router = jnp.clip(jnp.exp(math.log(3.279600235828184e-08) - 2.7725887 * jax.random.uniform(key_of[18], (D, EXPERTS), jnp.float32) ** block_levels(key_of[18], (D, EXPERTS), ((0, 32),), -0.2, 0.2)), 2.049750147392615e-09, 3.279600235828184e-08)
    w_gains = jnp.clip(1.0 + 0.1 * jax.random.normal(key_of[19], (2, D), jnp.float32), 0.5, 1.5)
    m_gains = gaussian(key_of[20], (2, D), (0.11 * PARAMS ** -0.5), 9.1552734375e-05, ((1, 32),), jnp.float32)
    v_gains = jnp.clip(jnp.exp(math.log(8.199001200193123e-11) - 1.3862944 * jax.random.uniform(key_of[21], (2, D), jnp.float32) ** block_levels(key_of[21], (2, D), ((1, 32),), -0.2, 0.2)), 2.049750300048281e-11, 8.199001200193123e-11)
    w_expgu = gaussian(key_of[22], (EXPERTS, D, 2 * EXPERT_FF), D ** -0.5, 0.15625, ((0, 16), (1, 2)), jnp.float32)
    m_expgu = gaussian(key_of[23], (EXPERTS, D, 2 * EXPERT_FF), (0.11 * PARAMS ** -0.5), 9.1552734375e-05, ((0, 16), (1, 2)), jnp.float32)
    v_expgu = jnp.clip(jnp.exp(math.log(8.199001200193123e-11) - 1.3862944 * jax.random.uniform(key_of[24], (EXPERTS, D, 2 * EXPERT_FF), jnp.float32) ** block_levels(key_of[24], (EXPERTS, D, 2 * EXPERT_FF), ((0, 16), (1, 2)), -0.2, 0.2)), 2.049750300048281e-11, 8.199001200193123e-11)
    w_expdown = gaussian(key_of[25], (EXPERTS, EXPERT_FF, D), (EXPERT_FF // 8) ** -0.5, 0.75, ((0, 16), (1, 2)), jnp.float32)
    m_expdown = gaussian(key_of[26], (EXPERTS, EXPERT_FF, D), (0.04 * PARAMS ** -0.5), 3.0517578125e-05, ((0, 16), (1, 2)), jnp.float32)
    v_expdown = jnp.clip(jnp.exp(math.log(3.279600332625754e-12) - 1.3862944 * jax.random.uniform(key_of[27], (EXPERTS, EXPERT_FF, D), jnp.float32) ** block_levels(key_of[27], (EXPERTS, EXPERT_FF, D), ((0, 16), (1, 2)), -0.2, 0.2)), 8.199000831564385e-13, 3.279600332625754e-12)
    return dict(tokens=tokens, cotangent=cotangent, lengths=lengths, routes=routes, w_qkv=w_qkv, m_qkv=m_qkv, v_qkv=v_qkv, w_out=w_out, m_out=m_out, v_out=v_out, w_shgu=w_shgu, m_shgu=m_shgu, v_shgu=v_shgu, w_shdown=w_shdown, m_shdown=m_shdown, v_shdown=v_shdown, w_router=w_router, m_router=m_router, v_router=v_router, w_gains=w_gains, m_gains=m_gains, v_gains=v_gains, w_expgu=w_expgu, m_expgu=m_expgu, v_expgu=v_expgu, w_expdown=w_expdown, m_expdown=m_expdown, v_expdown=v_expdown)


precise = lax.Precision.HIGHEST
norm_eps = 1e-05
adam_eps = 1e-08
learn_rate = 0.02
first_decay = 0.9
second_decay = 0.999
weight_decay = 0.1
clip_norm = 1.0
masked_score = -1e+30

@jax.custom_vjp
def low(v):
    return lax.optimization_barrier(v.astype(jnp.bfloat16)).astype(jnp.float32)

@jax.custom_vjp
def low_back(v):
    return v

def low_keep(v):
    return (low(v), None)

def low_pass(kept, grad):
    return (grad,)

def back_keep(v):
    return (v, None)

def back_low(kept, grad):
    return (low(grad),)
low.defvjp(low_keep, low_pass)
low_back.defvjp(back_keep, back_low)

def matmul(left, right):
    return jnp.dot(left, right, precision=precise, preferred_element_type=jnp.float32)

def rms_norm(values, gain):
    inverse = lax.rsqrt(lax.optimization_barrier(jnp.mean(values * values, axis=-1, keepdims=True)) + norm_eps)
    return values * inverse * gain

def silu_mix(hidden, width):
    return jax.nn.silu(hidden[:, :width]) * hidden[:, width:]

def attend_block(query_block, keys_seq, values_seq, length, start):
    count = query_block.shape[0]
    raw = jnp.einsum('qkgd,skd->kgqs', query_block, keys_seq, precision=precise, preferred_element_type=jnp.float32)
    scores = low_back(raw * HEAD_DIM ** (-0.5))
    query_pos = start + jnp.arange(count, dtype=jnp.int32)
    key_pos = jnp.arange(keys_seq.shape[0], dtype=jnp.int32)
    allowed = (key_pos[None, :] <= query_pos[:, None]) & (key_pos[None, :] < length)
    scores = jnp.where(allowed, scores, masked_score)
    total = jax.nn.logsumexp(scores, axis=-1, keepdims=True)
    weights = low(jnp.exp(scores - total))
    return jnp.einsum('kgqs,skd->qkgd', weights, values_seq, precision=precise, preferred_element_type=jnp.float32)

def attention(queries, keys, values, lengths):
    block = math.gcd(SLOT, 512)
    count = SLOT // block
    attend = jax.checkpoint(attend_block)
    starts = jnp.arange(count, dtype=jnp.int32) * block

    def one_sequence(items):
        query_seq, keys_seq, values_seq, length = items
        blocks = query_seq.reshape(count, block, KV_HEADS, GROUP, HEAD_DIM)

        def one_block(pair):
            return attend(pair[0], keys_seq, values_seq, length, pair[1])
        return lax.map(one_block, (blocks, starts)).reshape(SLOT, KV_HEADS, GROUP, HEAD_DIM)
    return lax.map(one_sequence, (queries, keys, values, lengths))

def slot_tables(routes):
    total_rows = SLOT * SEQS
    per_device = STRETCH * SEQS
    flat_routes = routes.reshape(total_rows, TOP).astype(jnp.int32)
    hits = flat_routes[:, :, None] == jnp.arange(EXPERTS, dtype=jnp.int32)[None, None, :]
    named = lax.optimization_barrier(jnp.sum(hits.astype(jnp.int32), axis=1)).astype(jnp.int32).reshape(DEVICES, per_device, EXPERTS)
    before = (jnp.cumsum(named, axis=1).astype(jnp.int32) - named).reshape(total_rows, EXPERTS)
    slots = lax.optimization_barrier(jnp.sum(jnp.where(hits, before[:, None, :], 0), axis=2)).astype(jnp.int32)
    device = jnp.arange(total_rows, dtype=jnp.int32) // per_device
    place = (device[:, None] * CAP + slots).reshape(-1).astype(jnp.int32)
    entry = jnp.arange(total_rows * TOP, dtype=jnp.int32)
    table = jnp.full((EXPERTS, DEVICES * CAP), total_rows * TOP, jnp.int32)
    table = table.at[flat_routes.reshape(-1), place].set(entry)
    return (hits, table)

def mixture(normed_rows, router, expert_gate_up, expert_down, hits, table):
    total_rows = normed_rows.shape[0]
    logits = low_back(matmul(normed_rows, router))
    picked = lax.optimization_barrier(jnp.sum(jnp.where(hits, logits[:, None, :], 0.0), axis=2))
    gates = jax.nn.softmax(picked, axis=-1)
    padded_rows = jnp.concatenate([normed_rows, jnp.zeros((1, D), jnp.float32)], axis=0)
    padded_gates = jnp.concatenate([gates.reshape(-1), jnp.zeros((1,), jnp.float32)])

    def expert_step(total, items):
        gate_up, down, entries = items
        token_rows = (entries // TOP).astype(jnp.int32)
        chosen = low_back(jnp.take(padded_rows, token_rows, axis=0))
        hidden = low_back(matmul(chosen, gate_up))
        middle = low(silu_mix(hidden, EXPERT_FF))
        result = low_back(low(matmul(middle, down)))
        weight = jnp.take(padded_gates, entries)
        return (total.at[token_rows].add(weight[:, None] * result), None)
    start_total = jnp.zeros((total_rows + 1, D), jnp.float32)
    total, unused = lax.scan(jax.checkpoint(expert_step), start_total, (expert_gate_up, expert_down, table))
    return total[:total_rows]

def forward(weights, tokens_f, lengths, hits, table):
    w_qkv, w_out, w_shgu, w_shdown, w_router, w_gains, w_expgu, w_expdown = [low(item) for item in weights]
    normed_in = low(rms_norm(tokens_f, w_gains[0]))
    projected = matmul(normed_in.reshape(-1, D), w_qkv).reshape(SEQS, SLOT, KV_HEADS, GROUP + 2, HEAD_DIM)
    projected = low_back(low(projected))
    attended = attention(projected[:, :, :, :GROUP], projected[:, :, :, GROUP], projected[:, :, :, GROUP + 1], lengths)
    attended = low_back(low(attended))
    branch = low_back(matmul(attended.reshape(-1, HEADS * HEAD_DIM), w_out)).reshape(SEQS, SLOT, D)
    middle = tokens_f + branch
    normed_mid = low(rms_norm(middle, w_gains[1]))
    mid_rows = jnp.transpose(normed_mid, (1, 0, 2)).reshape(SLOT * SEQS, D)
    routed = mixture(mid_rows, w_router, w_expgu, w_expdown, hits, table)
    routed = jnp.transpose(routed.reshape(SLOT, SEQS, D), (1, 0, 2))
    shared_hidden = low_back(matmul(normed_mid.reshape(-1, D), w_shgu))
    shared_mid = low(silu_mix(shared_hidden, SHARED))
    shared_out = low_back(matmul(shared_mid, w_shdown)).reshape(SEQS, SLOT, D)
    final = middle + routed + shared_out
    return (final, (branch, middle))

def adam_update(weight, first, second, grad, factor):
    clipped = grad * factor
    first_new = first_decay * first + (1.0 - first_decay) * clipped
    second_new = second_decay * second + (1.0 - second_decay) * clipped * clipped
    first_fix = 1.0 - first_decay ** ADAM_STEP
    second_fix = 1.0 - second_decay ** ADAM_STEP
    change = -learn_rate * (first_new / first_fix / (jnp.sqrt(second_new / second_fix) + adam_eps) + weight_decay * weight)
    return (first_new, second_new, change)

def reference(tokens, cotangent, lengths, routes, w_qkv, m_qkv, v_qkv, w_out, m_out, v_out, w_shgu, m_shgu, v_shgu, w_shdown, m_shdown, v_shdown, w_router, m_router, v_router, w_gains, m_gains, v_gains, w_expgu, m_expgu, v_expgu, w_expdown, m_expdown, v_expdown):
    weights = [w_qkv, w_out, w_shgu, w_shdown, w_router, w_gains, w_expgu, w_expdown]
    hits, table = slot_tables(routes)
    tokens_f = tokens.astype(jnp.float32)

    def run(params, inputs):
        return forward(params, inputs, lengths, hits, table)
    final, pullback, kept = jax.vjp(run, weights, tokens_f, has_aux=True)
    branch, middle = kept
    valid = (jnp.arange(SLOT, dtype=jnp.int32)[None, :] < lengths[:, None]).astype(jnp.float32)[:, :, None]
    grads, token_grad = pullback(cotangent.astype(jnp.float32) * valid)
    count = jnp.sum(lengths).astype(jnp.float32) * D

    def root_mean(values):
        return jnp.sqrt(jnp.sum(values * values * valid) / count)
    stats = jnp.stack([root_mean(branch), root_mean(middle), root_mean(final)])
    squares = jnp.sum(jnp.stack([jnp.sum(item * item) for item in grads]))
    grad_norm = jnp.sqrt(squares)
    factor = clip_norm / jnp.maximum(grad_norm, clip_norm)
    g_qkv, g_out, g_shgu, g_shdown, g_router, g_gains, g_expgu, g_expdown = grads
    a_qkv, b_qkv, c_qkv = adam_update(w_qkv, m_qkv, v_qkv, g_qkv, factor)
    a_out, b_out, c_out = adam_update(w_out, m_out, v_out, g_out, factor)
    a_shgu, b_shgu, c_shgu = adam_update(w_shgu, m_shgu, v_shgu, g_shgu, factor)
    a_shdown, b_shdown, c_shdown = adam_update(w_shdown, m_shdown, v_shdown, g_shdown, factor)
    a_router, b_router, c_router = adam_update(w_router, m_router, v_router, g_router, factor)
    a_gains, b_gains, c_gains = adam_update(w_gains, m_gains, v_gains, g_gains, factor)
    a_expgu, b_expgu, c_expgu = adam_update(w_expgu, m_expgu, v_expgu, g_expgu, factor)
    a_expdown, b_expdown, c_expdown = adam_update(w_expdown, m_expdown, v_expdown, g_expdown, factor)
    return (final.astype(jnp.bfloat16), token_grad, g_qkv, a_qkv, b_qkv, c_qkv, g_out, a_out, b_out, c_out, g_shgu, a_shgu, b_shgu, c_shgu, g_shdown, a_shdown, b_shdown, c_shdown, g_router, a_router, b_router, c_router, g_gains, a_gains, b_gains, c_gains, g_expgu, a_expgu, b_expgu, c_expgu, g_expdown, a_expdown, b_expdown, c_expdown, grad_norm, stats)
```

```python
import functools

import jax
import jax.numpy as jnp
from jax import lax
from jax.experimental import pallas as pl
from jax.experimental.pallas import tpu as pltpu
from jax.sharding import PartitionSpec as P

HEADS = 12
KV_HEADS = 4
HEAD_DIM = 128
EXPERT_FF = 512
SHARED = 1024
TOP = 6
ADAM_STEP = 10
GROUP = 3


norm_eps = 1e-05
adam_eps = 1e-08
learn_rate = 0.02
first_decay = 0.9
second_decay = 0.999
weight_decay = 0.1
clip_norm = 1.0
masked_score = -1e30
group_turn = 4


def to_experts(buffer):
    return lax.all_to_all(buffer, "blk", split_axis=0, concat_axis=0, tiled=True)


def from_experts(buffer):
    return lax.all_to_all(buffer, "blk", split_axis=0, concat_axis=0, tiled=True)


def outer_dot(left, right):
    return lax.dot_general(
        left, right, (((0,), (0,)), ((), ())), preferred_element_type=jnp.float32
    )


def back_dot(left, right):
    return lax.dot_general(
        left, right, (((1,), (1,)), ((), ())), preferred_element_type=jnp.float32
    )


def silu_grad(values):
    logistic = jax.nn.sigmoid(values)
    return logistic * (1.0 + values * (1.0 - logistic))


def local_fold(function, init, gathered):
    turns = gathered[0].shape[0] // group_turn

    def advance(turn, carry):
        start = turn * group_turn
        piece = (
            lax.dynamic_slice_in_dim(gathered[0], start, group_turn, 0),
            lax.dynamic_slice_in_dim(gathered[1], start, group_turn, 0),
        )
        return function(carry, piece, start)

    return lax.fori_loop(0, turns, advance, init)


def adam_update(weight, first, second, grad, factor):
    clipped = grad * factor
    first_new = first_decay * first + (1.0 - first_decay) * clipped
    second_new = second_decay * second + (1.0 - second_decay) * clipped * clipped
    first_fix = 1.0 - first_decay**ADAM_STEP
    second_fix = 1.0 - second_decay**ADAM_STEP
    change = -learn_rate * (
        first_new / first_fix / (jnp.sqrt(second_new / second_fix) + adam_eps)
        + weight_decay * weight
    )
    return (first_new, second_new, change)


WIDTH_ROWS = 512


def axis_bits(name):
    size = lax.axis_size(name)
    return [(name, 1 << k) for k in reversed(range(size.bit_length() - 1))]


def swap(values, step):
    name, bit = step
    size = lax.axis_size(name)
    return lax.ppermute(values, name, [(i, i ^ bit) for i in range(size)])


def own_bit(step):
    return (lax.axis_index(step[0]) // step[1]) % 2


def both_orders():
    head_bits, blk_bits = axis_bits("head"), axis_bits("blk")
    first = blk_bits[:-1] + head_bits + blk_bits[-1:]
    second = blk_bits[:-2] + head_bits + blk_bits[-2:]
    return (first, second)


def blk_orders():
    blk_bits = axis_bits("blk")
    return (blk_bits, blk_bits[-2:-1] + blk_bits[:-2] + blk_bits[-1:])


def lockstep(pieces, orders, act, backwards=False):
    count = len(orders[0])
    for turn in reversed(range(count)) if backwards else range(count):
        pieces = [act(piece, order[turn]) for piece, order in zip(pieces, orders)]
    return pieces


def gather_relative(pieces, orders):
    def act(piece, step):
        return jnp.concatenate([piece, swap(piece, step)], axis=0)

    return lockstep([piece[None] for piece in pieces], orders, act)


def scatter_relative(pieces, orders):
    def act(piece, step):
        half = piece.shape[0] // 2
        return piece[:half] + swap(piece[half:], step)

    return [piece[0] for piece in lockstep(pieces, orders, act, backwards=True)]


def gather_rows(pieces, orders):
    places = axis_bits("head") + axis_bits("blk")

    def act(piece, step):
        place = places.index(step)
        shape = [1] * piece.ndim
        shape[place] = 2
        mine = lax.broadcasted_iota(jnp.int32, shape, place) == own_bit(step)
        return jnp.where(mine, piece, swap(piece, step))

    wide = [piece.reshape((1,) * len(places) + piece.shape) for piece in pieces]
    return [
        full.reshape(-1, full.shape[-1]) for full in lockstep(wide, orders, act)
    ]


def scatter_rows(pieces, orders):
    places = axis_bits("head") + axis_bits("blk")
    devices = 1 << len(places)

    def act(piece, step):
        place = places.index(step)
        bit = own_bit(step)
        mine = lax.dynamic_slice_in_dim(piece, bit, 1, place)
        theirs = lax.dynamic_slice_in_dim(piece, 1 - bit, 1, place)
        return mine + swap(theirs, step)

    wide = [
        piece.reshape((2,) * len(places) + (piece.shape[0] // devices, piece.shape[1]))
        for piece in pieces
    ]
    return [
        own.reshape(own.shape[-2:]) for own in lockstep(wide, orders, act, backwards=True)
    ]


def sum_everywhere(values):
    for step in axis_bits("blk") + axis_bits("head"):
        values = values + swap(values, step)
    return values


def block_devices(order):
    offsets = [(0, 0)]
    for name, bit in order:
        offsets = offsets + [
            (h ^ bit, b) if name == "head" else (h, b ^ bit) for h, b in offsets
        ]
    head_index, blk_index = lax.axis_index("head"), lax.axis_index("blk")
    heads = jnp.array([h for h, _ in offsets], jnp.int32)
    blks = jnp.array([b for _, b in offsets], jnp.int32)
    return (head_index ^ heads) * lax.axis_size("blk") + (blk_index ^ blks)


def stack_heads(block):
    return jnp.concatenate(
        [block[:, i * HEAD_DIM : (i + 1) * HEAD_DIM] for i in range(GROUP)], axis=0
    )


def group_scores(query, keys, limit, key_pos):
    scores = lax.dot_general(
        query, keys, (((1,), (1,)), ((), ())), preferred_element_type=jnp.float32
    ) * (HEAD_DIM ** (-0.5))
    return jnp.where(key_pos <= limit, scores, masked_score)


def attend_kernel(q_ref, kv_ref, pos_ref, limit_ref, out_ref, low_ref, log_ref):
    stretch = q_ref.shape[0]
    query = stack_heads(q_ref[...])
    keys = kv_ref[:, :, :HEAD_DIM].reshape(-1, HEAD_DIM)
    values = kv_ref[:, :, HEAD_DIM:].reshape(-1, HEAD_DIM)
    limit = jnp.concatenate([limit_ref[...]] * GROUP, axis=0)
    scores = group_scores(query, keys, limit, pos_ref[...])
    top = jnp.max(scores, axis=1, keepdims=True)
    weights = jnp.exp(scores - top)
    total = jnp.sum(weights, axis=1, keepdims=True)
    out = jnp.dot(weights.astype(jnp.bfloat16), values, preferred_element_type=jnp.float32)
    out = out / total
    log_ref[0] = top + jnp.log(total)
    for i in range(GROUP):
        part = out[i * stretch : (i + 1) * stretch]
        columns = slice(i * HEAD_DIM, (i + 1) * HEAD_DIM)
        out_ref[:, columns] = part
        low_ref[:, columns] = part.astype(jnp.bfloat16)


def attend_back_kernel(
    q_ref, kv_ref, pos_ref, limit_ref, grad_ref, out_ref, log_ref, dq_ref, dkv_ref
):
    stretch = q_ref.shape[0]
    scale = HEAD_DIM ** (-0.5)
    low_type = jnp.bfloat16
    query = stack_heads(q_ref[...])
    keys = kv_ref[:, :, :HEAD_DIM].reshape(-1, HEAD_DIM)
    values = kv_ref[:, :, HEAD_DIM:].reshape(-1, HEAD_DIM)
    grad = stack_heads(grad_ref[...])
    row_dot = jnp.sum(
        grad.astype(jnp.float32) * stack_heads(out_ref[...]), axis=1, keepdims=True
    )
    limit = jnp.concatenate([limit_ref[...]] * GROUP, axis=0)
    scores = group_scores(query, keys, limit, pos_ref[...])
    weights = jnp.exp(scores - log_ref[0])
    grad_weights = lax.dot_general(
        grad, values, (((1,), (1,)), ((), ())), preferred_element_type=jnp.float32
    )
    grad_scores = (weights * (grad_weights - row_dot)).astype(low_type)
    weights_low = weights.astype(low_type)
    dq = jnp.dot(grad_scores, keys, preferred_element_type=jnp.float32) * scale
    dk = outer_dot(grad_scores, query) * scale
    dv = outer_dot(weights_low, grad)
    block = dkv_ref.shape[:2] + (HEAD_DIM,)
    dkv_ref[:, :, :HEAD_DIM] = dk.astype(low_type).reshape(block)
    dkv_ref[:, :, HEAD_DIM:] = dv.astype(low_type).reshape(block)
    for i in range(GROUP):
        part = dq[i * stretch : (i + 1) * stretch]
        dq_ref[:, i * HEAD_DIM : (i + 1) * HEAD_DIM] = part.astype(low_type)


def attention_specs(stretch, devices):
    wide = pl.BlockSpec((stretch, GROUP * HEAD_DIM), lambda s: (s, 0))
    pair = pl.BlockSpec((devices, stretch, 2 * HEAD_DIM), lambda s: (0, s, 0))
    pos = pl.BlockSpec((1, devices * stretch), lambda s: (0, 0))
    limit = pl.BlockSpec((stretch, 1), lambda s: (s, 0))
    log = pl.BlockSpec((1, GROUP * stretch, 1), lambda s: (s, 0, 0))
    return wide, pair, pos, limit, log


def attention_cost(seqs, stretch, devices, matmuls):
    scores = seqs * GROUP * stretch * devices * stretch
    return pl.CostEstimate(
        flops=2 * matmuls * scores * HEAD_DIM,
        bytes_accessed=devices * seqs * stretch * 2 * HEAD_DIM * 2,
        transcendentals=scores,
    )


def attend(query, pair, key_pos, limit, seqs, stretch):
    devices = pair.shape[0]
    wide, kv, pos, lim, log = attention_specs(stretch, devices)
    return pl.pallas_call(
        attend_kernel,
        grid=(seqs,),
        in_specs=[wide, kv, pos, lim],
        out_specs=[wide, wide, log],
        out_shape=[
            jax.ShapeDtypeStruct(query.shape, jnp.float32),
            jax.ShapeDtypeStruct(query.shape, jnp.bfloat16),
            jax.ShapeDtypeStruct((seqs, GROUP * stretch, 1), jnp.float32),
        ],
        compiler_params=pltpu.CompilerParams(vmem_limit_bytes=48 << 20),
        cost_estimate=attention_cost(seqs, stretch, devices, 2),
        name="attend",
    )(query, pair, key_pos, limit)


def attend_back(query, pair, key_pos, limit, grad, out, log_total, seqs, stretch):
    devices = pair.shape[0]
    wide, kv, pos, lim, log = attention_specs(stretch, devices)
    return pl.pallas_call(
        attend_back_kernel,
        grid=(seqs,),
        in_specs=[wide, kv, pos, lim, wide, wide, log],
        out_specs=[wide, kv],
        out_shape=[
            jax.ShapeDtypeStruct(query.shape, jnp.bfloat16),
            jax.ShapeDtypeStruct(pair.shape, jnp.bfloat16),
        ],
        compiler_params=pltpu.CompilerParams(vmem_limit_bytes=48 << 20),
        cost_estimate=attention_cost(seqs, stretch, devices, 5),
        name="attend_back",
    )(query, pair, key_pos, limit, grad, out, log_total)


def local(
    tokens,
    cotangent,
    lengths,
    routes,
    w_qkv,
    m_qkv,
    v_qkv,
    w_out,
    m_out,
    v_out,
    w_shgu,
    m_shgu,
    v_shgu,
    w_shdown,
    m_shdown,
    v_shdown,
    w_router,
    m_router,
    v_router,
    w_gains,
    m_gains,
    v_gains,
    w_expgu,
    m_expgu,
    v_expgu,
    w_expdown,
    m_expdown,
    v_expdown,
):
    low_type = jnp.bfloat16
    full_type = jnp.float32
    heads_axis = lax.axis_size("head")
    blocks_axis = lax.axis_size("blk")
    head_index = lax.axis_index("head")
    blk_index = lax.axis_index("blk")
    seqs, stretch, width = tokens.shape
    rows = seqs * stretch
    experts = w_router.shape[1]
    capacity = min(rows, max(2, 2 * rows * TOP // experts))
    kv_local = KV_HEADS // heads_axis
    span = blocks_axis * stretch
    scale = HEAD_DIM ** (-0.5)
    queries_rows = heads_axis * stretch
    dense = (
        lax.all_gather(w_qkv.astype(low_type), ("head", "blk"), axis=0, tiled=True),
        lax.all_gather(w_out.astype(low_type), ("head", "blk"), axis=0, tiled=True),
        lax.all_gather(w_shgu.astype(low_type), ("head", "blk"), axis=0, tiled=True),
        lax.all_gather(w_shdown.astype(low_type), ("head", "blk"), axis=0, tiled=True),
        lax.all_gather(w_router.astype(low_type), ("head", "blk"), axis=0, tiled=True),
        lax.all_gather(w_gains.astype(low_type), ("head", "blk"), axis=1, tiled=True),
    )
    qkv_full, out_full, shgu_full, shdown_full, router_full, gains_full = dense
    expert_full = (
        lax.all_gather(w_expgu.astype(low_type), "head", axis=1, tiled=True),
        lax.all_gather(w_expdown.astype(low_type), "head", axis=1, tiled=True),
    )
    expgu_full = expert_full[0][0]
    expdown_full = expert_full[1][0]
    gain_in = gains_full[0].astype(full_type)
    gain_mid = gains_full[1].astype(full_type)
    inputs = tokens.astype(full_type).reshape(rows, width)
    inverse_in = lax.rsqrt(jnp.mean(inputs * inputs, axis=1, keepdims=True) + norm_eps)
    normed_in = (inputs * inverse_in * gain_in).astype(low_type)
    projected = jnp.dot(normed_in, qkv_full, preferred_element_type=full_type).astype(low_type)
    stacked = projected.reshape(1, rows, heads_axis, kv_local * (GROUP + 2) * HEAD_DIM)
    by_head = lax.all_to_all(stacked, "head", split_axis=2, concat_axis=0, tiled=True)
    by_head = by_head.reshape(heads_axis, seqs, stretch, kv_local, GROUP + 2, HEAD_DIM)
    queries = by_head[:, :, :, :, :GROUP, :]
    keys = by_head[:, :, :, :, GROUP, :]
    values = by_head[:, :, :, :, GROUP + 1, :]
    query_pos = (
        jnp.arange(heads_axis)[:, None] * span + blk_index * stretch + jnp.arange(stretch)[None, :]
    ).reshape(-1)

    def piece_scores(key_piece, start):
        count = key_piece.shape[0]
        raw = jnp.einsum(
            "astkgd,nbsukd->skgatnbu", queries, key_piece, preferred_element_type=full_type
        )
        raw = raw.reshape(seqs, kv_local, GROUP, queries_rows, count * heads_axis * stretch) * scale
        key_pos = (
            (start + jnp.arange(count))[:, None, None] * stretch
            + jnp.arange(heads_axis)[None, :, None] * span
            + jnp.arange(stretch)[None, None, :]
        ).reshape(-1)
        allowed = (key_pos[None, None, :] <= query_pos[None, :, None]) & (
            key_pos[None, None, :] < lengths[:, None, None]
        )
        allowed = allowed[:, None, None]
        return (jnp.where(allowed, raw, masked_score), allowed)

    kept = (
        lax.all_gather(keys[None], "blk", axis=0, tiled=True),
        lax.all_gather(values[None], "blk", axis=0, tiled=True),
    )

    def norm_fold(carry, piece, start):
        top, total = carry
        scores, allowed = piece_scores(piece[0], start)
        new_top = jnp.maximum(top, jnp.max(scores, axis=-1))
        shifted = jnp.where(allowed, jnp.exp(scores - new_top[..., None]), 0.0)
        return (new_top, total * jnp.exp(top - new_top) + jnp.sum(shifted, axis=-1))

    stat_shape = (seqs, kv_local, GROUP, queries_rows)
    top, total = local_fold(
        norm_fold,
        (jnp.full(stat_shape, masked_score, full_type), jnp.zeros(stat_shape, full_type)),
        kept,
    )
    log_total = top + jnp.log(total)

    def out_fold(carry, piece, start):
        keys_part, values_part = piece
        count = keys_part.shape[0]
        scores, allowed = piece_scores(keys_part, start)
        weights = jnp.where(allowed, jnp.exp(scores - log_total[..., None]), 0.0).astype(low_type)
        weights = weights.reshape(
            seqs, kv_local, GROUP, heads_axis, stretch, count, heads_axis, stretch
        )
        return carry + jnp.einsum(
            "skgatnbu,nbsukd->astkgd", weights, values_part, preferred_element_type=full_type
        )

    outputs = local_fold(out_fold, jnp.zeros(queries.shape, full_type), kept)
    attended = outputs.astype(low_type).reshape(heads_axis, rows, 1, kv_local * GROUP * HEAD_DIM)
    attended_tok = lax.all_to_all(
        attended, "head", split_axis=0, concat_axis=2, tiled=True
    ).reshape(rows, HEADS * HEAD_DIM)
    branch = jnp.dot(attended_tok, out_full, preferred_element_type=full_type)
    middle = inputs + branch
    inverse_mid = lax.rsqrt(jnp.mean(middle * middle, axis=1, keepdims=True) + norm_eps)
    normed_mid = (middle * inverse_mid * gain_mid).astype(low_type)
    expert_ids = jnp.arange(experts, dtype=jnp.int32)
    hits_ts = routes[..., None] == expert_ids
    named_ts = jnp.sum(hits_ts.astype(jnp.int32), axis=2).reshape(rows, experts)
    before_ts = (jnp.cumsum(named_ts, axis=0) - named_ts).reshape(stretch, seqs, experts)
    route_rows = jnp.transpose(routes, (1, 0, 2)).reshape(rows, TOP)
    hits = jnp.transpose(hits_ts, (1, 0, 2, 3)).reshape(rows, TOP, experts)
    before = jnp.transpose(before_ts, (1, 0, 2)).reshape(rows, experts)
    slots = jnp.sum(jnp.where(hits, before[:, None, :], 0), axis=2)
    flat_route = route_rows.reshape(-1)
    flat_slot = slots.reshape(-1)
    logits = jnp.dot(normed_mid, router_full, preferred_element_type=full_type)
    picked = jnp.sum(jnp.where(hits, logits[:, None, :], 0.0), axis=2)
    gates = jax.nn.softmax(picked, axis=1)
    outgoing = (
        jnp.zeros((experts, capacity, width), low_type)
        .at[flat_route, flat_slot]
        .set(jnp.repeat(normed_mid, TOP, axis=0))
    )
    arrived = to_experts(outgoing)
    flat_in = arrived.reshape(-1, width)
    hidden = jnp.dot(flat_in, expgu_full, preferred_element_type=full_type)
    gate_part = hidden[:, :EXPERT_FF]
    up_part = hidden[:, EXPERT_FF:]
    middle_act = (jax.nn.silu(gate_part) * up_part).astype(low_type)
    expert_out = jnp.dot(middle_act, expdown_full, preferred_element_type=full_type).astype(
        low_type
    )
    returned = from_experts(expert_out.reshape(arrived.shape))
    gathered_out = returned[flat_route, flat_slot].reshape(rows, TOP, width).astype(full_type)
    routed = jnp.sum(gates[:, :, None] * gathered_out, axis=1)
    shared_hidden = jnp.dot(normed_mid, shgu_full, preferred_element_type=full_type)
    shared_gate = shared_hidden[:, :SHARED]
    shared_up = shared_hidden[:, SHARED:]
    shared_mid = (jax.nn.silu(shared_gate) * shared_up).astype(low_type)
    shared_out = jnp.dot(shared_mid, shdown_full, preferred_element_type=full_type)
    final = middle + routed + shared_out
    block_out = final.astype(low_type).reshape(seqs, stretch, width)
    own_pos = (head_index * blocks_axis + blk_index) * stretch + jnp.arange(stretch)
    valid = (own_pos[None, :] < lengths[:, None]).astype(full_type).reshape(rows, 1)
    stat_sums = jnp.stack(
        [
            jnp.sum(branch * branch * valid),
            jnp.sum(middle * middle * valid),
            jnp.sum(final * final * valid),
        ]
    )
    grad_final = cotangent.astype(full_type).reshape(rows, width) * valid
    grad_low = grad_final.astype(low_type)
    grad_shdown = outer_dot(shared_mid, grad_low)
    grad_shared_mid = back_dot(grad_low, shdown_full)
    grad_shared_hidden = jnp.concatenate(
        [
            grad_shared_mid * shared_up * silu_grad(shared_gate),
            grad_shared_mid * jax.nn.silu(shared_gate),
        ],
        axis=1,
    ).astype(low_type)
    grad_shgu = outer_dot(normed_mid, grad_shared_hidden)
    grad_normed = back_dot(grad_shared_hidden, shgu_full)
    grad_gates = jnp.sum(grad_final[:, None, :] * gathered_out, axis=2)
    grad_picked = gates * (grad_gates - jnp.sum(gates * grad_gates, axis=1, keepdims=True))
    grad_logits = jnp.sum(jnp.where(hits, grad_picked[:, :, None], 0.0), axis=1).astype(low_type)
    grad_router = outer_dot(normed_mid, grad_logits)
    grad_normed = grad_normed + back_dot(grad_logits, router_full)
    grad_outputs = (
        (gates[:, :, None] * grad_final[:, None, :]).astype(low_type).reshape(rows * TOP, width)
    )
    outgoing_grad = (
        jnp.zeros((experts, capacity, width), low_type).at[flat_route, flat_slot].set(grad_outputs)
    )
    arrived_grad = to_experts(outgoing_grad).reshape(-1, width)
    grad_expdown = outer_dot(middle_act, arrived_grad)
    grad_middle_act = back_dot(arrived_grad, expdown_full)
    grad_hidden = jnp.concatenate(
        [
            grad_middle_act * up_part * silu_grad(gate_part),
            grad_middle_act * jax.nn.silu(gate_part),
        ],
        axis=1,
    ).astype(low_type)
    grad_expgu = outer_dot(flat_in, grad_hidden)
    grad_in = back_dot(grad_hidden, expgu_full).astype(low_type).reshape(arrived.shape)
    returned_grad = from_experts(grad_in)
    grad_normed = grad_normed + jnp.sum(
        returned_grad[flat_route, flat_slot].reshape(rows, TOP, width).astype(full_type), axis=1
    )
    scaled_mid = grad_normed * gain_mid
    grad_gain_mid = jnp.sum(grad_normed * middle * inverse_mid, axis=0)
    grad_mid_total = (
        grad_final
        + inverse_mid * scaled_mid
        - middle * inverse_mid**3 * jnp.mean(scaled_mid * middle, axis=1, keepdims=True)
    )
    grad_branch = grad_mid_total.astype(low_type)
    grad_out_w = outer_dot(attended_tok, grad_branch)
    grad_attended = back_dot(grad_branch, out_full).astype(low_type)
    grad_heads = lax.all_to_all(
        grad_attended.reshape(1, rows, heads_axis, kv_local * GROUP * HEAD_DIM),
        "head",
        split_axis=2,
        concat_axis=0,
        tiled=True,
    )
    grad_heads = grad_heads.reshape(queries.shape)
    row_dot = jnp.sum(grad_heads.astype(full_type) * outputs, axis=-1)
    row_dot = jnp.transpose(row_dot, (1, 3, 4, 0, 2)).reshape(stat_shape)

    def piece_grads(grad_q, keys_part, values_part, start):
        count = keys_part.shape[0]
        scores, allowed = piece_scores(keys_part, start)
        weights = jnp.where(allowed, jnp.exp(scores - log_total[..., None]), 0.0)
        full_shape = (seqs, kv_local, GROUP, heads_axis, stretch, count, heads_axis, stretch)
        weights_low = weights.astype(low_type).reshape(full_shape)
        grad_weights = jnp.einsum(
            "astkgd,nbsukd->skgatnbu", grad_heads, values_part, preferred_element_type=full_type
        )
        grad_weights = grad_weights.reshape(weights.shape)
        grad_scores = (
            (weights * (grad_weights - row_dot[..., None])).astype(low_type).reshape(full_shape)
        )
        grad_q = (
            grad_q
            + jnp.einsum(
                "skgatnbu,nbsukd->astkgd", grad_scores, keys_part, preferred_element_type=full_type
            )
            * scale
        )
        piece_k = (
            jnp.einsum(
                "skgatnbu,astkgd->nbsukd", grad_scores, queries, preferred_element_type=full_type
            )
            * scale
        )
        piece_v = jnp.einsum(
            "skgatnbu,astkgd->nbsukd", weights_low, grad_heads, preferred_element_type=full_type
        )
        return (grad_q, piece_k, piece_v)

    def back_fold(carry, piece, start):
        grad_q, grad_k_all, grad_v_all = carry
        grad_q, piece_k, piece_v = piece_grads(grad_q, piece[0], piece[1], start)
        grad_k_all = lax.dynamic_update_slice_in_dim(grad_k_all, piece_k, start, 0)
        grad_v_all = lax.dynamic_update_slice_in_dim(grad_v_all, piece_v, start, 0)
        return (grad_q, grad_k_all, grad_v_all)

    buffer_shape = (blocks_axis,) + keys.shape
    start_carry = (
        jnp.zeros(queries.shape, full_type),
        jnp.zeros(buffer_shape, full_type),
        jnp.zeros(buffer_shape, full_type),
    )
    grad_q, grad_k_all, grad_v_all = local_fold(back_fold, start_carry, kept)
    key_sums = (
        lax.psum_scatter(grad_k_all, "blk", scatter_dimension=0, tiled=True),
        lax.psum_scatter(grad_v_all, "blk", scatter_dimension=0, tiled=True),
    )
    key_grad_sum = key_sums[0][0]
    value_grad_sum = key_sums[1][0]
    grad_stack = jnp.concatenate(
        [grad_q, key_grad_sum[:, :, :, :, None, :], value_grad_sum[:, :, :, :, None, :]], axis=4
    )
    grad_stack = grad_stack.astype(low_type).reshape(
        heads_axis, rows, 1, kv_local * (GROUP + 2) * HEAD_DIM
    )
    grad_projected = lax.all_to_all(
        grad_stack, "head", split_axis=0, concat_axis=2, tiled=True
    ).reshape(rows, qkv_full.shape[1])
    grad_qkv = outer_dot(normed_in, grad_projected)
    grad_normed_in = back_dot(grad_projected, qkv_full)
    scaled_in = grad_normed_in * gain_in
    grad_gain_in = jnp.sum(grad_normed_in * inputs * inverse_in, axis=0)
    grad_inputs = (
        grad_mid_total
        + inverse_in * scaled_in
        - inputs * inverse_in**3 * jnp.mean(scaled_in * inputs, axis=1, keepdims=True)
    )
    token_grad = grad_inputs.reshape(seqs, stretch, width)
    shares = (
        lax.psum_scatter(grad_qkv, ("head", "blk"), scatter_dimension=0, tiled=True),
        lax.psum_scatter(grad_out_w, ("head", "blk"), scatter_dimension=0, tiled=True),
        lax.psum_scatter(grad_shgu, ("head", "blk"), scatter_dimension=0, tiled=True),
        lax.psum_scatter(grad_shdown, ("head", "blk"), scatter_dimension=0, tiled=True),
        lax.psum_scatter(grad_router, ("head", "blk"), scatter_dimension=0, tiled=True),
        lax.psum_scatter(
            jnp.stack([grad_gain_in, grad_gain_mid]),
            ("head", "blk"),
            scatter_dimension=1,
            tiled=True,
        ),
    )
    g_qkv, g_out, g_shgu, g_shdown, g_router, g_gains = shares
    expert_shares = (
        lax.psum_scatter(
            grad_expgu[None].astype(jnp.bfloat16), "head", scatter_dimension=1, tiled=True
        ).astype(jnp.float32),
        lax.psum_scatter(
            grad_expdown[None].astype(jnp.bfloat16), "head", scatter_dimension=1, tiled=True
        ).astype(jnp.float32),
    )
    g_expgu, g_expdown = expert_shares
    local_squares = (
        jnp.sum(g_qkv * g_qkv)
        + jnp.sum(g_out * g_out)
        + jnp.sum(g_shgu * g_shgu)
        + jnp.sum(g_shdown * g_shdown)
        + jnp.sum(g_router * g_router)
        + jnp.sum(g_gains * g_gains)
        + jnp.sum(g_expgu * g_expgu)
        + jnp.sum(g_expdown * g_expdown)
    )
    squares, stat_total = lax.psum((local_squares, stat_sums), ("head", "blk"))
    count = jnp.sum(lengths).astype(full_type) * width
    stats = jnp.sqrt(stat_total / count)
    grad_norm = jnp.sqrt(squares)
    factor = clip_norm / jnp.maximum(grad_norm, clip_norm)
    a_qkv, b_qkv, c_qkv = adam_update(w_qkv, m_qkv, v_qkv, g_qkv, factor)
    a_out, b_out, c_out = adam_update(w_out, m_out, v_out, g_out, factor)
    a_shgu, b_shgu, c_shgu = adam_update(w_shgu, m_shgu, v_shgu, g_shgu, factor)
    a_shdown, b_shdown, c_shdown = adam_update(w_shdown, m_shdown, v_shdown, g_shdown, factor)
    a_router, b_router, c_router = adam_update(w_router, m_router, v_router, g_router, factor)
    a_gains, b_gains, c_gains = adam_update(w_gains, m_gains, v_gains, g_gains, factor)
    a_expgu, b_expgu, c_expgu = adam_update(w_expgu, m_expgu, v_expgu, g_expgu, factor)
    a_expdown, b_expdown, c_expdown = adam_update(
        w_expdown, m_expdown, v_expdown, g_expdown, factor
    )
    return (
        block_out,
        token_grad,
        g_qkv,
        a_qkv,
        b_qkv,
        c_qkv,
        g_out,
        a_out,
        b_out,
        c_out,
        g_shgu,
        a_shgu,
        b_shgu,
        c_shgu,
        g_shdown,
        a_shdown,
        b_shdown,
        c_shdown,
        g_router,
        a_router,
        b_router,
        c_router,
        g_gains,
        a_gains,
        b_gains,
        c_gains,
        g_expgu,
        a_expgu,
        b_expgu,
        c_expgu,
        g_expdown,
        a_expdown,
        b_expdown,
        c_expdown,
        grad_norm,
        stats,
    )


def local_cube(
    tokens,
    cotangent,
    lengths,
    routes,
    w_qkv,
    m_qkv,
    v_qkv,
    w_out,
    m_out,
    v_out,
    w_shgu,
    m_shgu,
    v_shgu,
    w_shdown,
    m_shdown,
    v_shdown,
    w_router,
    m_router,
    v_router,
    w_gains,
    m_gains,
    v_gains,
    w_expgu,
    m_expgu,
    v_expgu,
    w_expdown,
    m_expdown,
    v_expdown,
):
    low_type = jnp.bfloat16
    full_type = jnp.float32
    heads_axis = lax.axis_size("head")
    blocks_axis = lax.axis_size("blk")
    head_index = lax.axis_index("head")
    blk_index = lax.axis_index("blk")
    devices = heads_axis * blocks_axis
    me = head_index * blocks_axis + blk_index
    seqs, stretch, width = tokens.shape
    rows = seqs * stretch
    experts = w_router.shape[1]
    shard = w_qkv.shape[0]
    group_cols = (GROUP + 2) * HEAD_DIM
    query_cols = GROUP * HEAD_DIM
    extra = -(-(experts + 2) // 128) * 128
    tail = -(-2 * experts // 128) * 128
    all_orders = both_orders()
    row_orders = blk_orders()
    head_bits = axis_bits("head")

    small = jnp.concatenate([w_router, w_gains.T], axis=1)
    small = jnp.pad(small, ((0, 0), (0, extra - experts - 2)))
    half_cols = w_qkv.shape[1] // 2
    first_half, second_half = gather_rows(
        [
            w_qkv[:, :half_cols].astype(low_type),
            jnp.concatenate([w_qkv[:, half_cols:], small], axis=1).astype(low_type),
        ],
        all_orders,
    )
    router_full = second_half[:, half_cols : half_cols + experts]
    gains_full = second_half[:, half_cols + experts : half_cols + experts + 2].astype(full_type)
    second_half = second_half[:, :half_cols]
    gain_in = gains_full[:, 0][None]
    gain_mid = gains_full[:, 1][None]
    out_full = lax.all_gather(w_out.astype(low_type), ("head", "blk"), axis=0, tiled=True)
    shgu_full = lax.all_gather(w_shgu.astype(low_type), ("head", "blk"), axis=0, tiled=True)
    shdown_full = lax.all_gather(w_shdown.astype(low_type), ("head", "blk"), axis=0, tiled=True)

    own_pos = me * stretch + jnp.arange(stretch, dtype=jnp.int32)
    valid = (own_pos[None, :] < lengths[:, None]).astype(full_type).reshape(rows, 1)
    limit = jnp.minimum(own_pos[None, :], lengths[:, None] - 1).reshape(rows, 1)
    grad_final = cotangent.astype(full_type).reshape(rows, width) * valid
    grad_low = grad_final.astype(low_type)

    inputs = tokens.astype(full_type).reshape(rows, width)
    inverse_in = lax.rsqrt(jnp.mean(inputs * inputs, axis=1, keepdims=True) + norm_eps)
    normed_in = (inputs * inverse_in * gain_in).astype(low_type)
    projected = [
        jnp.dot(normed_in, half, preferred_element_type=full_type).astype(low_type)
        for half in (first_half, second_half)
    ]
    per_half = KV_HEADS // 2
    group_parts = [
        projected[g // per_half][:, (g % per_half) * group_cols : (g % per_half + 1) * group_cols]
        for g in range(KV_HEADS)
    ]
    queries = [part[:, :query_cols] for part in group_parts]
    kv_orders = [all_orders[g % 2] for g in range(KV_HEADS)]
    pairs = gather_relative([part[:, query_cols:] for part in group_parts], kv_orders)
    key_pos = [
        (block_devices(order)[:, None] * stretch + jnp.arange(stretch, dtype=jnp.int32)).reshape(
            1, -1
        )
        for order in all_orders
    ]

    route_rows = jnp.transpose(routes, (1, 0, 2)).reshape(rows, TOP)
    hits = route_rows[:, :, None] == jnp.arange(experts, dtype=jnp.int32)
    named = jnp.sum(hits.astype(full_type), axis=1)
    early = jnp.concatenate(
        [grad_low, jnp.pad(named, ((0, 0), (0, tail - experts))).astype(low_type)], axis=1
    )
    early, projected[0] = lax.optimization_barrier((early, projected[0]))

    def to_columns(values):
        pieces = gather_relative(list(values.reshape(seqs, stretch, -1)), row_orders)
        return jnp.concatenate([piece.reshape(-1, values.shape[1]) for piece in pieces], axis=0)

    def from_columns(values):
        pieces = values.reshape(seqs, blocks_axis, stretch, -1)
        return jnp.concatenate(scatter_relative(list(pieces), row_orders), axis=0)

    early_all = to_columns(early)
    grads_all = early_all[:, :width]
    named_all = early_all[:, width : width + experts] > 0

    def gather_head(values):
        own = values.astype(low_type)[None]
        for step in reversed(head_bits):
            mine = jnp.arange(2).reshape(2, 1, 1, 1) == own_bit(step)
            own = jnp.where(mine, own[None], swap(own, step)[None])
            own = own.reshape((-1,) + own.shape[2:])
        return own.reshape(-1, values.shape[1])

    def scatter_head(values):
        for step in head_bits:
            half = values.shape[0] // 2
            bit = own_bit(step)
            mine = lax.dynamic_slice_in_dim(values, bit * half, half, 0)
            theirs = lax.dynamic_slice_in_dim(values, (1 - bit) * half, half, 0)
            values = mine + swap(theirs.astype(low_type), step).astype(full_type)
        return values

    expgu_full = gather_head(w_expgu[0])
    expdown_full = gather_head(w_expdown[0])

    attended = [
        attend(queries[g], pairs[g], key_pos[g % 2], limit, seqs, stretch)
        for g in range(KV_HEADS)
    ]
    attended_tok = jnp.concatenate([item[1] for item in attended], axis=1)
    branch = jnp.dot(attended_tok, out_full, preferred_element_type=full_type)
    middle = inputs + branch
    inverse_mid = lax.rsqrt(jnp.mean(middle * middle, axis=1, keepdims=True) + norm_eps)
    normed_mid = (middle * inverse_mid * gain_mid).astype(low_type)

    def all_gates(values, chosen):
        logits = jnp.dot(values, router_full, preferred_element_type=full_type)
        logits = jnp.where(chosen, logits, masked_score)
        raised = jnp.where(chosen, jnp.exp(logits - jnp.max(logits, axis=1, keepdims=True)), 0.0)
        return raised / jnp.sum(raised, axis=1, keepdims=True)

    own_expert = jnp.arange(experts, dtype=jnp.int32)[None] == blk_index
    mid_all = to_columns(normed_mid)
    gate = jnp.sum(
        jnp.where(own_expert, all_gates(mid_all, named_all), 0.0), axis=1, keepdims=True
    )
    hidden = jnp.dot(mid_all, expgu_full, preferred_element_type=full_type)
    gate_part = hidden[:, :EXPERT_FF]
    up_part = hidden[:, EXPERT_FF:]
    middle_act = (jax.nn.silu(gate_part) * up_part).astype(low_type).astype(full_type)
    weighed_act = (gate * middle_act).astype(low_type)
    pulled = back_dot(grads_all, expdown_full)
    routed_terms = jnp.dot(weighed_act, expdown_full, preferred_element_type=full_type)
    grad_gate = jnp.sum(pulled * middle_act, axis=1, keepdims=True)
    grad_middle_act = gate * pulled
    grad_hidden = jnp.concatenate(
        [
            grad_middle_act * up_part * silu_grad(gate_part),
            grad_middle_act * jax.nn.silu(gate_part),
        ],
        axis=1,
    ).astype(low_type)
    gate_high = grad_gate.astype(low_type).astype(full_type)
    lanes = jnp.arange(tail, dtype=jnp.int32)[None]
    gate_lanes = jnp.where(lanes == blk_index, gate_high, 0.0) + jnp.where(
        lanes == experts + blk_index, grad_gate - gate_high, 0.0
    )
    in_terms = jnp.concatenate([back_dot(grad_hidden, expgu_full), gate_lanes], axis=1)
    back_sums = from_columns(in_terms.astype(low_type)).astype(full_type)
    routed = from_columns(routed_terms.astype(low_type)).astype(full_type)
    grad_expdown = outer_dot(weighed_act, grads_all)
    grad_expgu = outer_dot(mid_all, grad_hidden)
    g_expgu = scatter_head(grad_expgu)[None]
    g_expdown = scatter_head(grad_expdown)[None]

    shared_hidden = jnp.dot(normed_mid, shgu_full, preferred_element_type=full_type)
    shared_gate = shared_hidden[:, :SHARED]
    shared_up = shared_hidden[:, SHARED:]
    shared_mid = (jax.nn.silu(shared_gate) * shared_up).astype(low_type)
    shared_out = jnp.dot(shared_mid, shdown_full, preferred_element_type=full_type)
    final = middle + routed + shared_out
    block_out = final.astype(low_type).reshape(seqs, stretch, width)
    stat_sums = jnp.stack(
        [
            jnp.sum(branch * branch * valid),
            jnp.sum(middle * middle * valid),
            jnp.sum(final * final * valid),
        ]
    )

    def sum_rows(values):
        return lax.psum_scatter(
            values.astype(low_type), ("head", "blk"), scatter_dimension=0, tiled=True
        ).astype(full_type)

    grad_shdown = outer_dot(shared_mid, grad_low)
    grad_shared_mid = back_dot(grad_low, shdown_full)
    grad_shared_hidden = jnp.concatenate(
        [
            grad_shared_mid * shared_up * silu_grad(shared_gate),
            grad_shared_mid * jax.nn.silu(shared_gate),
        ],
        axis=1,
    ).astype(low_type)
    grad_shgu = outer_dot(normed_mid, grad_shared_hidden)
    g_shdown = sum_rows(grad_shdown)
    g_shgu = sum_rows(grad_shgu)
    grad_normed = back_dot(grad_shared_hidden, shgu_full)

    chosen = named > 0
    gates = all_gates(normed_mid, chosen)
    grad_gates = back_sums[:, width : width + experts] + (
        back_sums[:, width + experts : width + 2 * experts]
    )
    grad_logits = gates * (grad_gates - jnp.sum(gates * grad_gates, axis=1, keepdims=True))
    grad_logits = jnp.where(chosen, grad_logits, 0.0).astype(low_type)
    grad_router = outer_dot(normed_mid, grad_logits)
    grad_normed = grad_normed + back_dot(grad_logits, router_full) + back_sums[:, :width]
    scaled_mid = grad_normed * gain_mid
    grad_gain_mid = jnp.sum(grad_normed * middle * inverse_mid, axis=0)
    grad_mid_total = (
        grad_final
        + inverse_mid * scaled_mid
        - middle * inverse_mid**3 * jnp.mean(scaled_mid * middle, axis=1, keepdims=True)
    )
    grad_branch = grad_mid_total.astype(low_type)
    grad_attended = back_dot(grad_branch, out_full).astype(low_type)
    g_out = sum_rows(outer_dot(attended_tok, grad_branch))

    back = [
        attend_back(
            queries[g],
            pairs[g],
            key_pos[g % 2],
            limit,
            grad_attended[:, g * query_cols : (g + 1) * query_cols],
            attended[g][0],
            attended[g][2],
            seqs,
            stretch,
        )
        for g in range(KV_HEADS)
    ]
    pair_sums = scatter_relative([item[1] for item in back], kv_orders)
    grad_groups = [
        jnp.concatenate([item[0], pair], axis=1) for item, pair in zip(back, pair_sums)
    ]
    grad_halves = [
        jnp.concatenate(grad_groups[:per_half], axis=1),
        jnp.concatenate(grad_groups[per_half:], axis=1),
    ]
    grad_normed_in = back_dot(grad_halves[0], first_half) + back_dot(grad_halves[1], second_half)
    scaled_in = grad_normed_in * gain_in
    grad_gain_in = jnp.sum(grad_normed_in * inputs * inverse_in, axis=0)
    grad_inputs = (
        grad_mid_total
        + inverse_in * scaled_in
        - inputs * inverse_in**3 * jnp.mean(scaled_in * inputs, axis=1, keepdims=True)
    )
    token_grad = grad_inputs.reshape(seqs, stretch, width)
    grad_small = jnp.concatenate(
        [grad_router, jnp.stack([grad_gain_in, grad_gain_mid], axis=1)], axis=1
    )
    grad_small = jnp.pad(grad_small, ((0, 0), (0, extra - experts - 2)))
    sums = scatter_rows(
        [
            outer_dot(normed_in, grad_halves[0]).astype(low_type),
            jnp.concatenate([outer_dot(normed_in, grad_halves[1]), grad_small], axis=1).astype(
                low_type
            ),
        ],
        all_orders,
    )
    g_qkv = jnp.concatenate([sums[0], sums[1][:, :half_cols]], axis=1).astype(full_type)
    g_router = sums[1][:, half_cols : half_cols + experts].astype(full_type)
    g_gains = sums[1][:, half_cols + experts : half_cols + experts + 2].astype(full_type).T

    local_squares = (
        jnp.sum(g_qkv * g_qkv)
        + jnp.sum(g_out * g_out)
        + jnp.sum(g_shgu * g_shgu)
        + jnp.sum(g_shdown * g_shdown)
        + jnp.sum(g_router * g_router)
        + jnp.sum(g_gains * g_gains)
        + jnp.sum(g_expgu * g_expgu)
        + jnp.sum(g_expdown * g_expdown)
    )
    scalars = jnp.concatenate([local_squares[None], stat_sums])
    totals = sum_everywhere(jnp.pad(scalars, (0, 124)).reshape(1, 128))[0]
    count = jnp.sum(lengths).astype(full_type) * width
    stats = jnp.sqrt(totals[1:4] / count)
    grad_norm = jnp.sqrt(totals[0])
    factor = clip_norm / jnp.maximum(grad_norm, clip_norm)
    outputs = [block_out, token_grad]
    for weight, first, second, grad in (
        (w_qkv, m_qkv, v_qkv, g_qkv),
        (w_out, m_out, v_out, g_out),
        (w_shgu, m_shgu, v_shgu, g_shgu),
        (w_shdown, m_shdown, v_shdown, g_shdown),
        (w_router, m_router, v_router, g_router),
        (w_gains, m_gains, v_gains, g_gains),
        (w_expgu, m_expgu, v_expgu, g_expgu),
        (w_expdown, m_expdown, v_expdown, g_expdown),
    ):
        outputs.append(grad)
        outputs.extend(adam_update(weight, first, second, grad, factor))
    return (*outputs, grad_norm, stats)


def solution(mesh):
    in_specs = (
        P(None, ("head", "blk"), None),
        P(None, ("head", "blk"), None),
        P(),
        P(("head", "blk"), None, None),
        P(("head", "blk"), None),
        P(("head", "blk"), None),
        P(("head", "blk"), None),
        P(("head", "blk"), None),
        P(("head", "blk"), None),
        P(("head", "blk"), None),
        P(("head", "blk"), None),
        P(("head", "blk"), None),
        P(("head", "blk"), None),
        P(("head", "blk"), None),
        P(("head", "blk"), None),
        P(("head", "blk"), None),
        P(("head", "blk"), None),
        P(("head", "blk"), None),
        P(("head", "blk"), None),
        P(None, ("head", "blk")),
        P(None, ("head", "blk")),
        P(None, ("head", "blk")),
        P("blk", "head", None),
        P("blk", "head", None),
        P("blk", "head", None),
        P("blk", "head", None),
        P("blk", "head", None),
        P("blk", "head", None),
    )
    out_specs = (
        P(None, ("head", "blk"), None),
        P(None, ("head", "blk"), None),
        P(("head", "blk"), None),
        P(("head", "blk"), None),
        P(("head", "blk"), None),
        P(("head", "blk"), None),
        P(("head", "blk"), None),
        P(("head", "blk"), None),
        P(("head", "blk"), None),
        P(("head", "blk"), None),
        P(("head", "blk"), None),
        P(("head", "blk"), None),
        P(("head", "blk"), None),
        P(("head", "blk"), None),
        P(("head", "blk"), None),
        P(("head", "blk"), None),
        P(("head", "blk"), None),
        P(("head", "blk"), None),
        P(("head", "blk"), None),
        P(("head", "blk"), None),
        P(("head", "blk"), None),
        P(("head", "blk"), None),
        P(None, ("head", "blk")),
        P(None, ("head", "blk")),
        P(None, ("head", "blk")),
        P(None, ("head", "blk")),
        P("blk", "head", None),
        P("blk", "head", None),
        P("blk", "head", None),
        P("blk", "head", None),
        P("blk", "head", None),
        P("blk", "head", None),
        P("blk", "head", None),
        P("blk", "head", None),
        P(),
        P(),
    )
    shards = mesh.size
    cubes = all(size & (size - 1) == 0 for size in mesh.shape.values())
    step = local_cube if cubes and WIDTH_ROWS % (16 * shards) == 0 else local
    return jax.shard_map(step, mesh=mesh, in_specs=in_specs, out_specs=out_specs, check_vma=False)
```

```python
import functools

import functools

import jax
import jax.numpy as jnp
from jax import lax
from jax.experimental import pallas as pl
from jax.experimental.pallas import tpu as pltpu
from jax.sharding import PartitionSpec as P

HEADS = 12
KV_HEADS = 4
HEAD_DIM = 128
EXPERT_FF = 512
SHARED = 1024
TOP = 6
ADAM_STEP = 10
GROUP = 3


norm_eps = 1e-05
adam_eps = 1e-08
learn_rate = 0.02
first_decay = 0.9
second_decay = 0.999
weight_decay = 0.1
clip_norm = 1.0
masked_score = -1e30
group_turn = 4


def to_experts(buffer):
    return lax.all_to_all(buffer, "blk", split_axis=0, concat_axis=0, tiled=True)


def from_experts(buffer):
    return lax.all_to_all(buffer, "blk", split_axis=0, concat_axis=0, tiled=True)


def outer_dot(left, right):
    return lax.dot_general(
        left, right, (((0,), (0,)), ((), ())), preferred_element_type=jnp.float32
    )


def back_dot(left, right):
    return lax.dot_general(
        left, right, (((1,), (1,)), ((), ())), preferred_element_type=jnp.float32
    )


def silu_grad(values):
    logistic = jax.nn.sigmoid(values)
    return logistic * (1.0 + values * (1.0 - logistic))


def local_fold(function, init, gathered):
    turns = gathered[0].shape[0] // group_turn

    def advance(turn, carry):
        start = turn * group_turn
        piece = (
            lax.dynamic_slice_in_dim(gathered[0], start, group_turn, 0),
            lax.dynamic_slice_in_dim(gathered[1], start, group_turn, 0),
        )
        return function(carry, piece, start)

    return lax.fori_loop(0, turns, advance, init)


def adam_update(weight, first, second, grad, factor):
    clipped = grad * factor
    first_new = first_decay * first + (1.0 - first_decay) * clipped
    second_new = second_decay * second + (1.0 - second_decay) * clipped * clipped
    first_fix = 1.0 - first_decay**ADAM_STEP
    second_fix = 1.0 - second_decay**ADAM_STEP
    change = -learn_rate * (
        first_new / first_fix / (jnp.sqrt(second_new / second_fix) + adam_eps)
        + weight_decay * weight
    )
    return (first_new, second_new, change)


WAVES_KV = (0, 0, 1, 1)
WAVES_COL = None
WIDTH_ROWS = 512


def axis_bits(name):
    size = lax.axis_size(name)
    return [(name, 1 << k) for k in reversed(range(size.bit_length() - 1))]


def swap(values, step):
    name, bit = step
    size = lax.axis_size(name)
    return lax.ppermute(values, name, [(i, i ^ bit) for i in range(size)])


def after(values, *earlier):
    return lax.optimization_barrier((values, earlier))[0]


def own_bit(step):
    return (lax.axis_index(step[0]) // step[1]) % 2


def both_orders():
    head_bits, blk_bits = axis_bits("head"), axis_bits("blk")
    first = blk_bits[:-1] + head_bits + blk_bits[-1:]
    second = blk_bits[:-2] + head_bits + blk_bits[-2:]
    return (first, second)


def blk_orders():
    blk_bits = axis_bits("blk")
    return (blk_bits, blk_bits[-2:-1] + blk_bits[:-2] + blk_bits[-1:])


def lockstep(pieces, orders, act, backwards=False, waves=None, beside=None):
    count = len(orders[0])
    pieces = list(pieces)
    for turn, at in enumerate(reversed(range(count)) if backwards else range(count)):
        before = list(pieces)
        for place, order in enumerate(orders):
            piece = pieces[place]
            if waves is not None and waves[place] > 0:
                ahead = [p for p, wave in zip(pieces, waves) if wave == waves[place] - 1]
                piece = after(piece, ahead)
            pieces[place] = act(piece, order[at])
        if beside is not None:
            work, results = beside
            if work is None:
                pieces = lax.optimization_barrier(pieces)
            elif turn in work:
                found = work[turn](before)
                pieces, found = lax.optimization_barrier((pieces, found))
                results.append(found)
    return pieces


def gather_relative(pieces, orders, waves=None, beside=None):
    def act(piece, step):
        piece = piece[0] if len(piece) == 1 else jnp.concatenate(piece, axis=0)
        return (piece, swap(piece, step))

    return lockstep([(piece[None],) for piece in pieces], orders, act, False, waves, beside)


def scatter_relative(pieces, orders, waves=None, beside=None):
    def act(piece, step):
        kept, sent = piece
        total = kept + swap(sent, step)
        half = total.shape[0] // 2
        return (total[:half], total[half:]) if half else total

    return [piece[0] for piece in lockstep(pieces, orders, act, True, waves, beside)]


def transpose_blk(values):
    places = axis_bits("blk")
    shape = values.shape
    values = values.reshape((2,) * len(places) + shape[1:])
    for place, step in enumerate(places):
        bit = own_bit(step)
        mine = lax.dynamic_slice_in_dim(values, bit, 1, place)
        theirs = lax.dynamic_slice_in_dim(values, 1 - bit, 1, place)
        index = [1] * values.ndim
        index[place] = 2
        here = lax.broadcasted_iota(jnp.int32, index, place) == bit
        values = jnp.where(here, mine, swap(theirs, step))
    return values.reshape(shape)


def gather_rows(pieces, orders):
    places = axis_bits("head") + axis_bits("blk")

    def act(piece, step):
        place = places.index(step)
        shape = [1] * piece.ndim
        shape[place] = 2
        mine = lax.broadcasted_iota(jnp.int32, shape, place) == own_bit(step)
        return jnp.where(mine, piece, swap(piece, step))

    wide = [piece.reshape((1,) * len(places) + piece.shape) for piece in pieces]
    return [
        full.reshape(-1, full.shape[-1])
        for full in lockstep(wide, orders, act, beside=(None, []))
    ]


def scatter_rows(pieces, orders):
    places = axis_bits("head") + axis_bits("blk")
    devices = 1 << len(places)

    def act(piece, step):
        place = places.index(step)
        bit = own_bit(step)
        mine = lax.dynamic_slice_in_dim(piece, bit, 1, place)
        theirs = lax.dynamic_slice_in_dim(piece, 1 - bit, 1, place)
        return mine + swap(theirs, step)

    wide = [
        piece.reshape((2,) * len(places) + (piece.shape[0] // devices, piece.shape[1]))
        for piece in pieces
    ]
    return [
        own.reshape(own.shape[-2:])
        for own in lockstep(wide, orders, act, True)
    ]


def swap_both(values, first, second):
    sizes = {name: lax.axis_size(name) for name in ("head", "blk")}
    flip = {"head": 0, "blk": 0}
    for name, bit in (first, second):
        flip[name] ^= bit
    pairs = [
        (h * sizes["blk"] + b, (h ^ flip["head"]) * sizes["blk"] + (b ^ flip["blk"]))
        for h in range(sizes["head"])
        for b in range(sizes["blk"])
    ]
    return lax.ppermute(values, ("head", "blk"), pairs)


def sum_everywhere(values):
    blk_bits = axis_bits("blk")
    steps = blk_bits[:-1] + axis_bits("head")
    while len(steps) > 1:
        first, second, steps = steps[0], steps[1], steps[2:]
        values = (values + swap(values, first)) + (
            swap(values, second) + swap_both(values, first, second)
        )
    for step in steps + blk_bits[-1:]:
        values = values + swap(values, step)
    return values


def blk_blocks(order):
    offsets = [0]
    for _, bit in order:
        offsets = offsets + [offset ^ bit for offset in offsets]
    return lax.axis_index("blk") ^ jnp.array(offsets, jnp.int32)


def block_devices(order):
    offsets = [(0, 0)]
    for name, bit in order:
        offsets = offsets + [
            (h ^ bit, b) if name == "head" else (h, b ^ bit) for h, b in offsets
        ]
    head_index, blk_index = lax.axis_index("head"), lax.axis_index("blk")
    heads = jnp.array([h for h, _ in offsets], jnp.int32)
    blks = jnp.array([b for _, b in offsets], jnp.int32)
    return (head_index ^ heads) * lax.axis_size("blk") + (blk_index ^ blks)


def stack_heads(block):
    return jnp.concatenate(
        [block[:, i * HEAD_DIM : (i + 1) * HEAD_DIM] for i in range(GROUP)], axis=0
    )


def group_scores(query, keys, limit, key_pos):
    scores = lax.dot_general(
        query, keys, (((1,), (1,)), ((), ())), preferred_element_type=jnp.float32
    ) * (HEAD_DIM ** (-0.5))
    return jnp.where(key_pos <= limit, scores, masked_score)


def join(low_ref, high_ref, start):
    parts = [ref[:, :, start : start + HEAD_DIM].reshape(-1, HEAD_DIM) for ref in (low_ref, high_ref)]
    return jnp.concatenate(parts, axis=0)


def attend_kernel(q_ref, kv0_ref, kv1_ref, pos_ref, limit_ref, out_ref, low_ref, log_ref):
    stretch = q_ref.shape[0]
    query = stack_heads(q_ref[...])
    keys = join(kv0_ref, kv1_ref, 0)
    values = join(kv0_ref, kv1_ref, HEAD_DIM)
    limit = jnp.concatenate([limit_ref[...]] * GROUP, axis=0)
    scores = group_scores(query, keys, limit, pos_ref[...])
    top = jnp.max(scores, axis=1, keepdims=True)
    weights = jnp.exp(scores - top)
    total = jnp.sum(weights, axis=1, keepdims=True)
    out = jnp.dot(weights.astype(jnp.bfloat16), values, preferred_element_type=jnp.float32)
    out = out / total
    log_ref[0] = top + jnp.log(total)
    for i in range(GROUP):
        part = out[i * stretch : (i + 1) * stretch]
        columns = slice(i * HEAD_DIM, (i + 1) * HEAD_DIM)
        out_ref[:, columns] = part
        low_ref[:, columns] = part.astype(jnp.bfloat16)


def attend_back_kernel(
    q_ref,
    kv0_ref,
    kv1_ref,
    pos_ref,
    limit_ref,
    grad_ref,
    out_ref,
    log_ref,
    dq_ref,
    dkv0_ref,
    dkv1_ref,
):
    stretch = q_ref.shape[0]
    scale = HEAD_DIM ** (-0.5)
    low_type = jnp.bfloat16
    query = stack_heads(q_ref[...])
    keys = join(kv0_ref, kv1_ref, 0)
    values = join(kv0_ref, kv1_ref, HEAD_DIM)
    grad = stack_heads(grad_ref[...])
    row_dot = jnp.sum(
        grad.astype(jnp.float32) * stack_heads(out_ref[...]), axis=1, keepdims=True
    )
    limit = jnp.concatenate([limit_ref[...]] * GROUP, axis=0)
    scores = group_scores(query, keys, limit, pos_ref[...])
    weights = jnp.exp(scores - log_ref[0])
    grad_weights = lax.dot_general(
        grad, values, (((1,), (1,)), ((), ())), preferred_element_type=jnp.float32
    )
    grad_scores = (weights * (grad_weights - row_dot)).astype(low_type)
    weights_low = weights.astype(low_type)
    dq = jnp.dot(grad_scores, keys, preferred_element_type=jnp.float32) * scale
    dk = outer_dot(grad_scores, query) * scale
    dv = outer_dot(weights_low, grad)
    block = dkv0_ref.shape[:2] + (HEAD_DIM,)
    half = dk.shape[0] // 2
    for start, ref in ((0, dkv0_ref), (half, dkv1_ref)):
        ref[:, :, :HEAD_DIM] = dk[start : start + half].astype(low_type).reshape(block)
        ref[:, :, HEAD_DIM:] = dv[start : start + half].astype(low_type).reshape(block)
    for i in range(GROUP):
        part = dq[i * stretch : (i + 1) * stretch]
        dq_ref[:, i * HEAD_DIM : (i + 1) * HEAD_DIM] = part.astype(low_type)


def attention_specs(stretch, devices):
    wide = pl.BlockSpec((stretch, GROUP * HEAD_DIM), lambda g: (0, g))
    pair = pl.BlockSpec((devices // 2, stretch, 2 * HEAD_DIM), lambda g: (0, 0, g))
    pos = pl.BlockSpec((1, devices * stretch), lambda g: (0, 0))
    limit = pl.BlockSpec((stretch, 1), lambda g: (0, 0))
    log = pl.BlockSpec((1, GROUP * stretch, 1), lambda g: (g, 0, 0))
    return wide, pair, pos, limit, log


def attention_cost(groups, stretch, devices, matmuls):
    scores = groups * GROUP * stretch * devices * stretch
    return pl.CostEstimate(
        flops=2 * matmuls * scores * HEAD_DIM,
        bytes_accessed=devices * groups * stretch * 2 * HEAD_DIM * 2,
        transcendentals=scores,
    )


def attend(query, pair, key_pos, limit):
    stretch = query.shape[0]
    groups = query.shape[1] // (GROUP * HEAD_DIM)
    devices = 2 * pair[0].shape[0]
    wide, kv, pos, lim, log = attention_specs(stretch, devices)
    return pl.pallas_call(
        attend_kernel,
        grid=(groups,),
        in_specs=[wide, kv, kv, pos, lim],
        out_specs=[wide, wide, log],
        out_shape=[
            jax.ShapeDtypeStruct(query.shape, jnp.float32),
            jax.ShapeDtypeStruct(query.shape, jnp.bfloat16),
            jax.ShapeDtypeStruct((groups, GROUP * stretch, 1), jnp.float32),
        ],
        compiler_params=pltpu.CompilerParams(vmem_limit_bytes=48 << 20),
        cost_estimate=attention_cost(groups, stretch, devices, 2),
        name="attend",
    )(query, *pair, key_pos, limit)


def attend_back(query, pair, key_pos, limit, grad, out, log_total):
    stretch = query.shape[0]
    groups = query.shape[1] // (GROUP * HEAD_DIM)
    devices = 2 * pair[0].shape[0]
    wide, kv, pos, lim, log = attention_specs(stretch, devices)
    return pl.pallas_call(
        attend_back_kernel,
        grid=(groups,),
        in_specs=[wide, kv, kv, pos, lim, wide, wide, log],
        out_specs=[wide, kv, kv],
        out_shape=[
            jax.ShapeDtypeStruct(query.shape, jnp.bfloat16),
            jax.ShapeDtypeStruct(pair[0].shape, jnp.bfloat16),
            jax.ShapeDtypeStruct(pair[1].shape, jnp.bfloat16),
        ],
        compiler_params=pltpu.CompilerParams(vmem_limit_bytes=48 << 20),
        cost_estimate=attention_cost(groups, stretch, devices, 5),
        name="attend_back",
    )(query, *pair, key_pos, limit, grad, out, log_total)


def expert_kernel(blocks, place_ref, low_ref, high_ref, router_ref, own_ref, gu_ref, *refs):
    pulled_refs, named_refs = refs[:blocks], refs[blocks : 2 * blocks]
    out_low_ref, out_high_ref, act_ref, hid_ref = refs[2 * blocks :]
    low_type = jnp.bfloat16
    turn = pl.program_id(0)
    half = pl.num_programs(0) // 2
    first = jnp.where(turn < half, half + turn, turn - half) * blocks
    values = jnp.where(turn < half, high_ref[...], low_ref[...])
    width = values.shape[1]
    stretch = values.shape[0] // blocks
    chosen = jnp.concatenate([ref[...].reshape(stretch, -1) for ref in named_refs], axis=0) > 0
    pulled = jnp.concatenate([ref[...].reshape(stretch, -1) for ref in pulled_refs], axis=0)
    logits = jnp.dot(values, router_ref[...], preferred_element_type=jnp.float32)
    logits = jnp.where(chosen, logits, masked_score)
    raised = jnp.where(chosen, jnp.exp(logits - jnp.max(logits, axis=1, keepdims=True)), 0.0)
    own = own_ref[...]
    gate = jnp.sum(raised * own[:1], axis=1, keepdims=True) / jnp.sum(
        raised, axis=1, keepdims=True
    )
    hidden = jnp.dot(values, gu_ref[...], preferred_element_type=jnp.float32)
    shared = (hidden.shape[1] - 2 * EXPERT_FF) // 2

    def mixed(gate_part, up_part, grad_act, start):
        logistic = 1.0 / (1.0 + jnp.exp(-gate_part))
        smooth = gate_part * logistic
        slope = logistic * (1.0 + gate_part * (1.0 - logistic))
        size = gate_part.shape[1]
        hid_ref[:, start : start + size] = (grad_act * up_part * slope).astype(low_type)
        hid_ref[:, start + size : start + 2 * size] = (grad_act * smooth).astype(low_type)
        return (smooth * up_part).astype(low_type)

    start = 2 * EXPERT_FF
    act = mixed(
        hidden[:, :EXPERT_FF], hidden[:, EXPERT_FF:start], gate * pulled[:, :EXPERT_FF], 0
    ).astype(jnp.float32)
    grad_gate = jnp.sum(pulled[:, :EXPERT_FF] * act, axis=1, keepdims=True)
    shared_act = mixed(
        hidden[:, start : start + shared],
        hidden[:, start + shared :],
        pulled[:, EXPERT_FF : EXPERT_FF + shared],
        start,
    )
    rest = act_ref.shape[2] - EXPERT_FF - shared
    acts = jnp.concatenate(
        [
            (gate * act).astype(low_type),
            shared_act,
            jnp.zeros((values.shape[0], rest), low_type),
        ],
        axis=1,
    )
    for block in range(blocks):
        act_ref[place_ref[first + block]] = acts[block * stretch : (block + 1) * stretch]
    out = back_dot(hid_ref[...], gu_ref[...]).astype(low_type)
    high = grad_gate.astype(low_type).astype(jnp.float32)
    lanes = (high * own[:1] + (grad_gate - high) * own[1:]).astype(low_type)

    @pl.when(turn < half)
    def _():
        out_high_ref[:, :width] = out
        out_high_ref[:, width:] = lanes

    @pl.when(turn >= half)
    def _():
        out_low_ref[:, :width] = out
        out_low_ref[:, width:] = lanes


def run_expert(mid, pulled, early, router, own, gate_up, places, seq):
    rows, width = mid[0].shape
    devices, _, stretch, acts = pulled.shape
    block = min(rows, 256)
    blocks = block // stretch
    half = rows // block
    lanes = own.shape[1]
    hid = gate_up.shape[1]
    low_type = jnp.bfloat16

    def fixed(shape):
        return pl.BlockSpec(shape, lambda i, _: (0,) * len(shape))

    def first(i):
        return jnp.where(i < half, half + i, i - half) * blocks

    def scattered(piece, size, column):
        return pl.BlockSpec(
            (1, 1, stretch, size), lambda i, place: (place[first(i) + piece], seq, 0, column)
        )

    def low_rows(size):
        return pl.BlockSpec((block, size), lambda i, _: (jnp.maximum(i - half, 0), 0))

    def high_rows(size):
        return pl.BlockSpec((block, size), lambda i, _: (jnp.minimum(i, half - 1), 0))

    return pl.pallas_call(
        functools.partial(expert_kernel, blocks),
        grid_spec=pltpu.PrefetchScalarGridSpec(
            num_scalar_prefetch=1,
            grid=(2 * half,),
            in_specs=[
                low_rows(width),
                high_rows(width),
                fixed(router.shape),
                fixed(own.shape),
                fixed(gate_up.shape),
            ]
            + [scattered(piece, acts, 0) for piece in range(blocks)]
            + [scattered(piece, lanes, width // lanes) for piece in range(blocks)],
            out_specs=[
                low_rows(width + lanes),
                high_rows(width + lanes),
                fixed((devices, stretch, acts)),
                pl.BlockSpec((block, hid), lambda i, _: (first(i) // blocks, 0)),
            ],
        ),
        out_shape=[
            jax.ShapeDtypeStruct((rows, width + lanes), low_type),
            jax.ShapeDtypeStruct((rows, width + lanes), low_type),
            jax.ShapeDtypeStruct((devices, stretch, acts), low_type),
            jax.ShapeDtypeStruct((2 * rows, hid), low_type),
        ],
        compiler_params=pltpu.CompilerParams(vmem_limit_bytes=48 << 20),
        cost_estimate=pl.CostEstimate(
            flops=8 * rows * width * hid,
            bytes_accessed=4 * rows * (2 * width + 3 * acts + hid),
            transcendentals=2 * rows * acts,
        ),
        name="expert",
    )(places, mid[0], mid[1], router, own, gate_up, *[pulled] * blocks, *[early] * blocks)


def outer_experts_kernel(low0_ref, high0_ref, low1_ref, high1_ref, right0_ref, right1_ref, out_ref):
    total = None
    rows = low0_ref.shape[0]
    for refs, right in (((low0_ref, high0_ref), right0_ref), ((low1_ref, high1_ref), right1_ref)):
        for part, ref in enumerate(refs):
            term = outer_dot(ref[...], right[part * rows : (part + 1) * rows])
            total = term if total is None else total + term
    out_ref[...] = total.astype(out_ref.dtype)


def outer_experts(mid, hids):
    rows, width = mid[0][0].shape
    columns = hids[0].shape[1]
    block = 256
    lefts = pl.BlockSpec((rows, block), lambda i: (0, i))
    rights = pl.BlockSpec((2 * rows, columns), lambda i: (0, 0))
    return pl.pallas_call(
        outer_experts_kernel,
        grid=(width // block,),
        in_specs=[lefts] * 4 + [rights] * 2,
        out_specs=pl.BlockSpec((block, columns), lambda i: (i, 0)),
        out_shape=jax.ShapeDtypeStruct((width, columns), jnp.bfloat16),
        compiler_params=pltpu.CompilerParams(vmem_limit_bytes=48 << 20),
        cost_estimate=pl.CostEstimate(
            flops=8 * rows * width * columns,
            bytes_accessed=8 * rows * (width + columns) + 2 * width * columns,
            transcendentals=0,
        ),
        name="outer_experts",
    )(*mid[0], *mid[1], *hids)


def outer_acts_kernel(left0_ref, left1_ref, right_ref, out_ref):
    total = None
    for seq, ref in enumerate((left0_ref, left1_ref)):
        left = ref[...].reshape(-1, ref.shape[2])
        right = right_ref[:, seq].reshape(-1, right_ref.shape[3])
        term = outer_dot(left, right)
        total = term if total is None else total + term
    out_ref[...] = total.astype(out_ref.dtype)


def outer_acts(acts, early, width):
    devices, stretch, size = acts[0].shape
    block = 128
    lefts = pl.BlockSpec((devices, stretch, block), lambda i: (0, 0, i))
    rights = pl.BlockSpec((devices, 2, stretch, width), lambda i: (0, 0, 0, 0))
    return pl.pallas_call(
        outer_acts_kernel,
        grid=(size // block,),
        in_specs=[lefts] * 2 + [rights],
        out_specs=pl.BlockSpec((block, width), lambda i: (i, 0)),
        out_shape=jax.ShapeDtypeStruct((size, width), jnp.bfloat16),
        compiler_params=pltpu.CompilerParams(vmem_limit_bytes=48 << 20),
        cost_estimate=pl.CostEstimate(
            flops=4 * devices * stretch * size * width,
            bytes_accessed=4 * devices * stretch * (width + size) + 2 * size * width,
            transcendentals=0,
        ),
        name="outer_acts",
    )(*acts, early)


def local(
    tokens,
    cotangent,
    lengths,
    routes,
    w_qkv,
    m_qkv,
    v_qkv,
    w_out,
    m_out,
    v_out,
    w_shgu,
    m_shgu,
    v_shgu,
    w_shdown,
    m_shdown,
    v_shdown,
    w_router,
    m_router,
    v_router,
    w_gains,
    m_gains,
    v_gains,
    w_expgu,
    m_expgu,
    v_expgu,
    w_expdown,
    m_expdown,
    v_expdown,
):
    low_type = jnp.bfloat16
    full_type = jnp.float32
    heads_axis = lax.axis_size("head")
    blocks_axis = lax.axis_size("blk")
    head_index = lax.axis_index("head")
    blk_index = lax.axis_index("blk")
    seqs, stretch, width = tokens.shape
    rows = seqs * stretch
    experts = w_router.shape[1]
    capacity = min(rows, max(2, 2 * rows * TOP // experts))
    kv_local = KV_HEADS // heads_axis
    span = blocks_axis * stretch
    scale = HEAD_DIM ** (-0.5)
    queries_rows = heads_axis * stretch
    dense = (
        lax.all_gather(w_qkv.astype(low_type), ("head", "blk"), axis=0, tiled=True),
        lax.all_gather(w_out.astype(low_type), ("head", "blk"), axis=0, tiled=True),
        lax.all_gather(w_shgu.astype(low_type), ("head", "blk"), axis=0, tiled=True),
        lax.all_gather(w_shdown.astype(low_type), ("head", "blk"), axis=0, tiled=True),
        lax.all_gather(w_router.astype(low_type), ("head", "blk"), axis=0, tiled=True),
        lax.all_gather(w_gains.astype(low_type), ("head", "blk"), axis=1, tiled=True),
    )
    qkv_full, out_full, shgu_full, shdown_full, router_full, gains_full = dense
    expert_full = (
        lax.all_gather(w_expgu.astype(low_type), "head", axis=1, tiled=True),
        lax.all_gather(w_expdown.astype(low_type), "head", axis=1, tiled=True),
    )
    expgu_full = expert_full[0][0]
    expdown_full = expert_full[1][0]
    gain_in = gains_full[0].astype(full_type)
    gain_mid = gains_full[1].astype(full_type)
    inputs = tokens.astype(full_type).reshape(rows, width)
    inverse_in = lax.rsqrt(jnp.mean(inputs * inputs, axis=1, keepdims=True) + norm_eps)
    normed_in = (inputs * inverse_in * gain_in).astype(low_type)
    projected = jnp.dot(normed_in, qkv_full, preferred_element_type=full_type).astype(low_type)
    stacked = projected.reshape(1, rows, heads_axis, kv_local * (GROUP + 2) * HEAD_DIM)
    by_head = lax.all_to_all(stacked, "head", split_axis=2, concat_axis=0, tiled=True)
    by_head = by_head.reshape(heads_axis, seqs, stretch, kv_local, GROUP + 2, HEAD_DIM)
    queries = by_head[:, :, :, :, :GROUP, :]
    keys = by_head[:, :, :, :, GROUP, :]
    values = by_head[:, :, :, :, GROUP + 1, :]
    query_pos = (
        jnp.arange(heads_axis)[:, None] * span + blk_index * stretch + jnp.arange(stretch)[None, :]
    ).reshape(-1)

    def piece_scores(key_piece, start):
        count = key_piece.shape[0]
        raw = jnp.einsum(
            "astkgd,nbsukd->skgatnbu", queries, key_piece, preferred_element_type=full_type
        )
        raw = raw.reshape(seqs, kv_local, GROUP, queries_rows, count * heads_axis * stretch) * scale
        key_pos = (
            (start + jnp.arange(count))[:, None, None] * stretch
            + jnp.arange(heads_axis)[None, :, None] * span
            + jnp.arange(stretch)[None, None, :]
        ).reshape(-1)
        allowed = (key_pos[None, None, :] <= query_pos[None, :, None]) & (
            key_pos[None, None, :] < lengths[:, None, None]
        )
        allowed = allowed[:, None, None]
        return (jnp.where(allowed, raw, masked_score), allowed)

    kept = (
        lax.all_gather(keys[None], "blk", axis=0, tiled=True),
        lax.all_gather(values[None], "blk", axis=0, tiled=True),
    )

    def norm_fold(carry, piece, start):
        top, total = carry
        scores, allowed = piece_scores(piece[0], start)
        new_top = jnp.maximum(top, jnp.max(scores, axis=-1))
        shifted = jnp.where(allowed, jnp.exp(scores - new_top[..., None]), 0.0)
        return (new_top, total * jnp.exp(top - new_top) + jnp.sum(shifted, axis=-1))

    stat_shape = (seqs, kv_local, GROUP, queries_rows)
    top, total = local_fold(
        norm_fold,
        (jnp.full(stat_shape, masked_score, full_type), jnp.zeros(stat_shape, full_type)),
        kept,
    )
    log_total = top + jnp.log(total)

    def out_fold(carry, piece, start):
        keys_part, values_part = piece
        count = keys_part.shape[0]
        scores, allowed = piece_scores(keys_part, start)
        weights = jnp.where(allowed, jnp.exp(scores - log_total[..., None]), 0.0).astype(low_type)
        weights = weights.reshape(
            seqs, kv_local, GROUP, heads_axis, stretch, count, heads_axis, stretch
        )
        return carry + jnp.einsum(
            "skgatnbu,nbsukd->astkgd", weights, values_part, preferred_element_type=full_type
        )

    outputs = local_fold(out_fold, jnp.zeros(queries.shape, full_type), kept)
    attended = outputs.astype(low_type).reshape(heads_axis, rows, 1, kv_local * GROUP * HEAD_DIM)
    attended_tok = lax.all_to_all(
        attended, "head", split_axis=0, concat_axis=2, tiled=True
    ).reshape(rows, HEADS * HEAD_DIM)
    branch = jnp.dot(attended_tok, out_full, preferred_element_type=full_type)
    middle = inputs + branch
    inverse_mid = lax.rsqrt(jnp.mean(middle * middle, axis=1, keepdims=True) + norm_eps)
    normed_mid = (middle * inverse_mid * gain_mid).astype(low_type)
    expert_ids = jnp.arange(experts, dtype=jnp.int32)
    hits_ts = routes[..., None] == expert_ids
    named_ts = jnp.sum(hits_ts.astype(jnp.int32), axis=2).reshape(rows, experts)
    before_ts = (jnp.cumsum(named_ts, axis=0) - named_ts).reshape(stretch, seqs, experts)
    route_rows = jnp.transpose(routes, (1, 0, 2)).reshape(rows, TOP)
    hits = jnp.transpose(hits_ts, (1, 0, 2, 3)).reshape(rows, TOP, experts)
    before = jnp.transpose(before_ts, (1, 0, 2)).reshape(rows, experts)
    slots = jnp.sum(jnp.where(hits, before[:, None, :], 0), axis=2)
    flat_route = route_rows.reshape(-1)
    flat_slot = slots.reshape(-1)
    logits = jnp.dot(normed_mid, router_full, preferred_element_type=full_type)
    picked = jnp.sum(jnp.where(hits, logits[:, None, :], 0.0), axis=2)
    gates = jax.nn.softmax(picked, axis=1)
    outgoing = (
        jnp.zeros((experts, capacity, width), low_type)
        .at[flat_route, flat_slot]
        .set(jnp.repeat(normed_mid, TOP, axis=0))
    )
    arrived = to_experts(outgoing)
    flat_in = arrived.reshape(-1, width)
    hidden = jnp.dot(flat_in, expgu_full, preferred_element_type=full_type)
    gate_part = hidden[:, :EXPERT_FF]
    up_part = hidden[:, EXPERT_FF:]
    middle_act = (jax.nn.silu(gate_part) * up_part).astype(low_type)
    expert_out = jnp.dot(middle_act, expdown_full, preferred_element_type=full_type).astype(
        low_type
    )
    returned = from_experts(expert_out.reshape(arrived.shape))
    gathered_out = returned[flat_route, flat_slot].reshape(rows, TOP, width).astype(full_type)
    routed = jnp.sum(gates[:, :, None] * gathered_out, axis=1)
    shared_hidden = jnp.dot(normed_mid, shgu_full, preferred_element_type=full_type)
    shared_gate = shared_hidden[:, :SHARED]
    shared_up = shared_hidden[:, SHARED:]
    shared_mid = (jax.nn.silu(shared_gate) * shared_up).astype(low_type)
    shared_out = jnp.dot(shared_mid, shdown_full, preferred_element_type=full_type)
    final = middle + routed + shared_out
    block_out = final.astype(low_type).reshape(seqs, stretch, width)
    own_pos = (head_index * blocks_axis + blk_index) * stretch + jnp.arange(stretch)
    valid = (own_pos[None, :] < lengths[:, None]).astype(full_type).reshape(rows, 1)
    stat_sums = jnp.stack(
        [
            jnp.sum(branch * branch * valid),
            jnp.sum(middle * middle * valid),
            jnp.sum(final * final * valid),
        ]
    )
    grad_final = cotangent.astype(full_type).reshape(rows, width) * valid
    grad_low = grad_final.astype(low_type)
    grad_shdown = outer_dot(shared_mid, grad_low)
    grad_shared_mid = back_dot(grad_low, shdown_full)
    grad_shared_hidden = jnp.concatenate(
        [
            grad_shared_mid * shared_up * silu_grad(shared_gate),
            grad_shared_mid * jax.nn.silu(shared_gate),
        ],
        axis=1,
    ).astype(low_type)
    grad_shgu = outer_dot(normed_mid, grad_shared_hidden)
    grad_normed = back_dot(grad_shared_hidden, shgu_full)
    grad_gates = jnp.sum(grad_final[:, None, :] * gathered_out, axis=2)
    grad_picked = gates * (grad_gates - jnp.sum(gates * grad_gates, axis=1, keepdims=True))
    grad_logits = jnp.sum(jnp.where(hits, grad_picked[:, :, None], 0.0), axis=1).astype(low_type)
    grad_router = outer_dot(normed_mid, grad_logits)
    grad_normed = grad_normed + back_dot(grad_logits, router_full)
    grad_outputs = (
        (gates[:, :, None] * grad_final[:, None, :]).astype(low_type).reshape(rows * TOP, width)
    )
    outgoing_grad = (
        jnp.zeros((experts, capacity, width), low_type).at[flat_route, flat_slot].set(grad_outputs)
    )
    arrived_grad = to_experts(outgoing_grad).reshape(-1, width)
    grad_expdown = outer_dot(middle_act, arrived_grad)
    grad_middle_act = back_dot(arrived_grad, expdown_full)
    grad_hidden = jnp.concatenate(
        [
            grad_middle_act * up_part * silu_grad(gate_part),
            grad_middle_act * jax.nn.silu(gate_part),
        ],
        axis=1,
    ).astype(low_type)
    grad_expgu = outer_dot(flat_in, grad_hidden)
    grad_in = back_dot(grad_hidden, expgu_full).astype(low_type).reshape(arrived.shape)
    returned_grad = from_experts(grad_in)
    grad_normed = grad_normed + jnp.sum(
        returned_grad[flat_route, flat_slot].reshape(rows, TOP, width).astype(full_type), axis=1
    )
    scaled_mid = grad_normed * gain_mid
    grad_gain_mid = jnp.sum(grad_normed * middle * inverse_mid, axis=0)
    grad_mid_total = (
        grad_final
        + inverse_mid * scaled_mid
        - middle * inverse_mid**3 * jnp.mean(scaled_mid * middle, axis=1, keepdims=True)
    )
    grad_branch = grad_mid_total.astype(low_type)
    grad_out_w = outer_dot(attended_tok, grad_branch)
    grad_attended = back_dot(grad_branch, out_full).astype(low_type)
    grad_heads = lax.all_to_all(
        grad_attended.reshape(1, rows, heads_axis, kv_local * GROUP * HEAD_DIM),
        "head",
        split_axis=2,
        concat_axis=0,
        tiled=True,
    )
    grad_heads = grad_heads.reshape(queries.shape)
    row_dot = jnp.sum(grad_heads.astype(full_type) * outputs, axis=-1)
    row_dot = jnp.transpose(row_dot, (1, 3, 4, 0, 2)).reshape(stat_shape)

    def piece_grads(grad_q, keys_part, values_part, start):
        count = keys_part.shape[0]
        scores, allowed = piece_scores(keys_part, start)
        weights = jnp.where(allowed, jnp.exp(scores - log_total[..., None]), 0.0)
        full_shape = (seqs, kv_local, GROUP, heads_axis, stretch, count, heads_axis, stretch)
        weights_low = weights.astype(low_type).reshape(full_shape)
        grad_weights = jnp.einsum(
            "astkgd,nbsukd->skgatnbu", grad_heads, values_part, preferred_element_type=full_type
        )
        grad_weights = grad_weights.reshape(weights.shape)
        grad_scores = (
            (weights * (grad_weights - row_dot[..., None])).astype(low_type).reshape(full_shape)
        )
        grad_q = (
            grad_q
            + jnp.einsum(
                "skgatnbu,nbsukd->astkgd", grad_scores, keys_part, preferred_element_type=full_type
            )
            * scale
        )
        piece_k = (
            jnp.einsum(
                "skgatnbu,astkgd->nbsukd", grad_scores, queries, preferred_element_type=full_type
            )
            * scale
        )
        piece_v = jnp.einsum(
            "skgatnbu,astkgd->nbsukd", weights_low, grad_heads, preferred_element_type=full_type
        )
        return (grad_q, piece_k, piece_v)

    def back_fold(carry, piece, start):
        grad_q, grad_k_all, grad_v_all = carry
        grad_q, piece_k, piece_v = piece_grads(grad_q, piece[0], piece[1], start)
        grad_k_all = lax.dynamic_update_slice_in_dim(grad_k_all, piece_k, start, 0)
        grad_v_all = lax.dynamic_update_slice_in_dim(grad_v_all, piece_v, start, 0)
        return (grad_q, grad_k_all, grad_v_all)

    buffer_shape = (blocks_axis,) + keys.shape
    start_carry = (
        jnp.zeros(queries.shape, full_type),
        jnp.zeros(buffer_shape, full_type),
        jnp.zeros(buffer_shape, full_type),
    )
    grad_q, grad_k_all, grad_v_all = local_fold(back_fold, start_carry, kept)
    key_sums = (
        lax.psum_scatter(grad_k_all, "blk", scatter_dimension=0, tiled=True),
        lax.psum_scatter(grad_v_all, "blk", scatter_dimension=0, tiled=True),
    )
    key_grad_sum = key_sums[0][0]
    value_grad_sum = key_sums[1][0]
    grad_stack = jnp.concatenate(
        [grad_q, key_grad_sum[:, :, :, :, None, :], value_grad_sum[:, :, :, :, None, :]], axis=4
    )
    grad_stack = grad_stack.astype(low_type).reshape(
        heads_axis, rows, 1, kv_local * (GROUP + 2) * HEAD_DIM
    )
    grad_projected = lax.all_to_all(
        grad_stack, "head", split_axis=0, concat_axis=2, tiled=True
    ).reshape(rows, qkv_full.shape[1])
    grad_qkv = outer_dot(normed_in, grad_projected)
    grad_normed_in = back_dot(grad_projected, qkv_full)
    scaled_in = grad_normed_in * gain_in
    grad_gain_in = jnp.sum(grad_normed_in * inputs * inverse_in, axis=0)
    grad_inputs = (
        grad_mid_total
        + inverse_in * scaled_in
        - inputs * inverse_in**3 * jnp.mean(scaled_in * inputs, axis=1, keepdims=True)
    )
    token_grad = grad_inputs.reshape(seqs, stretch, width)
    shares = (
        lax.psum_scatter(grad_qkv, ("head", "blk"), scatter_dimension=0, tiled=True),
        lax.psum_scatter(grad_out_w, ("head", "blk"), scatter_dimension=0, tiled=True),
        lax.psum_scatter(grad_shgu, ("head", "blk"), scatter_dimension=0, tiled=True),
        lax.psum_scatter(grad_shdown, ("head", "blk"), scatter_dimension=0, tiled=True),
        lax.psum_scatter(grad_router, ("head", "blk"), scatter_dimension=0, tiled=True),
        lax.psum_scatter(
            jnp.stack([grad_gain_in, grad_gain_mid]),
            ("head", "blk"),
            scatter_dimension=1,
            tiled=True,
        ),
    )
    g_qkv, g_out, g_shgu, g_shdown, g_router, g_gains = shares
    expert_shares = (
        lax.psum_scatter(
            grad_expgu[None].astype(jnp.bfloat16), "head", scatter_dimension=1, tiled=True
        ).astype(jnp.float32),
        lax.psum_scatter(
            grad_expdown[None].astype(jnp.bfloat16), "head", scatter_dimension=1, tiled=True
        ).astype(jnp.float32),
    )
    g_expgu, g_expdown = expert_shares
    local_squares = (
        jnp.sum(g_qkv * g_qkv)
        + jnp.sum(g_out * g_out)
        + jnp.sum(g_shgu * g_shgu)
        + jnp.sum(g_shdown * g_shdown)
        + jnp.sum(g_router * g_router)
        + jnp.sum(g_gains * g_gains)
        + jnp.sum(g_expgu * g_expgu)
        + jnp.sum(g_expdown * g_expdown)
    )
    squares, stat_total = lax.psum((local_squares, stat_sums), ("head", "blk"))
    count = jnp.sum(lengths).astype(full_type) * width
    stats = jnp.sqrt(stat_total / count)
    grad_norm = jnp.sqrt(squares)
    factor = clip_norm / jnp.maximum(grad_norm, clip_norm)
    a_qkv, b_qkv, c_qkv = adam_update(w_qkv, m_qkv, v_qkv, g_qkv, factor)
    a_out, b_out, c_out = adam_update(w_out, m_out, v_out, g_out, factor)
    a_shgu, b_shgu, c_shgu = adam_update(w_shgu, m_shgu, v_shgu, g_shgu, factor)
    a_shdown, b_shdown, c_shdown = adam_update(w_shdown, m_shdown, v_shdown, g_shdown, factor)
    a_router, b_router, c_router = adam_update(w_router, m_router, v_router, g_router, factor)
    a_gains, b_gains, c_gains = adam_update(w_gains, m_gains, v_gains, g_gains, factor)
    a_expgu, b_expgu, c_expgu = adam_update(w_expgu, m_expgu, v_expgu, g_expgu, factor)
    a_expdown, b_expdown, c_expdown = adam_update(
        w_expdown, m_expdown, v_expdown, g_expdown, factor
    )
    return (
        block_out,
        token_grad,
        g_qkv,
        a_qkv,
        b_qkv,
        c_qkv,
        g_out,
        a_out,
        b_out,
        c_out,
        g_shgu,
        a_shgu,
        b_shgu,
        c_shgu,
        g_shdown,
        a_shdown,
        b_shdown,
        c_shdown,
        g_router,
        a_router,
        b_router,
        c_router,
        g_gains,
        a_gains,
        b_gains,
        c_gains,
        g_expgu,
        a_expgu,
        b_expgu,
        c_expgu,
        g_expdown,
        a_expdown,
        b_expdown,
        c_expdown,
        grad_norm,
        stats,
    )


def local_cube(
    tokens,
    cotangent,
    lengths,
    routes,
    w_qkv,
    m_qkv,
    v_qkv,
    w_out,
    m_out,
    v_out,
    w_shgu,
    m_shgu,
    v_shgu,
    w_shdown,
    m_shdown,
    v_shdown,
    w_router,
    m_router,
    v_router,
    w_gains,
    m_gains,
    v_gains,
    w_expgu,
    m_expgu,
    v_expgu,
    w_expdown,
    m_expdown,
    v_expdown,
):
    low_type = jnp.bfloat16
    full_type = jnp.float32
    heads_axis = lax.axis_size("head")
    blocks_axis = lax.axis_size("blk")
    head_index = lax.axis_index("head")
    blk_index = lax.axis_index("blk")
    devices = heads_axis * blocks_axis
    me = head_index * blocks_axis + blk_index
    seqs, stretch, width = tokens.shape
    rows = seqs * stretch
    experts = w_router.shape[1]
    shard = w_qkv.shape[0]
    group_cols = (GROUP + 2) * HEAD_DIM
    query_cols = GROUP * HEAD_DIM
    extra = -(-(experts + 2) // 128) * 128
    tail = -(-2 * experts // 128) * 128
    all_orders = both_orders()
    row_orders = blk_orders()
    head_bits = axis_bits("head")

    small = jnp.concatenate([w_router, w_gains.T], axis=1)
    small = jnp.pad(small, ((0, 0), (0, extra - experts - 2)))
    half_cols = w_qkv.shape[1] // 2
    first_half, second_half, small_full = gather_rows(
        [
            w_qkv[:, :half_cols].astype(low_type),
            w_qkv[:, half_cols:].astype(low_type),
            small.astype(low_type),
        ],
        (all_orders[0], all_orders[1], all_orders[0]),
    )
    router_full = small_full[:, :experts]
    gains_full = small_full[:, experts : experts + 2].astype(full_type)
    gain_in = gains_full[:, 0][None]
    gain_mid = gains_full[:, 1][None]
    out_low = w_out.astype(low_type)
    out_full = lax.all_gather(out_low, ("head", "blk"), axis=0, tiled=True)
    own_pos = me * stretch + jnp.arange(stretch, dtype=jnp.int32)
    valid = (own_pos[None, :] < lengths[:, None]).astype(full_type).reshape(rows, 1)
    limit = jnp.minimum(own_pos[None, :], lengths[:, None] - 1).reshape(rows, 1)
    grad_final = cotangent.astype(full_type).reshape(rows, width) * valid
    grad_low = grad_final.astype(low_type)

    inputs = tokens.astype(full_type).reshape(rows, width)
    inverse_in = lax.rsqrt(jnp.mean(inputs * inputs, axis=1, keepdims=True) + norm_eps)
    normed_in = (inputs * inverse_in * gain_in).astype(low_type)
    projected = [
        jnp.dot(normed_in, half, preferred_element_type=full_type).astype(low_type)
        for half in (first_half, second_half)
    ]
    per_half = KV_HEADS // 2
    by_group = [half.reshape(seqs, stretch, per_half, group_cols) for half in projected]
    queries = [
        [half[s, :, :, :query_cols].reshape(stretch, -1) for half in by_group]
        for s in range(seqs)
    ]
    pairs = gather_relative(
        [
            half[s, :, :, query_cols:].reshape(stretch, -1)
            for s in range(seqs)
            for half in by_group
        ],
        [order for s in range(seqs) for order in all_orders],
        WAVES_KV,
    )
    pairs = [pairs[2 * s : 2 * s + 2] for s in range(seqs)]
    limits = limit.reshape(seqs, stretch, 1)
    key_pos = [
        (block_devices(order)[:, None] * stretch + jnp.arange(stretch, dtype=jnp.int32)).reshape(
            1, -1
        )
        for order in all_orders
    ]

    route_rows = jnp.transpose(routes, (1, 0, 2)).reshape(rows, TOP)
    hits = route_rows[:, :, None] == jnp.arange(experts, dtype=jnp.int32)
    named = jnp.sum(hits.astype(full_type), axis=1)
    early = jnp.concatenate(
        [grad_low, jnp.pad(named, ((0, 0), (0, tail - experts))).astype(low_type)], axis=1
    )
    early_all = lax.all_gather(early, "blk", axis=0, tiled=True).reshape(
        blocks_axis, seqs, stretch, -1
    )

    def to_columns(values, beside):
        spread = gather_relative(values, row_orders, WAVES_COL, beside)
        return [[half.reshape(-1, half.shape[-1]) for half in pair] for pair in spread]

    def rows_of(values):
        return list(values.reshape(seqs, stretch, -1))


    def gather_head(values, *earlier):
        own = values.astype(low_type)[None]
        for step in reversed(head_bits):
            mine = jnp.arange(2).reshape(2, 1, 1, 1) == own_bit(step)
            own = jnp.where(mine, own[None], after(swap(own, step), *earlier)[None])
            own = own.reshape((-1,) + own.shape[2:])
        return own.reshape(-1, values.shape[1])

    def scatter_head(values, *earlier):
        for step in head_bits:
            half = values.shape[0] // 2
            bit = own_bit(step)
            mine = lax.dynamic_slice_in_dim(values, bit * half, half, 0)
            theirs = lax.dynamic_slice_in_dim(values, (1 - bit) * half, half, 0)
            others = after(swap(theirs.astype(low_type), step), *earlier)
            values = mine.astype(full_type) + others.astype(full_type)
        return values

    attended, attended_tok, branch, middle, inverse_mid, normed_mid = [], [], [], [], [], []
    for s in range(seqs):
        asked = queries[s] if s == 0 else after(queries[s], normed_mid[s - 1])
        attended.append(
            [
                attend(query, pair, pos, limits[s])
                for query, pair, pos in zip(asked, pairs[s], key_pos)
            ]
        )
        attended_tok.append(jnp.concatenate([item[1] for item in attended[s]], axis=1))
        branch.append(jnp.dot(attended_tok[s], out_full, preferred_element_type=full_type))
        middle.append(rows_of(inputs)[s] + branch[s])
        squares = jnp.mean(middle[s] * middle[s], axis=1, keepdims=True)
        inverse_mid.append(lax.rsqrt(squares + norm_eps))
        normed_mid.append((middle[s] * inverse_mid[s] * gain_mid).astype(low_type))

    unit = SHARED // devices
    w_shgu_late = after(w_shgu, projected)
    w_expgu_late = after(w_expgu, projected)
    units = 2 * heads_axis * unit
    sliced = jnp.transpose(
        w_shgu_late.astype(low_type).reshape(shard, 2 * heads_axis, blocks_axis, unit), (2, 0, 1, 3)
    ).reshape(blocks_axis, shard, units)
    sliced = gather_head(transpose_blk(sliced).reshape(blocks_axis * shard, units))
    gate_up_full = jnp.concatenate([gather_head(w_expgu_late[0], normed_mid), sliced], axis=1)
    down_full = jnp.concatenate([gather_head(w_expdown[0], projected), gather_head(w_shdown, projected)], axis=0)
    act_rows = -(-down_full.shape[0] // 128) * 128
    down_full = jnp.pad(down_full, ((0, act_rows - down_full.shape[0]), (0, 0)))

    def pull(_):
        flat = early_all.reshape(-1, early_all.shape[-1])[:, :width]
        return back_dot(flat, down_full).reshape(blocks_axis, seqs, stretch, -1)

    found = []
    mid_all = to_columns(normed_mid, ({1: pull}, found))
    pulled = found[0]

    lanes = jnp.arange(tail, dtype=jnp.int32)[None]
    own = jnp.concatenate([lanes == blk_index, lanes == experts + blk_index]).astype(full_type)
    router_wide = jnp.pad(router_full, ((0, 0), (0, tail - experts)))
    places = [blk_blocks(order) for order in row_orders]

    done, back_sums = [], []
    for s in range(seqs):
        mid = mid_all[s] if s == 0 else after(mid_all[s], done[s - 1][0])
        result = run_expert(
            mid, pulled, early_all, router_wide, own, gate_up_full, places[s], s
        )
        done.append(result)
        back_sums.append(
            tuple(item.reshape(blocks_axis // 2, stretch, -1) for item in result[:2])
        )
    acts = [item[2] for item in done]
    hids = [item[3] for item in done]

    def outer_gate_up(before):
        return outer_experts(mid_all, after(hids, before))

    def outer_down(before):
        return outer_acts(after(acts, before), early_all, width)

    def routed(before):
        terms = [
            jnp.dot(act.reshape(-1, act.shape[2]), down_full, preferred_element_type=full_type)
            .astype(low_type)
            .reshape(blocks_axis, stretch, width)
            for act in after(acts, before)
        ]
        return jnp.concatenate(terms, axis=1).reshape(-1, width)

    found = []
    back_sums = scatter_relative(
        back_sums,
        row_orders,
        beside=({1: outer_gate_up, 2: outer_down, 3: routed}, found),
    )
    back_sums = [item.astype(full_type) for item in back_sums]
    grad_gate_up, grad_down, routed_terms = found
    added = lax.psum_scatter(routed_terms, "blk", scatter_dimension=0, tiled=True)

    def sum_rows(values):
        return lax.psum_scatter(
            values.astype(low_type), ("head", "blk"), scatter_dimension=0, tiled=True
        ).astype(full_type)

    def all_gates(values, chosen):
        logits = jnp.dot(values, router_full, preferred_element_type=full_type)
        logits = jnp.where(chosen, logits, masked_score)
        raised = jnp.where(chosen, jnp.exp(logits - jnp.max(logits, axis=1, keepdims=True)), 0.0)
        return raised / jnp.sum(raised, axis=1, keepdims=True)

    chosen = rows_of(named > 0)
    finals = rows_of(grad_final)
    grad_router, grad_gain_mid, grad_mid_total, grad_branch, back = [], [], [], [], []
    for s in range(seqs):
        gates = all_gates(normed_mid[s], chosen[s])
        sums = back_sums[s]
        grad_gates = sums[:, width : width + experts] + (
            sums[:, width + experts : width + 2 * experts]
        )
        grad_logits = gates * (grad_gates - jnp.sum(gates * grad_gates, axis=1, keepdims=True))
        grad_logits = jnp.where(chosen[s], grad_logits, 0.0).astype(low_type)
        grad_router.append(outer_dot(normed_mid[s], grad_logits))
        grad_normed = back_dot(grad_logits, router_full) + sums[:, :width]
        scaled_mid = grad_normed * gain_mid
        grad_gain_mid.append(jnp.sum(grad_normed * middle[s] * inverse_mid[s], axis=0))
        grad_mid_total.append(
            finals[s]
            + inverse_mid[s] * scaled_mid
            - middle[s]
            * inverse_mid[s] ** 3
            * jnp.mean(scaled_mid * middle[s], axis=1, keepdims=True)
        )
        grad_branch.append(grad_mid_total[s].astype(low_type))
        grad_attended = back_dot(grad_branch[s], out_full).astype(low_type)
        cols = per_half * query_cols
        back.append(
            [
                attend_back(
                    queries[s][half],
                    pairs[s][half],
                    key_pos[half],
                    limits[s],
                    grad_attended[:, half * cols : (half + 1) * cols],
                    attended[s][half][0],
                    attended[s][half][2],
                )
                for half in range(2)
            ]
        )
    grad_router = sum(grad_router)
    grad_gain_mid = sum(grad_gain_mid)
    grad_mid_total = jnp.concatenate(grad_mid_total, axis=0)
    g_out = sum_rows(
        outer_dot(jnp.concatenate(attended_tok, axis=0), jnp.concatenate(grad_branch, axis=0))
    )
    g_shgu = scatter_head(grad_gate_up[:, 2 * EXPERT_FF :], grad_branch).astype(low_type)
    g_shgu = transpose_blk(g_shgu.reshape(blocks_axis, shard, units))
    g_shgu = (
        jnp.transpose(
            g_shgu.reshape(blocks_axis, shard, 2 * heads_axis, unit), (1, 2, 0, 3)
        )
        .reshape(w_shgu.shape)
        .astype(full_type)
    )

    pair_sums = scatter_relative(
        [item[1:] for part in back for item in part],
        [order for s in range(seqs) for order in all_orders],
        WAVES_KV,
    )
    grad_halves = [
        jnp.concatenate(
            [
                jnp.concatenate(
                    [
                        back[s][half][0].reshape(stretch, per_half, query_cols),
                        pair_sums[2 * s + half].reshape(stretch, per_half, 2 * HEAD_DIM),
                    ],
                    axis=2,
                ).reshape(stretch, -1)
                for s in range(seqs)
            ],
            axis=0,
        )
        for half in range(2)
    ]
    branch = jnp.concatenate(branch, axis=0)
    middle = jnp.concatenate(middle, axis=0)
    final = middle + added.astype(full_type)
    block_out = final.astype(low_type).reshape(seqs, stretch, width)
    stat_sums = jnp.stack(
        [
            jnp.sum(branch * branch * valid),
            jnp.sum(middle * middle * valid),
            jnp.sum(final * final * valid),
        ]
    )
    grad_halves = after(grad_halves, g_shgu)
    g_expgu = scatter_head(grad_gate_up[:, : 2 * EXPERT_FF], grad_halves)[None]
    g_expdown = scatter_head(grad_down[:EXPERT_FF], grad_halves)[None]
    g_shdown = scatter_head(grad_down[EXPERT_FF : EXPERT_FF + heads_axis * unit], grad_halves)
    grad_normed_in = back_dot(grad_halves[0], first_half) + back_dot(grad_halves[1], second_half)
    scaled_in = grad_normed_in * gain_in
    grad_gain_in = jnp.sum(grad_normed_in * inputs * inverse_in, axis=0)
    grad_inputs = (
        grad_mid_total
        + inverse_in * scaled_in
        - inputs * inverse_in**3 * jnp.mean(scaled_in * inputs, axis=1, keepdims=True)
    )
    token_grad = grad_inputs.reshape(seqs, stretch, width)
    grad_small = jnp.concatenate(
        [grad_router, jnp.stack([grad_gain_in, grad_gain_mid], axis=1)], axis=1
    )
    grad_small = jnp.pad(grad_small, ((0, 0), (0, extra - experts - 2)))
    sums = scatter_rows(
        [outer_dot(normed_in, half).astype(low_type) for half in grad_halves]
        + [grad_small.astype(low_type)],
        (all_orders[0], all_orders[1], all_orders[0]),
    )
    g_qkv = jnp.concatenate(sums[:2], axis=1).astype(full_type)
    g_router = sums[2][:, :experts].astype(full_type)
    g_gains = sums[2][:, experts : experts + 2].astype(full_type).T

    local_squares = (
        jnp.sum(g_qkv * g_qkv)
        + jnp.sum(g_out * g_out)
        + jnp.sum(g_shgu * g_shgu)
        + jnp.sum(g_shdown * g_shdown)
        + jnp.sum(g_router * g_router)
        + jnp.sum(g_gains * g_gains)
        + jnp.sum(g_expgu * g_expgu)
        + jnp.sum(g_expdown * g_expdown)
    )
    scalars = jnp.concatenate([local_squares[None], stat_sums])
    totals = sum_everywhere(jnp.pad(scalars, (0, 124)).reshape(1, 128))[0]
    count = jnp.sum(lengths).astype(full_type) * width
    stats = jnp.sqrt(totals[1:4] / count)
    grad_norm = jnp.sqrt(totals[0])
    factor = clip_norm / jnp.maximum(grad_norm, clip_norm)
    outputs = [block_out, token_grad]
    for weight, first, second, grad in (
        (w_qkv, m_qkv, v_qkv, g_qkv),
        (w_out, m_out, v_out, g_out),
        (w_shgu, m_shgu, v_shgu, g_shgu),
        (w_shdown, m_shdown, v_shdown, g_shdown),
        (w_router, m_router, v_router, g_router),
        (w_gains, m_gains, v_gains, g_gains),
        (w_expgu, m_expgu, v_expgu, g_expgu),
        (w_expdown, m_expdown, v_expdown, g_expdown),
    ):
        outputs.append(grad)
        outputs.extend(adam_update(weight, first, second, grad, factor))
    return (*outputs, grad_norm, stats)


def solution(mesh):
    in_specs = (
        P(None, ("head", "blk"), None),
        P(None, ("head", "blk"), None),
        P(),
        P(("head", "blk"), None, None),
        P(("head", "blk"), None),
        P(("head", "blk"), None),
        P(("head", "blk"), None),
        P(("head", "blk"), None),
        P(("head", "blk"), None),
        P(("head", "blk"), None),
        P(("head", "blk"), None),
        P(("head", "blk"), None),
        P(("head", "blk"), None),
        P(("head", "blk"), None),
        P(("head", "blk"), None),
        P(("head", "blk"), None),
        P(("head", "blk"), None),
        P(("head", "blk"), None),
        P(("head", "blk"), None),
        P(None, ("head", "blk")),
        P(None, ("head", "blk")),
        P(None, ("head", "blk")),
        P("blk", "head", None),
        P("blk", "head", None),
        P("blk", "head", None),
        P("blk", "head", None),
        P("blk", "head", None),
        P("blk", "head", None),
    )
    out_specs = (
        P(None, ("head", "blk"), None),
        P(None, ("head", "blk"), None),
        P(("head", "blk"), None),
        P(("head", "blk"), None),
        P(("head", "blk"), None),
        P(("head", "blk"), None),
        P(("head", "blk"), None),
        P(("head", "blk"), None),
        P(("head", "blk"), None),
        P(("head", "blk"), None),
        P(("head", "blk"), None),
        P(("head", "blk"), None),
        P(("head", "blk"), None),
        P(("head", "blk"), None),
        P(("head", "blk"), None),
        P(("head", "blk"), None),
        P(("head", "blk"), None),
        P(("head", "blk"), None),
        P(("head", "blk"), None),
        P(("head", "blk"), None),
        P(("head", "blk"), None),
        P(("head", "blk"), None),
        P(None, ("head", "blk")),
        P(None, ("head", "blk")),
        P(None, ("head", "blk")),
        P(None, ("head", "blk")),
        P("blk", "head", None),
        P("blk", "head", None),
        P("blk", "head", None),
        P("blk", "head", None),
        P("blk", "head", None),
        P("blk", "head", None),
        P("blk", "head", None),
        P("blk", "head", None),
        P(),
        P(),
    )
    shards = mesh.size
    cubes = all(size & (size - 1) == 0 for size in mesh.shape.values())
    cubes = cubes and mesh.shape["head"] == 2
    step = local_cube if cubes and WIDTH_ROWS % (16 * shards) == 0 else local
    return jax.shard_map(step, mesh=mesh, in_specs=in_specs, out_specs=out_specs, check_vma=False)
```

```python
import functools

import functools

import jax
import jax.numpy as jnp
from jax import lax
from jax.experimental import pallas as pl
from jax.experimental.pallas import tpu as pltpu
from jax.sharding import PartitionSpec as P

HEADS = 12
KV_HEADS = 4
HEAD_DIM = 128
EXPERT_FF = 512
SHARED = 1024
TOP = 6
ADAM_STEP = 10
GROUP = 3


norm_eps = 1e-05
adam_eps = 1e-08
learn_rate = 0.02
first_decay = 0.9
second_decay = 0.999
weight_decay = 0.1
clip_norm = 1.0
masked_score = -1e30
group_turn = 4


def to_experts(buffer):
    return lax.all_to_all(buffer, "blk", split_axis=0, concat_axis=0, tiled=True)


def from_experts(buffer):
    return lax.all_to_all(buffer, "blk", split_axis=0, concat_axis=0, tiled=True)


def outer_dot(left, right):
    return lax.dot_general(
        left, right, (((0,), (0,)), ((), ())), preferred_element_type=jnp.float32
    )


def back_dot(left, right):
    return lax.dot_general(
        left, right, (((1,), (1,)), ((), ())), preferred_element_type=jnp.float32
    )


def silu_grad(values):
    logistic = jax.nn.sigmoid(values)
    return logistic * (1.0 + values * (1.0 - logistic))


def local_fold(function, init, gathered):
    turns = gathered[0].shape[0] // group_turn

    def advance(turn, carry):
        start = turn * group_turn
        piece = (
            lax.dynamic_slice_in_dim(gathered[0], start, group_turn, 0),
            lax.dynamic_slice_in_dim(gathered[1], start, group_turn, 0),
        )
        return function(carry, piece, start)

    return lax.fori_loop(0, turns, advance, init)


def adam_update(weight, first, second, grad, factor):
    clipped = grad * factor
    first_new = first_decay * first + (1.0 - first_decay) * clipped
    second_new = second_decay * second + (1.0 - second_decay) * clipped * clipped
    first_fix = 1.0 - first_decay**ADAM_STEP
    second_fix = 1.0 - second_decay**ADAM_STEP
    change = -learn_rate * (
        first_new / first_fix / (jnp.sqrt(second_new / second_fix) + adam_eps)
        + weight_decay * weight
    )
    return (first_new, second_new, change)


WAVES_KV = (0, 0, 1, 1)
WAVES_COL = None
WIDTH_ROWS = 512


def axis_bits(name):
    size = lax.axis_size(name)
    return [(name, 1 << k) for k in reversed(range(size.bit_length() - 1))]


def swap(values, step):
    name, bit = step
    size = lax.axis_size(name)
    return lax.ppermute(values, name, [(i, i ^ bit) for i in range(size)])


def after(values, *earlier):
    return lax.optimization_barrier((values, earlier))[0]


def own_bit(step):
    return (lax.axis_index(step[0]) // step[1]) % 2


def both_orders():
    head_bits, blk_bits = axis_bits("head"), axis_bits("blk")
    first = blk_bits[:-1] + head_bits + blk_bits[-1:]
    second = blk_bits[:-2] + head_bits + blk_bits[-2:]
    return (first, second)


def blk_orders():
    blk_bits = axis_bits("blk")
    return (blk_bits, blk_bits[-2:-1] + blk_bits[:-2] + blk_bits[-1:])


def lockstep(pieces, orders, act, backwards=False, waves=None, beside=None):
    count = len(orders[0])
    pieces = list(pieces)
    for turn, at in enumerate(reversed(range(count)) if backwards else range(count)):
        before = list(pieces)
        for place, order in enumerate(orders):
            piece = pieces[place]
            if waves is not None and waves[place] > 0:
                ahead = [p for p, wave in zip(pieces, waves) if wave == waves[place] - 1]
                piece = after(piece, ahead)
            pieces[place] = act(piece, order[at])
        if beside is not None:
            work, results = beside
            if work is None:
                pieces = lax.optimization_barrier(pieces)
            elif turn in work:
                found = work[turn](before)
                pieces, found = lax.optimization_barrier((pieces, found))
                results.append(found)
    return pieces


def gather_relative(pieces, orders, waves=None, beside=None):
    def act(piece, step):
        piece = piece[0] if len(piece) == 1 else jnp.concatenate(piece, axis=0)
        return (piece, swap(piece, step))

    return lockstep([(piece[None],) for piece in pieces], orders, act, False, waves, beside)


def scatter_relative(pieces, orders, waves=None, beside=None):
    def act(piece, step):
        kept, sent = piece
        total = kept + swap(sent, step)
        half = total.shape[0] // 2
        return (total[:half], total[half:]) if half else total

    return [piece[0] for piece in lockstep(pieces, orders, act, True, waves, beside)]


def transpose_blk(values):
    return lax.all_to_all(values, "blk", split_axis=0, concat_axis=0, tiled=True)


def gather_rows(pieces, orders):
    places = axis_bits("head") + axis_bits("blk")

    def act(piece, step):
        place = places.index(step)
        shape = [1] * piece.ndim
        shape[place] = 2
        mine = lax.broadcasted_iota(jnp.int32, shape, place) == own_bit(step)
        return jnp.where(mine, piece, swap(piece, step))

    wide = [piece.reshape((1,) * len(places) + piece.shape) for piece in pieces]
    return [
        full.reshape(-1, full.shape[-1])
        for full in lockstep(wide, orders, act, beside=(None, []))
    ]


def scatter_rows(pieces, orders):
    places = axis_bits("head") + axis_bits("blk")
    devices = 1 << len(places)

    def act(piece, step):
        place = places.index(step)
        bit = own_bit(step)
        mine = lax.dynamic_slice_in_dim(piece, bit, 1, place)
        theirs = lax.dynamic_slice_in_dim(piece, 1 - bit, 1, place)
        return mine + swap(theirs, step)

    wide = [
        piece.reshape((2,) * len(places) + (piece.shape[0] // devices, piece.shape[1]))
        for piece in pieces
    ]
    return [
        own.reshape(own.shape[-2:])
        for own in lockstep(wide, orders, act, True)
    ]


def swap_both(values, first, second):
    sizes = {name: lax.axis_size(name) for name in ("head", "blk")}
    flip = {"head": 0, "blk": 0}
    for name, bit in (first, second):
        flip[name] ^= bit
    pairs = [
        (h * sizes["blk"] + b, (h ^ flip["head"]) * sizes["blk"] + (b ^ flip["blk"]))
        for h in range(sizes["head"])
        for b in range(sizes["blk"])
    ]
    return lax.ppermute(values, ("head", "blk"), pairs)


def sum_everywhere(values):
    blk_bits = axis_bits("blk")
    steps = blk_bits[:-1] + axis_bits("head")
    while len(steps) > 1:
        first, second, steps = steps[0], steps[1], steps[2:]
        values = (values + swap(values, first)) + (
            swap(values, second) + swap_both(values, first, second)
        )
    for step in steps + blk_bits[-1:]:
        values = values + swap(values, step)
    return values


def blk_blocks(order):
    offsets = [0]
    for _, bit in order:
        offsets = offsets + [offset ^ bit for offset in offsets]
    return lax.axis_index("blk") ^ jnp.array(offsets, jnp.int32)


def block_devices(order):
    offsets = [(0, 0)]
    for name, bit in order:
        offsets = offsets + [
            (h ^ bit, b) if name == "head" else (h, b ^ bit) for h, b in offsets
        ]
    head_index, blk_index = lax.axis_index("head"), lax.axis_index("blk")
    heads = jnp.array([h for h, _ in offsets], jnp.int32)
    blks = jnp.array([b for _, b in offsets], jnp.int32)
    return (head_index ^ heads) * lax.axis_size("blk") + (blk_index ^ blks)


def stack_heads(block):
    return jnp.concatenate(
        [block[:, i * HEAD_DIM : (i + 1) * HEAD_DIM] for i in range(GROUP)], axis=0
    )


def group_scores(query, keys, limit, key_pos):
    scores = lax.dot_general(
        query, keys, (((1,), (1,)), ((), ())), preferred_element_type=jnp.float32
    ) * (HEAD_DIM ** (-0.5))
    return jnp.where(key_pos <= limit, scores, masked_score)


def join(low_ref, high_ref, start):
    parts = [ref[:, :, start : start + HEAD_DIM].reshape(-1, HEAD_DIM) for ref in (low_ref, high_ref)]
    return jnp.concatenate(parts, axis=0)


def attend_kernel(q_ref, kv0_ref, kv1_ref, pos_ref, limit_ref, out_ref, low_ref, log_ref):
    stretch = q_ref.shape[0]
    query = stack_heads(q_ref[...])
    keys = join(kv0_ref, kv1_ref, 0)
    values = join(kv0_ref, kv1_ref, HEAD_DIM)
    limit = jnp.concatenate([limit_ref[...]] * GROUP, axis=0)
    scores = group_scores(query, keys, limit, pos_ref[...])
    top = jnp.max(scores, axis=1, keepdims=True)
    weights = jnp.exp(scores - top)
    total = jnp.sum(weights, axis=1, keepdims=True)
    out = jnp.dot(weights.astype(jnp.bfloat16), values, preferred_element_type=jnp.float32)
    out = out / total
    log_ref[0] = top + jnp.log(total)
    for i in range(GROUP):
        part = out[i * stretch : (i + 1) * stretch]
        columns = slice(i * HEAD_DIM, (i + 1) * HEAD_DIM)
        out_ref[:, columns] = part
        low_ref[:, columns] = part.astype(jnp.bfloat16)


def attend_back_kernel(
    q_ref,
    kv0_ref,
    kv1_ref,
    pos_ref,
    limit_ref,
    grad_ref,
    out_ref,
    log_ref,
    dq_ref,
    dkv0_ref,
    dkv1_ref,
):
    stretch = q_ref.shape[0]
    scale = HEAD_DIM ** (-0.5)
    low_type = jnp.bfloat16
    query = stack_heads(q_ref[...])
    keys = join(kv0_ref, kv1_ref, 0)
    values = join(kv0_ref, kv1_ref, HEAD_DIM)
    grad = stack_heads(grad_ref[...])
    row_dot = jnp.sum(
        grad.astype(jnp.float32) * stack_heads(out_ref[...]), axis=1, keepdims=True
    )
    limit = jnp.concatenate([limit_ref[...]] * GROUP, axis=0)
    scores = group_scores(query, keys, limit, pos_ref[...])
    weights = jnp.exp(scores - log_ref[0])
    grad_weights = lax.dot_general(
        grad, values, (((1,), (1,)), ((), ())), preferred_element_type=jnp.float32
    )
    grad_scores = (weights * (grad_weights - row_dot)).astype(low_type)
    weights_low = weights.astype(low_type)
    dq = jnp.dot(grad_scores, keys, preferred_element_type=jnp.float32) * scale
    dk = outer_dot(grad_scores, query) * scale
    dv = outer_dot(weights_low, grad)
    block = dkv0_ref.shape[:2] + (HEAD_DIM,)
    half = dk.shape[0] // 2
    for start, ref in ((0, dkv0_ref), (half, dkv1_ref)):
        ref[:, :, :HEAD_DIM] = dk[start : start + half].astype(low_type).reshape(block)
        ref[:, :, HEAD_DIM:] = dv[start : start + half].astype(low_type).reshape(block)
    for i in range(GROUP):
        part = dq[i * stretch : (i + 1) * stretch]
        dq_ref[:, i * HEAD_DIM : (i + 1) * HEAD_DIM] = part.astype(low_type)


def attention_specs(stretch, devices):
    wide = pl.BlockSpec((stretch, GROUP * HEAD_DIM), lambda g: (0, g))
    pair = pl.BlockSpec((devices // 2, stretch, 2 * HEAD_DIM), lambda g: (0, 0, g))
    pos = pl.BlockSpec((1, devices * stretch), lambda g: (0, 0))
    limit = pl.BlockSpec((stretch, 1), lambda g: (0, 0))
    log = pl.BlockSpec((1, GROUP * stretch, 1), lambda g: (g, 0, 0))
    return wide, pair, pos, limit, log


def attention_cost(groups, stretch, devices, matmuls):
    scores = groups * GROUP * stretch * devices * stretch
    return pl.CostEstimate(
        flops=2 * matmuls * scores * HEAD_DIM,
        bytes_accessed=devices * groups * stretch * 2 * HEAD_DIM * 2,
        transcendentals=scores,
    )


def attend(query, pair, key_pos, limit):
    stretch = query.shape[0]
    groups = query.shape[1] // (GROUP * HEAD_DIM)
    devices = 2 * pair[0].shape[0]
    wide, kv, pos, lim, log = attention_specs(stretch, devices)
    return pl.pallas_call(
        attend_kernel,
        grid=(groups,),
        in_specs=[wide, kv, kv, pos, lim],
        out_specs=[wide, wide, log],
        out_shape=[
            jax.ShapeDtypeStruct(query.shape, jnp.float32),
            jax.ShapeDtypeStruct(query.shape, jnp.bfloat16),
            jax.ShapeDtypeStruct((groups, GROUP * stretch, 1), jnp.float32),
        ],
        compiler_params=pltpu.CompilerParams(vmem_limit_bytes=48 << 20),
        cost_estimate=attention_cost(groups, stretch, devices, 2),
        name="attend",
    )(query, *pair, key_pos, limit)


def attend_back(query, pair, key_pos, limit, grad, out, log_total):
    stretch = query.shape[0]
    groups = query.shape[1] // (GROUP * HEAD_DIM)
    devices = 2 * pair[0].shape[0]
    wide, kv, pos, lim, log = attention_specs(stretch, devices)
    return pl.pallas_call(
        attend_back_kernel,
        grid=(groups,),
        in_specs=[wide, kv, kv, pos, lim, wide, wide, log],
        out_specs=[wide, kv, kv],
        out_shape=[
            jax.ShapeDtypeStruct(query.shape, jnp.bfloat16),
            jax.ShapeDtypeStruct(pair[0].shape, jnp.bfloat16),
            jax.ShapeDtypeStruct(pair[1].shape, jnp.bfloat16),
        ],
        compiler_params=pltpu.CompilerParams(vmem_limit_bytes=48 << 20),
        cost_estimate=attention_cost(groups, stretch, devices, 5),
        name="attend_back",
    )(query, *pair, key_pos, limit, grad, out, log_total)


def expert_kernel(blocks, place_ref, low_ref, high_ref, router_ref, own_ref, gu_ref, *refs):
    pulled_refs, named_refs = refs[:blocks], refs[blocks : 2 * blocks]
    out_low_ref, out_high_ref, act_ref, hid_ref = refs[2 * blocks :]
    low_type = jnp.bfloat16
    turn = pl.program_id(0)
    half = pl.num_programs(0) // 2
    first = jnp.where(turn < half, half + turn, turn - half) * blocks
    values = jnp.where(turn < half, high_ref[...], low_ref[...])
    width = values.shape[1]
    stretch = values.shape[0] // blocks
    chosen = jnp.concatenate([ref[...].reshape(stretch, -1) for ref in named_refs], axis=0) > 0
    pulled = jnp.concatenate([ref[...].reshape(stretch, -1) for ref in pulled_refs], axis=0)
    logits = jnp.dot(values, router_ref[...], preferred_element_type=jnp.float32)
    logits = jnp.where(chosen, logits, masked_score)
    raised = jnp.where(chosen, jnp.exp(logits - jnp.max(logits, axis=1, keepdims=True)), 0.0)
    own = own_ref[...]
    gate = jnp.sum(raised * own[:1], axis=1, keepdims=True) / jnp.sum(
        raised, axis=1, keepdims=True
    )
    hidden = jnp.dot(values, gu_ref[...], preferred_element_type=jnp.float32)
    shared = (hidden.shape[1] - 2 * EXPERT_FF) // 2

    def mixed(gate_part, up_part, grad_act, start):
        logistic = 1.0 / (1.0 + jnp.exp(-gate_part))
        smooth = gate_part * logistic
        slope = logistic * (1.0 + gate_part * (1.0 - logistic))
        size = gate_part.shape[1]
        hid_ref[:, start : start + size] = (grad_act * up_part * slope).astype(low_type)
        hid_ref[:, start + size : start + 2 * size] = (grad_act * smooth).astype(low_type)
        return (smooth * up_part).astype(low_type)

    start = 2 * EXPERT_FF
    act = mixed(
        hidden[:, :EXPERT_FF], hidden[:, EXPERT_FF:start], gate * pulled[:, :EXPERT_FF], 0
    ).astype(jnp.float32)
    grad_gate = jnp.sum(pulled[:, :EXPERT_FF] * act, axis=1, keepdims=True)
    shared_act = mixed(
        hidden[:, start : start + shared],
        hidden[:, start + shared :],
        pulled[:, EXPERT_FF : EXPERT_FF + shared],
        start,
    )
    rest = act_ref.shape[2] - EXPERT_FF - shared
    acts = jnp.concatenate(
        [
            (gate * act).astype(low_type),
            shared_act,
            jnp.zeros((values.shape[0], rest), low_type),
        ],
        axis=1,
    )
    for block in range(blocks):
        act_ref[place_ref[first + block]] = acts[block * stretch : (block + 1) * stretch]
    out = back_dot(hid_ref[...], gu_ref[...]).astype(low_type)
    high = grad_gate.astype(low_type).astype(jnp.float32)
    lanes = (high * own[:1] + (grad_gate - high) * own[1:]).astype(low_type)

    @pl.when(turn < half)
    def _():
        out_high_ref[:, :width] = out
        out_high_ref[:, width:] = lanes

    @pl.when(turn >= half)
    def _():
        out_low_ref[:, :width] = out
        out_low_ref[:, width:] = lanes


def run_expert(mid, pulled, early, router, own, gate_up, places, seq):
    rows, width = mid[0].shape
    devices, _, stretch, acts = pulled.shape
    block = min(rows, 256)
    blocks = block // stretch
    half = rows // block
    lanes = own.shape[1]
    hid = gate_up.shape[1]
    low_type = jnp.bfloat16

    def fixed(shape):
        return pl.BlockSpec(shape, lambda i, _: (0,) * len(shape))

    def first(i):
        return jnp.where(i < half, half + i, i - half) * blocks

    def scattered(piece, size, column):
        return pl.BlockSpec(
            (1, 1, stretch, size), lambda i, place: (place[first(i) + piece], seq, 0, column)
        )

    def low_rows(size):
        return pl.BlockSpec((block, size), lambda i, _: (jnp.maximum(i - half, 0), 0))

    def high_rows(size):
        return pl.BlockSpec((block, size), lambda i, _: (jnp.minimum(i, half - 1), 0))

    return pl.pallas_call(
        functools.partial(expert_kernel, blocks),
        grid_spec=pltpu.PrefetchScalarGridSpec(
            num_scalar_prefetch=1,
            grid=(2 * half,),
            in_specs=[
                low_rows(width),
                high_rows(width),
                fixed(router.shape),
                fixed(own.shape),
                fixed(gate_up.shape),
            ]
            + [scattered(piece, acts, 0) for piece in range(blocks)]
            + [scattered(piece, lanes, width // lanes) for piece in range(blocks)],
            out_specs=[
                low_rows(width + lanes),
                high_rows(width + lanes),
                fixed((devices, stretch, acts)),
                pl.BlockSpec((block, hid), lambda i, _: (first(i) // blocks, 0)),
            ],
        ),
        out_shape=[
            jax.ShapeDtypeStruct((rows, width + lanes), low_type),
            jax.ShapeDtypeStruct((rows, width + lanes), low_type),
            jax.ShapeDtypeStruct((devices, stretch, acts), low_type),
            jax.ShapeDtypeStruct((2 * rows, hid), low_type),
        ],
        compiler_params=pltpu.CompilerParams(vmem_limit_bytes=48 << 20),
        cost_estimate=pl.CostEstimate(
            flops=8 * rows * width * hid,
            bytes_accessed=4 * rows * (2 * width + 3 * acts + hid),
            transcendentals=2 * rows * acts,
        ),
        name="expert",
    )(places, mid[0], mid[1], router, own, gate_up, *[pulled] * blocks, *[early] * blocks)


def outer_experts_kernel(low0_ref, high0_ref, low1_ref, high1_ref, right0_ref, right1_ref, out_ref):
    total = None
    rows = low0_ref.shape[0]
    for refs, right in (((low0_ref, high0_ref), right0_ref), ((low1_ref, high1_ref), right1_ref)):
        for part, ref in enumerate(refs):
            term = outer_dot(ref[...], right[part * rows : (part + 1) * rows])
            total = term if total is None else total + term
    out_ref[...] = total.astype(out_ref.dtype)


def outer_experts(mid, hids):
    rows, width = mid[0][0].shape
    columns = hids[0].shape[1]
    block = 256
    lefts = pl.BlockSpec((rows, block), lambda i: (0, i))
    rights = pl.BlockSpec((2 * rows, columns), lambda i: (0, 0))
    return pl.pallas_call(
        outer_experts_kernel,
        grid=(width // block,),
        in_specs=[lefts] * 4 + [rights] * 2,
        out_specs=pl.BlockSpec((block, columns), lambda i: (i, 0)),
        out_shape=jax.ShapeDtypeStruct((width, columns), jnp.bfloat16),
        compiler_params=pltpu.CompilerParams(vmem_limit_bytes=48 << 20),
        cost_estimate=pl.CostEstimate(
            flops=8 * rows * width * columns,
            bytes_accessed=8 * rows * (width + columns) + 2 * width * columns,
            transcendentals=0,
        ),
        name="outer_experts",
    )(*mid[0], *mid[1], *hids)


def outer_acts_kernel(left0_ref, left1_ref, right_ref, out_ref):
    total = None
    for seq, ref in enumerate((left0_ref, left1_ref)):
        left = ref[...].reshape(-1, ref.shape[2])
        right = right_ref[:, seq].reshape(-1, right_ref.shape[3])
        term = outer_dot(left, right)
        total = term if total is None else total + term
    out_ref[...] = total.astype(out_ref.dtype)


def outer_acts(acts, early, width):
    devices, stretch, size = acts[0].shape
    block = 128
    lefts = pl.BlockSpec((devices, stretch, block), lambda i: (0, 0, i))
    rights = pl.BlockSpec((devices, 2, stretch, width), lambda i: (0, 0, 0, 0))
    return pl.pallas_call(
        outer_acts_kernel,
        grid=(size // block,),
        in_specs=[lefts] * 2 + [rights],
        out_specs=pl.BlockSpec((block, width), lambda i: (i, 0)),
        out_shape=jax.ShapeDtypeStruct((size, width), jnp.bfloat16),
        compiler_params=pltpu.CompilerParams(vmem_limit_bytes=48 << 20),
        cost_estimate=pl.CostEstimate(
            flops=4 * devices * stretch * size * width,
            bytes_accessed=4 * devices * stretch * (width + size) + 2 * size * width,
            transcendentals=0,
        ),
        name="outer_acts",
    )(*acts, early)


def local(
    tokens,
    cotangent,
    lengths,
    routes,
    w_qkv,
    m_qkv,
    v_qkv,
    w_out,
    m_out,
    v_out,
    w_shgu,
    m_shgu,
    v_shgu,
    w_shdown,
    m_shdown,
    v_shdown,
    w_router,
    m_router,
    v_router,
    w_gains,
    m_gains,
    v_gains,
    w_expgu,
    m_expgu,
    v_expgu,
    w_expdown,
    m_expdown,
    v_expdown,
):
    low_type = jnp.bfloat16
    full_type = jnp.float32
    heads_axis = lax.axis_size("head")
    blocks_axis = lax.axis_size("blk")
    head_index = lax.axis_index("head")
    blk_index = lax.axis_index("blk")
    seqs, stretch, width = tokens.shape
    rows = seqs * stretch
    experts = w_router.shape[1]
    capacity = min(rows, max(2, 2 * rows * TOP // experts))
    kv_local = KV_HEADS // heads_axis
    span = blocks_axis * stretch
    scale = HEAD_DIM ** (-0.5)
    queries_rows = heads_axis * stretch
    dense = (
        lax.all_gather(w_qkv.astype(low_type), ("head", "blk"), axis=0, tiled=True),
        lax.all_gather(w_out.astype(low_type), ("head", "blk"), axis=0, tiled=True),
        lax.all_gather(w_shgu.astype(low_type), ("head", "blk"), axis=0, tiled=True),
        lax.all_gather(w_shdown.astype(low_type), ("head", "blk"), axis=0, tiled=True),
        lax.all_gather(w_router.astype(low_type), ("head", "blk"), axis=0, tiled=True),
        lax.all_gather(w_gains.astype(low_type), ("head", "blk"), axis=1, tiled=True),
    )
    qkv_full, out_full, shgu_full, shdown_full, router_full, gains_full = dense
    expert_full = (
        lax.all_gather(w_expgu.astype(low_type), "head", axis=1, tiled=True),
        lax.all_gather(w_expdown.astype(low_type), "head", axis=1, tiled=True),
    )
    expgu_full = expert_full[0][0]
    expdown_full = expert_full[1][0]
    gain_in = gains_full[0].astype(full_type)
    gain_mid = gains_full[1].astype(full_type)
    inputs = tokens.astype(full_type).reshape(rows, width)
    inverse_in = lax.rsqrt(jnp.mean(inputs * inputs, axis=1, keepdims=True) + norm_eps)
    normed_in = (inputs * inverse_in * gain_in).astype(low_type)
    projected = jnp.dot(normed_in, qkv_full, preferred_element_type=full_type).astype(low_type)
    stacked = projected.reshape(1, rows, heads_axis, kv_local * (GROUP + 2) * HEAD_DIM)
    by_head = lax.all_to_all(stacked, "head", split_axis=2, concat_axis=0, tiled=True)
    by_head = by_head.reshape(heads_axis, seqs, stretch, kv_local, GROUP + 2, HEAD_DIM)
    queries = by_head[:, :, :, :, :GROUP, :]
    keys = by_head[:, :, :, :, GROUP, :]
    values = by_head[:, :, :, :, GROUP + 1, :]
    query_pos = (
        jnp.arange(heads_axis)[:, None] * span + blk_index * stretch + jnp.arange(stretch)[None, :]
    ).reshape(-1)

    def piece_scores(key_piece, start):
        count = key_piece.shape[0]
        raw = jnp.einsum(
            "astkgd,nbsukd->skgatnbu", queries, key_piece, preferred_element_type=full_type
        )
        raw = raw.reshape(seqs, kv_local, GROUP, queries_rows, count * heads_axis * stretch) * scale
        key_pos = (
            (start + jnp.arange(count))[:, None, None] * stretch
            + jnp.arange(heads_axis)[None, :, None] * span
            + jnp.arange(stretch)[None, None, :]
        ).reshape(-1)
        allowed = (key_pos[None, None, :] <= query_pos[None, :, None]) & (
            key_pos[None, None, :] < lengths[:, None, None]
        )
        allowed = allowed[:, None, None]
        return (jnp.where(allowed, raw, masked_score), allowed)

    kept = (
        lax.all_gather(keys[None], "blk", axis=0, tiled=True),
        lax.all_gather(values[None], "blk", axis=0, tiled=True),
    )

    def norm_fold(carry, piece, start):
        top, total = carry
        scores, allowed = piece_scores(piece[0], start)
        new_top = jnp.maximum(top, jnp.max(scores, axis=-1))
        shifted = jnp.where(allowed, jnp.exp(scores - new_top[..., None]), 0.0)
        return (new_top, total * jnp.exp(top - new_top) + jnp.sum(shifted, axis=-1))

    stat_shape = (seqs, kv_local, GROUP, queries_rows)
    top, total = local_fold(
        norm_fold,
        (jnp.full(stat_shape, masked_score, full_type), jnp.zeros(stat_shape, full_type)),
        kept,
    )
    log_total = top + jnp.log(total)

    def out_fold(carry, piece, start):
        keys_part, values_part = piece
        count = keys_part.shape[0]
        scores, allowed = piece_scores(keys_part, start)
        weights = jnp.where(allowed, jnp.exp(scores - log_total[..., None]), 0.0).astype(low_type)
        weights = weights.reshape(
            seqs, kv_local, GROUP, heads_axis, stretch, count, heads_axis, stretch
        )
        return carry + jnp.einsum(
            "skgatnbu,nbsukd->astkgd", weights, values_part, preferred_element_type=full_type
        )

    outputs = local_fold(out_fold, jnp.zeros(queries.shape, full_type), kept)
    attended = outputs.astype(low_type).reshape(heads_axis, rows, 1, kv_local * GROUP * HEAD_DIM)
    attended_tok = lax.all_to_all(
        attended, "head", split_axis=0, concat_axis=2, tiled=True
    ).reshape(rows, HEADS * HEAD_DIM)
    branch = jnp.dot(attended_tok, out_full, preferred_element_type=full_type)
    middle = inputs + branch
    inverse_mid = lax.rsqrt(jnp.mean(middle * middle, axis=1, keepdims=True) + norm_eps)
    normed_mid = (middle * inverse_mid * gain_mid).astype(low_type)
    expert_ids = jnp.arange(experts, dtype=jnp.int32)
    hits_ts = routes[..., None] == expert_ids
    named_ts = jnp.sum(hits_ts.astype(jnp.int32), axis=2).reshape(rows, experts)
    before_ts = (jnp.cumsum(named_ts, axis=0) - named_ts).reshape(stretch, seqs, experts)
    route_rows = jnp.transpose(routes, (1, 0, 2)).reshape(rows, TOP)
    hits = jnp.transpose(hits_ts, (1, 0, 2, 3)).reshape(rows, TOP, experts)
    before = jnp.transpose(before_ts, (1, 0, 2)).reshape(rows, experts)
    slots = jnp.sum(jnp.where(hits, before[:, None, :], 0), axis=2)
    flat_route = route_rows.reshape(-1)
    flat_slot = slots.reshape(-1)
    logits = jnp.dot(normed_mid, router_full, preferred_element_type=full_type)
    picked = jnp.sum(jnp.where(hits, logits[:, None, :], 0.0), axis=2)
    gates = jax.nn.softmax(picked, axis=1)
    outgoing = (
        jnp.zeros((experts, capacity, width), low_type)
        .at[flat_route, flat_slot]
        .set(jnp.repeat(normed_mid, TOP, axis=0))
    )
    arrived = to_experts(outgoing)
    flat_in = arrived.reshape(-1, width)
    hidden = jnp.dot(flat_in, expgu_full, preferred_element_type=full_type)
    gate_part = hidden[:, :EXPERT_FF]
    up_part = hidden[:, EXPERT_FF:]
    middle_act = (jax.nn.silu(gate_part) * up_part).astype(low_type)
    expert_out = jnp.dot(middle_act, expdown_full, preferred_element_type=full_type).astype(
        low_type
    )
    returned = from_experts(expert_out.reshape(arrived.shape))
    gathered_out = returned[flat_route, flat_slot].reshape(rows, TOP, width).astype(full_type)
    routed = jnp.sum(gates[:, :, None] * gathered_out, axis=1)
    shared_hidden = jnp.dot(normed_mid, shgu_full, preferred_element_type=full_type)
    shared_gate = shared_hidden[:, :SHARED]
    shared_up = shared_hidden[:, SHARED:]
    shared_mid = (jax.nn.silu(shared_gate) * shared_up).astype(low_type)
    shared_out = jnp.dot(shared_mid, shdown_full, preferred_element_type=full_type)
    final = middle + routed + shared_out
    block_out = final.astype(low_type).reshape(seqs, stretch, width)
    own_pos = (head_index * blocks_axis + blk_index) * stretch + jnp.arange(stretch)
    valid = (own_pos[None, :] < lengths[:, None]).astype(full_type).reshape(rows, 1)
    stat_sums = jnp.stack(
        [
            jnp.sum(branch * branch * valid),
            jnp.sum(middle * middle * valid),
            jnp.sum(final * final * valid),
        ]
    )
    grad_final = cotangent.astype(full_type).reshape(rows, width) * valid
    grad_low = grad_final.astype(low_type)
    grad_shdown = outer_dot(shared_mid, grad_low)
    grad_shared_mid = back_dot(grad_low, shdown_full)
    grad_shared_hidden = jnp.concatenate(
        [
            grad_shared_mid * shared_up * silu_grad(shared_gate),
            grad_shared_mid * jax.nn.silu(shared_gate),
        ],
        axis=1,
    ).astype(low_type)
    grad_shgu = outer_dot(normed_mid, grad_shared_hidden)
    grad_normed = back_dot(grad_shared_hidden, shgu_full)
    grad_gates = jnp.sum(grad_final[:, None, :] * gathered_out, axis=2)
    grad_picked = gates * (grad_gates - jnp.sum(gates * grad_gates, axis=1, keepdims=True))
    grad_logits = jnp.sum(jnp.where(hits, grad_picked[:, :, None], 0.0), axis=1).astype(low_type)
    grad_router = outer_dot(normed_mid, grad_logits)
    grad_normed = grad_normed + back_dot(grad_logits, router_full)
    grad_outputs = (
        (gates[:, :, None] * grad_final[:, None, :]).astype(low_type).reshape(rows * TOP, width)
    )
    outgoing_grad = (
        jnp.zeros((experts, capacity, width), low_type).at[flat_route, flat_slot].set(grad_outputs)
    )
    arrived_grad = to_experts(outgoing_grad).reshape(-1, width)
    grad_expdown = outer_dot(middle_act, arrived_grad)
    grad_middle_act = back_dot(arrived_grad, expdown_full)
    grad_hidden = jnp.concatenate(
        [
            grad_middle_act * up_part * silu_grad(gate_part),
            grad_middle_act * jax.nn.silu(gate_part),
        ],
        axis=1,
    ).astype(low_type)
    grad_expgu = outer_dot(flat_in, grad_hidden)
    grad_in = back_dot(grad_hidden, expgu_full).astype(low_type).reshape(arrived.shape)
    returned_grad = from_experts(grad_in)
    grad_normed = grad_normed + jnp.sum(
        returned_grad[flat_route, flat_slot].reshape(rows, TOP, width).astype(full_type), axis=1
    )
    scaled_mid = grad_normed * gain_mid
    grad_gain_mid = jnp.sum(grad_normed * middle * inverse_mid, axis=0)
    grad_mid_total = (
        grad_final
        + inverse_mid * scaled_mid
        - middle * inverse_mid**3 * jnp.mean(scaled_mid * middle, axis=1, keepdims=True)
    )
    grad_branch = grad_mid_total.astype(low_type)
    grad_out_w = outer_dot(attended_tok, grad_branch)
    grad_attended = back_dot(grad_branch, out_full).astype(low_type)
    grad_heads = lax.all_to_all(
        grad_attended.reshape(1, rows, heads_axis, kv_local * GROUP * HEAD_DIM),
        "head",
        split_axis=2,
        concat_axis=0,
        tiled=True,
    )
    grad_heads = grad_heads.reshape(queries.shape)
    row_dot = jnp.sum(grad_heads.astype(full_type) * outputs, axis=-1)
    row_dot = jnp.transpose(row_dot, (1, 3, 4, 0, 2)).reshape(stat_shape)

    def piece_grads(grad_q, keys_part, values_part, start):
        count = keys_part.shape[0]
        scores, allowed = piece_scores(keys_part, start)
        weights = jnp.where(allowed, jnp.exp(scores - log_total[..., None]), 0.0)
        full_shape = (seqs, kv_local, GROUP, heads_axis, stretch, count, heads_axis, stretch)
        weights_low = weights.astype(low_type).reshape(full_shape)
        grad_weights = jnp.einsum(
            "astkgd,nbsukd->skgatnbu", grad_heads, values_part, preferred_element_type=full_type
        )
        grad_weights = grad_weights.reshape(weights.shape)
        grad_scores = (
            (weights * (grad_weights - row_dot[..., None])).astype(low_type).reshape(full_shape)
        )
        grad_q = (
            grad_q
            + jnp.einsum(
                "skgatnbu,nbsukd->astkgd", grad_scores, keys_part, preferred_element_type=full_type
            )
            * scale
        )
        piece_k = (
            jnp.einsum(
                "skgatnbu,astkgd->nbsukd", grad_scores, queries, preferred_element_type=full_type
            )
            * scale
        )
        piece_v = jnp.einsum(
            "skgatnbu,astkgd->nbsukd", weights_low, grad_heads, preferred_element_type=full_type
        )
        return (grad_q, piece_k, piece_v)

    def back_fold(carry, piece, start):
        grad_q, grad_k_all, grad_v_all = carry
        grad_q, piece_k, piece_v = piece_grads(grad_q, piece[0], piece[1], start)
        grad_k_all = lax.dynamic_update_slice_in_dim(grad_k_all, piece_k, start, 0)
        grad_v_all = lax.dynamic_update_slice_in_dim(grad_v_all, piece_v, start, 0)
        return (grad_q, grad_k_all, grad_v_all)

    buffer_shape = (blocks_axis,) + keys.shape
    start_carry = (
        jnp.zeros(queries.shape, full_type),
        jnp.zeros(buffer_shape, full_type),
        jnp.zeros(buffer_shape, full_type),
    )
    grad_q, grad_k_all, grad_v_all = local_fold(back_fold, start_carry, kept)
    key_sums = (
        lax.psum_scatter(grad_k_all, "blk", scatter_dimension=0, tiled=True),
        lax.psum_scatter(grad_v_all, "blk", scatter_dimension=0, tiled=True),
    )
    key_grad_sum = key_sums[0][0]
    value_grad_sum = key_sums[1][0]
    grad_stack = jnp.concatenate(
        [grad_q, key_grad_sum[:, :, :, :, None, :], value_grad_sum[:, :, :, :, None, :]], axis=4
    )
    grad_stack = grad_stack.astype(low_type).reshape(
        heads_axis, rows, 1, kv_local * (GROUP + 2) * HEAD_DIM
    )
    grad_projected = lax.all_to_all(
        grad_stack, "head", split_axis=0, concat_axis=2, tiled=True
    ).reshape(rows, qkv_full.shape[1])
    grad_qkv = outer_dot(normed_in, grad_projected)
    grad_normed_in = back_dot(grad_projected, qkv_full)
    scaled_in = grad_normed_in * gain_in
    grad_gain_in = jnp.sum(grad_normed_in * inputs * inverse_in, axis=0)
    grad_inputs = (
        grad_mid_total
        + inverse_in * scaled_in
        - inputs * inverse_in**3 * jnp.mean(scaled_in * inputs, axis=1, keepdims=True)
    )
    token_grad = grad_inputs.reshape(seqs, stretch, width)
    shares = (
        lax.psum_scatter(grad_qkv, ("head", "blk"), scatter_dimension=0, tiled=True),
        lax.psum_scatter(grad_out_w, ("head", "blk"), scatter_dimension=0, tiled=True),
        lax.psum_scatter(grad_shgu, ("head", "blk"), scatter_dimension=0, tiled=True),
        lax.psum_scatter(grad_shdown, ("head", "blk"), scatter_dimension=0, tiled=True),
        lax.psum_scatter(grad_router, ("head", "blk"), scatter_dimension=0, tiled=True),
        lax.psum_scatter(
            jnp.stack([grad_gain_in, grad_gain_mid]),
            ("head", "blk"),
            scatter_dimension=1,
            tiled=True,
        ),
    )
    g_qkv, g_out, g_shgu, g_shdown, g_router, g_gains = shares
    expert_shares = (
        lax.psum_scatter(
            grad_expgu[None].astype(jnp.bfloat16), "head", scatter_dimension=1, tiled=True
        ).astype(jnp.float32),
        lax.psum_scatter(
            grad_expdown[None].astype(jnp.bfloat16), "head", scatter_dimension=1, tiled=True
        ).astype(jnp.float32),
    )
    g_expgu, g_expdown = expert_shares
    local_squares = (
        jnp.sum(g_qkv * g_qkv)
        + jnp.sum(g_out * g_out)
        + jnp.sum(g_shgu * g_shgu)
        + jnp.sum(g_shdown * g_shdown)
        + jnp.sum(g_router * g_router)
        + jnp.sum(g_gains * g_gains)
        + jnp.sum(g_expgu * g_expgu)
        + jnp.sum(g_expdown * g_expdown)
    )
    squares, stat_total = lax.psum((local_squares, stat_sums), ("head", "blk"))
    count = jnp.sum(lengths).astype(full_type) * width
    stats = jnp.sqrt(stat_total / count)
    grad_norm = jnp.sqrt(squares)
    factor = clip_norm / jnp.maximum(grad_norm, clip_norm)
    a_qkv, b_qkv, c_qkv = adam_update(w_qkv, m_qkv, v_qkv, g_qkv, factor)
    a_out, b_out, c_out = adam_update(w_out, m_out, v_out, g_out, factor)
    a_shgu, b_shgu, c_shgu = adam_update(w_shgu, m_shgu, v_shgu, g_shgu, factor)
    a_shdown, b_shdown, c_shdown = adam_update(w_shdown, m_shdown, v_shdown, g_shdown, factor)
    a_router, b_router, c_router = adam_update(w_router, m_router, v_router, g_router, factor)
    a_gains, b_gains, c_gains = adam_update(w_gains, m_gains, v_gains, g_gains, factor)
    a_expgu, b_expgu, c_expgu = adam_update(w_expgu, m_expgu, v_expgu, g_expgu, factor)
    a_expdown, b_expdown, c_expdown = adam_update(
        w_expdown, m_expdown, v_expdown, g_expdown, factor
    )
    return (
        block_out,
        token_grad,
        g_qkv,
        a_qkv,
        b_qkv,
        c_qkv,
        g_out,
        a_out,
        b_out,
        c_out,
        g_shgu,
        a_shgu,
        b_shgu,
        c_shgu,
        g_shdown,
        a_shdown,
        b_shdown,
        c_shdown,
        g_router,
        a_router,
        b_router,
        c_router,
        g_gains,
        a_gains,
        b_gains,
        c_gains,
        g_expgu,
        a_expgu,
        b_expgu,
        c_expgu,
        g_expdown,
        a_expdown,
        b_expdown,
        c_expdown,
        grad_norm,
        stats,
    )


def local_cube(
    tokens,
    cotangent,
    lengths,
    routes,
    w_qkv,
    m_qkv,
    v_qkv,
    w_out,
    m_out,
    v_out,
    w_shgu,
    m_shgu,
    v_shgu,
    w_shdown,
    m_shdown,
    v_shdown,
    w_router,
    m_router,
    v_router,
    w_gains,
    m_gains,
    v_gains,
    w_expgu,
    m_expgu,
    v_expgu,
    w_expdown,
    m_expdown,
    v_expdown,
):
    low_type = jnp.bfloat16
    full_type = jnp.float32
    heads_axis = lax.axis_size("head")
    blocks_axis = lax.axis_size("blk")
    head_index = lax.axis_index("head")
    blk_index = lax.axis_index("blk")
    devices = heads_axis * blocks_axis
    me = head_index * blocks_axis + blk_index
    seqs, stretch, width = tokens.shape
    rows = seqs * stretch
    experts = w_router.shape[1]
    shard = w_qkv.shape[0]
    group_cols = (GROUP + 2) * HEAD_DIM
    query_cols = GROUP * HEAD_DIM
    extra = -(-(experts + 2) // 128) * 128
    tail = -(-2 * experts // 128) * 128
    all_orders = both_orders()
    row_orders = blk_orders()
    head_bits = axis_bits("head")

    small = jnp.concatenate([w_router, w_gains.T], axis=1)
    small = jnp.pad(small, ((0, 0), (0, extra - experts - 2)))
    half_cols = w_qkv.shape[1] // 2
    first_half, second_half, small_full = gather_rows(
        [
            w_qkv[:, :half_cols].astype(low_type),
            w_qkv[:, half_cols:].astype(low_type),
            small.astype(low_type),
        ],
        (all_orders[0], all_orders[1], all_orders[0]),
    )
    router_full = small_full[:, :experts]
    gains_full = small_full[:, experts : experts + 2].astype(full_type)
    gain_in = gains_full[:, 0][None]
    gain_mid = gains_full[:, 1][None]
    out_low = w_out.astype(low_type)
    out_full = lax.all_gather(out_low, ("head", "blk"), axis=0, tiled=True)
    own_pos = me * stretch + jnp.arange(stretch, dtype=jnp.int32)
    valid = (own_pos[None, :] < lengths[:, None]).astype(full_type).reshape(rows, 1)
    limit = jnp.minimum(own_pos[None, :], lengths[:, None] - 1).reshape(rows, 1)
    grad_final = cotangent.astype(full_type).reshape(rows, width) * valid
    grad_low = grad_final.astype(low_type)

    inputs = tokens.astype(full_type).reshape(rows, width)
    inverse_in = lax.rsqrt(jnp.mean(inputs * inputs, axis=1, keepdims=True) + norm_eps)
    normed_in = (inputs * inverse_in * gain_in).astype(low_type)
    projected = [
        jnp.dot(normed_in, half, preferred_element_type=full_type).astype(low_type)
        for half in (first_half, second_half)
    ]
    per_half = KV_HEADS // 2
    by_group = [half.reshape(seqs, stretch, per_half, group_cols) for half in projected]
    queries = [
        [half[s, :, :, :query_cols].reshape(stretch, -1) for half in by_group]
        for s in range(seqs)
    ]
    pairs = gather_relative(
        [
            half[s, :, :, query_cols:].reshape(stretch, -1)
            for s in range(seqs)
            for half in by_group
        ],
        [order for s in range(seqs) for order in all_orders],
        WAVES_KV,
    )
    pairs = [pairs[2 * s : 2 * s + 2] for s in range(seqs)]
    limits = limit.reshape(seqs, stretch, 1)
    key_pos = [
        (block_devices(order)[:, None] * stretch + jnp.arange(stretch, dtype=jnp.int32)).reshape(
            1, -1
        )
        for order in all_orders
    ]

    route_rows = jnp.transpose(routes, (1, 0, 2)).reshape(rows, TOP)
    hits = route_rows[:, :, None] == jnp.arange(experts, dtype=jnp.int32)
    named = jnp.sum(hits.astype(full_type), axis=1)
    early = jnp.concatenate(
        [grad_low, jnp.pad(named, ((0, 0), (0, tail - experts))).astype(low_type)], axis=1
    )
    early_all = lax.all_gather(early, "blk", axis=0, tiled=True).reshape(
        blocks_axis, seqs, stretch, -1
    )

    def to_columns(values, beside):
        spread = gather_relative(values, row_orders, WAVES_COL, beside)
        return [[half.reshape(-1, half.shape[-1]) for half in pair] for pair in spread]

    def rows_of(values):
        return list(values.reshape(seqs, stretch, -1))


    def gather_head(values, *earlier):
        own = values.astype(low_type)[None]
        for step in reversed(head_bits):
            mine = jnp.arange(2).reshape(2, 1, 1, 1) == own_bit(step)
            own = jnp.where(mine, own[None], after(swap(own, step), *earlier)[None])
            own = own.reshape((-1,) + own.shape[2:])
        return own.reshape(-1, values.shape[1])

    def scatter_head(values, *earlier):
        for step in head_bits:
            half = values.shape[0] // 2
            bit = own_bit(step)
            mine = lax.dynamic_slice_in_dim(values, bit * half, half, 0)
            theirs = lax.dynamic_slice_in_dim(values, (1 - bit) * half, half, 0)
            others = after(swap(theirs.astype(low_type), step), *earlier)
            values = mine.astype(full_type) + others.astype(full_type)
        return values

    attended, attended_tok, branch, middle, inverse_mid, normed_mid = [], [], [], [], [], []
    for s in range(seqs):
        asked = queries[s] if s == 0 else after(queries[s], normed_mid[s - 1])
        attended.append(
            [
                attend(query, pair, pos, limits[s])
                for query, pair, pos in zip(asked, pairs[s], key_pos)
            ]
        )
        attended_tok.append(jnp.concatenate([item[1] for item in attended[s]], axis=1))
        branch.append(jnp.dot(attended_tok[s], out_full, preferred_element_type=full_type))
        middle.append(rows_of(inputs)[s] + branch[s])
        squares = jnp.mean(middle[s] * middle[s], axis=1, keepdims=True)
        inverse_mid.append(lax.rsqrt(squares + norm_eps))
        normed_mid.append((middle[s] * inverse_mid[s] * gain_mid).astype(low_type))

    unit = SHARED // devices
    w_shgu_late = after(w_shgu, projected)
    w_expgu_late = after(w_expgu, projected)
    units = 2 * heads_axis * unit
    sliced = jnp.transpose(
        w_shgu_late.astype(low_type).reshape(shard, 2 * heads_axis, blocks_axis, unit), (2, 0, 1, 3)
    ).reshape(blocks_axis, shard, units)
    sliced = gather_head(transpose_blk(sliced).reshape(blocks_axis * shard, units))
    gate_up_full = jnp.concatenate([gather_head(w_expgu_late[0], normed_mid), sliced], axis=1)
    down_full = jnp.concatenate([gather_head(w_expdown[0], projected), gather_head(w_shdown, projected)], axis=0)
    act_rows = -(-down_full.shape[0] // 128) * 128
    down_full = jnp.pad(down_full, ((0, act_rows - down_full.shape[0]), (0, 0)))

    def pull(_):
        flat = early_all.reshape(-1, early_all.shape[-1])[:, :width]
        return back_dot(flat, down_full).reshape(blocks_axis, seqs, stretch, -1)

    found = []
    mid_all = to_columns(normed_mid, ({1: pull}, found))
    pulled = found[0]

    lanes = jnp.arange(tail, dtype=jnp.int32)[None]
    own = jnp.concatenate([lanes == blk_index, lanes == experts + blk_index]).astype(full_type)
    router_wide = jnp.pad(router_full, ((0, 0), (0, tail - experts)))
    places = [blk_blocks(order) for order in row_orders]

    done, back_sums = [], []
    for s in range(seqs):
        mid = mid_all[s] if s == 0 else after(mid_all[s], done[s - 1][0])
        result = run_expert(
            mid, pulled, early_all, router_wide, own, gate_up_full, places[s], s
        )
        done.append(result)
        back_sums.append(
            tuple(item.reshape(blocks_axis // 2, stretch, -1) for item in result[:2])
        )
    acts = [item[2] for item in done]
    hids = [item[3] for item in done]

    def outer_gate_up(before):
        return outer_experts(mid_all, after(hids, before))

    def outer_down(before):
        return outer_acts(after(acts, before), early_all, width)

    def routed(before):
        terms = [
            jnp.dot(act.reshape(-1, act.shape[2]), down_full, preferred_element_type=full_type)
            .astype(low_type)
            .reshape(blocks_axis, stretch, width)
            for act in after(acts, before)
        ]
        return jnp.concatenate(terms, axis=1).reshape(-1, width)

    found = []
    back_sums = scatter_relative(
        back_sums,
        row_orders,
        beside=({1: outer_gate_up, 2: outer_down, 3: routed}, found),
    )
    back_sums = [item.astype(full_type) for item in back_sums]
    grad_gate_up, grad_down, routed_terms = found
    added = lax.psum_scatter(routed_terms, "blk", scatter_dimension=0, tiled=True)

    def sum_rows(values):
        return lax.psum_scatter(
            values.astype(low_type), ("head", "blk"), scatter_dimension=0, tiled=True
        ).astype(full_type)

    def all_gates(values, chosen):
        logits = jnp.dot(values, router_full, preferred_element_type=full_type)
        logits = jnp.where(chosen, logits, masked_score)
        raised = jnp.where(chosen, jnp.exp(logits - jnp.max(logits, axis=1, keepdims=True)), 0.0)
        return raised / jnp.sum(raised, axis=1, keepdims=True)

    chosen = rows_of(named > 0)
    finals = rows_of(grad_final)
    grad_router, grad_gain_mid, grad_mid_total, grad_branch, back = [], [], [], [], []
    for s in range(seqs):
        gates = all_gates(normed_mid[s], chosen[s])
        sums = back_sums[s]
        grad_gates = sums[:, width : width + experts] + (
            sums[:, width + experts : width + 2 * experts]
        )
        grad_logits = gates * (grad_gates - jnp.sum(gates * grad_gates, axis=1, keepdims=True))
        grad_logits = jnp.where(chosen[s], grad_logits, 0.0).astype(low_type)
        grad_router.append(outer_dot(normed_mid[s], grad_logits))
        grad_normed = back_dot(grad_logits, router_full) + sums[:, :width]
        scaled_mid = grad_normed * gain_mid
        grad_gain_mid.append(jnp.sum(grad_normed * middle[s] * inverse_mid[s], axis=0))
        grad_mid_total.append(
            finals[s]
            + inverse_mid[s] * scaled_mid
            - middle[s]
            * inverse_mid[s] ** 3
            * jnp.mean(scaled_mid * middle[s], axis=1, keepdims=True)
        )
        grad_branch.append(grad_mid_total[s].astype(low_type))
        grad_attended = back_dot(grad_branch[s], out_full).astype(low_type)
        cols = per_half * query_cols
        back.append(
            [
                attend_back(
                    queries[s][half],
                    pairs[s][half],
                    key_pos[half],
                    limits[s],
                    grad_attended[:, half * cols : (half + 1) * cols],
                    attended[s][half][0],
                    attended[s][half][2],
                )
                for half in range(2)
            ]
        )
    grad_router = sum(grad_router)
    grad_gain_mid = sum(grad_gain_mid)
    grad_mid_total = jnp.concatenate(grad_mid_total, axis=0)
    g_out = sum_rows(
        outer_dot(jnp.concatenate(attended_tok, axis=0), jnp.concatenate(grad_branch, axis=0))
    )
    g_shgu = scatter_head(grad_gate_up[:, 2 * EXPERT_FF :], grad_branch).astype(low_type)
    g_shgu = transpose_blk(g_shgu.reshape(blocks_axis, shard, units))
    g_shgu = (
        jnp.transpose(
            g_shgu.reshape(blocks_axis, shard, 2 * heads_axis, unit), (1, 2, 0, 3)
        )
        .reshape(w_shgu.shape)
        .astype(full_type)
    )

    pair_sums = scatter_relative(
        [item[1:] for part in back for item in part],
        [order for s in range(seqs) for order in all_orders],
        None,
    )
    grad_halves = [
        jnp.concatenate(
            [
                jnp.concatenate(
                    [
                        back[s][half][0].reshape(stretch, per_half, query_cols),
                        pair_sums[2 * s + half].reshape(stretch, per_half, 2 * HEAD_DIM),
                    ],
                    axis=2,
                ).reshape(stretch, -1)
                for s in range(seqs)
            ],
            axis=0,
        )
        for half in range(2)
    ]
    branch = jnp.concatenate(branch, axis=0)
    middle = jnp.concatenate(middle, axis=0)
    final = middle + added.astype(full_type)
    block_out = final.astype(low_type).reshape(seqs, stretch, width)
    stat_sums = jnp.stack(
        [
            jnp.sum(branch * branch * valid),
            jnp.sum(middle * middle * valid),
            jnp.sum(final * final * valid),
        ]
    )
    grad_halves = after(grad_halves, g_shgu)
    g_expgu = scatter_head(grad_gate_up[:, : 2 * EXPERT_FF], grad_halves)[None]
    g_expdown = scatter_head(grad_down[:EXPERT_FF], grad_halves)[None]
    g_shdown = scatter_head(grad_down[EXPERT_FF : EXPERT_FF + heads_axis * unit], grad_halves)
    grad_normed_in = back_dot(grad_halves[0], first_half) + back_dot(grad_halves[1], second_half)
    scaled_in = grad_normed_in * gain_in
    grad_gain_in = jnp.sum(grad_normed_in * inputs * inverse_in, axis=0)
    grad_inputs = (
        grad_mid_total
        + inverse_in * scaled_in
        - inputs * inverse_in**3 * jnp.mean(scaled_in * inputs, axis=1, keepdims=True)
    )
    token_grad = grad_inputs.reshape(seqs, stretch, width)
    grad_small = jnp.concatenate(
        [grad_router, jnp.stack([grad_gain_in, grad_gain_mid], axis=1)], axis=1
    )
    grad_small = jnp.pad(grad_small, ((0, 0), (0, extra - experts - 2)))
    sums = scatter_rows(
        [outer_dot(normed_in, half).astype(low_type) for half in grad_halves]
        + [grad_small.astype(low_type)],
        (all_orders[0], all_orders[1], all_orders[0]),
    )
    g_qkv = jnp.concatenate(sums[:2], axis=1).astype(full_type)
    g_router = sums[2][:, :experts].astype(full_type)
    g_gains = sums[2][:, experts : experts + 2].astype(full_type).T

    local_squares = (
        jnp.sum(g_qkv * g_qkv)
        + jnp.sum(g_out * g_out)
        + jnp.sum(g_shgu * g_shgu)
        + jnp.sum(g_shdown * g_shdown)
        + jnp.sum(g_router * g_router)
        + jnp.sum(g_gains * g_gains)
        + jnp.sum(g_expgu * g_expgu)
        + jnp.sum(g_expdown * g_expdown)
    )
    scalars = jnp.concatenate([local_squares[None], stat_sums])
    totals = sum_everywhere(jnp.pad(scalars, (0, 124)).reshape(1, 128))[0]
    count = jnp.sum(lengths).astype(full_type) * width
    stats = jnp.sqrt(totals[1:4] / count)
    grad_norm = jnp.sqrt(totals[0])
    factor = clip_norm / jnp.maximum(grad_norm, clip_norm)
    outputs = [block_out, token_grad]
    for weight, first, second, grad in (
        (w_qkv, m_qkv, v_qkv, g_qkv),
        (w_out, m_out, v_out, g_out),
        (w_shgu, m_shgu, v_shgu, g_shgu),
        (w_shdown, m_shdown, v_shdown, g_shdown),
        (w_router, m_router, v_router, g_router),
        (w_gains, m_gains, v_gains, g_gains),
        (w_expgu, m_expgu, v_expgu, g_expgu),
        (w_expdown, m_expdown, v_expdown, g_expdown),
    ):
        outputs.append(grad)
        outputs.extend(adam_update(weight, first, second, grad, factor))
    return (*outputs, grad_norm, stats)


def solution(mesh):
    in_specs = (
        P(None, ("head", "blk"), None),
        P(None, ("head", "blk"), None),
        P(),
        P(("head", "blk"), None, None),
        P(("head", "blk"), None),
        P(("head", "blk"), None),
        P(("head", "blk"), None),
        P(("head", "blk"), None),
        P(("head", "blk"), None),
        P(("head", "blk"), None),
        P(("head", "blk"), None),
        P(("head", "blk"), None),
        P(("head", "blk"), None),
        P(("head", "blk"), None),
        P(("head", "blk"), None),
        P(("head", "blk"), None),
        P(("head", "blk"), None),
        P(("head", "blk"), None),
        P(("head", "blk"), None),
        P(None, ("head", "blk")),
        P(None, ("head", "blk")),
        P(None, ("head", "blk")),
        P("blk", "head", None),
        P("blk", "head", None),
        P("blk", "head", None),
        P("blk", "head", None),
        P("blk", "head", None),
        P("blk", "head", None),
    )
    out_specs = (
        P(None, ("head", "blk"), None),
        P(None, ("head", "blk"), None),
        P(("head", "blk"), None),
        P(("head", "blk"), None),
        P(("head", "blk"), None),
        P(("head", "blk"), None),
        P(("head", "blk"), None),
        P(("head", "blk"), None),
        P(("head", "blk"), None),
        P(("head", "blk"), None),
        P(("head", "blk"), None),
        P(("head", "blk"), None),
        P(("head", "blk"), None),
        P(("head", "blk"), None),
        P(("head", "blk"), None),
        P(("head", "blk"), None),
        P(("head", "blk"), None),
        P(("head", "blk"), None),
        P(("head", "blk"), None),
        P(("head", "blk"), None),
        P(("head", "blk"), None),
        P(("head", "blk"), None),
        P(None, ("head", "blk")),
        P(None, ("head", "blk")),
        P(None, ("head", "blk")),
        P(None, ("head", "blk")),
        P("blk", "head", None),
        P("blk", "head", None),
        P("blk", "head", None),
        P("blk", "head", None),
        P("blk", "head", None),
        P("blk", "head", None),
        P("blk", "head", None),
        P("blk", "head", None),
        P(),
        P(),
    )
    shards = mesh.size
    cubes = all(size & (size - 1) == 0 for size in mesh.shape.values())
    cubes = cubes and mesh.shape["head"] == 2
    step = local_cube if cubes and WIDTH_ROWS % (16 * shards) == 0 else local
    return jax.shard_map(step, mesh=mesh, in_specs=in_specs, out_specs=out_specs, check_vma=False)
```

```python
import functools

import functools

import jax
import jax.numpy as jnp
from jax import lax
from jax.experimental import pallas as pl
from jax.experimental.pallas import tpu as pltpu
from jax.sharding import PartitionSpec as P

HEADS = 12
KV_HEADS = 4
HEAD_DIM = 128
EXPERT_FF = 512
SHARED = 1024
TOP = 6
ADAM_STEP = 10
GROUP = 3


norm_eps = 1e-05
adam_eps = 1e-08
learn_rate = 0.02
first_decay = 0.9
second_decay = 0.999
weight_decay = 0.1
clip_norm = 1.0
masked_score = -1e30
group_turn = 4


def to_experts(buffer):
    return lax.all_to_all(buffer, "blk", split_axis=0, concat_axis=0, tiled=True)


def from_experts(buffer):
    return lax.all_to_all(buffer, "blk", split_axis=0, concat_axis=0, tiled=True)


def outer_dot(left, right):
    return lax.dot_general(
        left, right, (((0,), (0,)), ((), ())), preferred_element_type=jnp.float32
    )


def back_dot(left, right):
    return lax.dot_general(
        left, right, (((1,), (1,)), ((), ())), preferred_element_type=jnp.float32
    )


def silu_grad(values):
    logistic = jax.nn.sigmoid(values)
    return logistic * (1.0 + values * (1.0 - logistic))


def local_fold(function, init, gathered):
    turns = gathered[0].shape[0] // group_turn

    def advance(turn, carry):
        start = turn * group_turn
        piece = (
            lax.dynamic_slice_in_dim(gathered[0], start, group_turn, 0),
            lax.dynamic_slice_in_dim(gathered[1], start, group_turn, 0),
        )
        return function(carry, piece, start)

    return lax.fori_loop(0, turns, advance, init)


def adam_update(weight, first, second, grad, factor):
    clipped = grad * factor
    first_new = first_decay * first + (1.0 - first_decay) * clipped
    second_new = second_decay * second + (1.0 - second_decay) * clipped * clipped
    first_fix = 1.0 - first_decay**ADAM_STEP
    second_fix = 1.0 - second_decay**ADAM_STEP
    change = -learn_rate * (
        first_new / first_fix / (jnp.sqrt(second_new / second_fix) + adam_eps)
        + weight_decay * weight
    )
    return (first_new, second_new, change)


WAVES_KV = (0, 0, 1, 1)
WAVES_COL = None
WIDTH_ROWS = 512


def axis_bits(name):
    size = lax.axis_size(name)
    return [(name, 1 << k) for k in reversed(range(size.bit_length() - 1))]


def swap(values, step):
    name, bit = step
    size = lax.axis_size(name)
    return lax.ppermute(values, name, [(i, i ^ bit) for i in range(size)])


def after(values, *earlier):
    return lax.optimization_barrier((values, earlier))[0]


def own_bit(step):
    return (lax.axis_index(step[0]) // step[1]) % 2


def both_orders():
    head_bits, blk_bits = axis_bits("head"), axis_bits("blk")
    first = blk_bits[:-1] + head_bits + blk_bits[-1:]
    second = blk_bits[:-2] + head_bits + blk_bits[-2:]
    return (first, second)


def blk_orders():
    blk_bits = axis_bits("blk")
    return (blk_bits, blk_bits[-2:-1] + blk_bits[:-2] + blk_bits[-1:])


def lockstep(pieces, orders, act, backwards=False, waves=None, beside=None):
    count = len(orders[0])
    pieces = list(pieces)
    for turn, at in enumerate(reversed(range(count)) if backwards else range(count)):
        before = list(pieces)
        for place, order in enumerate(orders):
            piece = pieces[place]
            if waves is not None and waves[place] > 0:
                ahead = [p for p, wave in zip(pieces, waves) if wave == waves[place] - 1]
                piece = after(piece, ahead)
            pieces[place] = act(piece, order[at])
        if beside is not None:
            work, results = beside
            if work is None:
                pieces = lax.optimization_barrier(pieces)
            elif turn in work:
                found = work[turn](before)
                pieces, found = lax.optimization_barrier((pieces, found))
                results.append(found)
    return pieces


def gather_relative(pieces, orders, waves=None, beside=None):
    def act(piece, step):
        piece = piece[0] if len(piece) == 1 else jnp.concatenate(piece, axis=0)
        return (piece, swap(piece, step))

    return lockstep([(piece[None],) for piece in pieces], orders, act, False, waves, beside)


def scatter_relative(pieces, orders, waves=None, beside=None):
    def act(piece, step):
        kept, sent = piece
        total = kept + swap(sent, step)
        half = total.shape[0] // 2
        return (total[:half], total[half:]) if half else total

    return [piece[0] for piece in lockstep(pieces, orders, act, True, waves, beside)]


def transpose_blk(values):
    return lax.all_to_all(values, "blk", split_axis=0, concat_axis=0, tiled=True)


def gather_rows(pieces, orders):
    places = axis_bits("head") + axis_bits("blk")

    def act(piece, step):
        place = places.index(step)
        shape = [1] * piece.ndim
        shape[place] = 2
        mine = lax.broadcasted_iota(jnp.int32, shape, place) == own_bit(step)
        return jnp.where(mine, piece, swap(piece, step))

    wide = [piece.reshape((1,) * len(places) + piece.shape) for piece in pieces]
    return [
        full.reshape(-1, full.shape[-1])
        for full in lockstep(wide, orders, act, beside=(None, []))
    ]


def scatter_rows(pieces, orders):
    places = axis_bits("head") + axis_bits("blk")
    devices = 1 << len(places)

    def act(piece, step):
        place = places.index(step)
        bit = own_bit(step)
        mine = lax.dynamic_slice_in_dim(piece, bit, 1, place)
        theirs = lax.dynamic_slice_in_dim(piece, 1 - bit, 1, place)
        return mine + swap(theirs, step)

    wide = [
        piece.reshape((2,) * len(places) + (piece.shape[0] // devices, piece.shape[1]))
        for piece in pieces
    ]
    return [
        own.reshape(own.shape[-2:])
        for own in lockstep(wide, orders, act, True)
    ]


def swap_both(values, first, second):
    sizes = {name: lax.axis_size(name) for name in ("head", "blk")}
    flip = {"head": 0, "blk": 0}
    for name, bit in (first, second):
        flip[name] ^= bit
    pairs = [
        (h * sizes["blk"] + b, (h ^ flip["head"]) * sizes["blk"] + (b ^ flip["blk"]))
        for h in range(sizes["head"])
        for b in range(sizes["blk"])
    ]
    return lax.ppermute(values, ("head", "blk"), pairs)


def sum_everywhere(values):
    blk_bits = axis_bits("blk")
    steps = blk_bits[:-1] + axis_bits("head")
    while len(steps) > 1:
        first, second, steps = steps[0], steps[1], steps[2:]
        values = (values + swap(values, first)) + (
            swap(values, second) + swap_both(values, first, second)
        )
    for step in steps + blk_bits[-1:]:
        values = values + swap(values, step)
    return values


def blk_blocks(order):
    offsets = [0]
    for _, bit in order:
        offsets = offsets + [offset ^ bit for offset in offsets]
    return lax.axis_index("blk") ^ jnp.array(offsets, jnp.int32)


def block_devices(order):
    offsets = [(0, 0)]
    for name, bit in order:
        offsets = offsets + [
            (h ^ bit, b) if name == "head" else (h, b ^ bit) for h, b in offsets
        ]
    head_index, blk_index = lax.axis_index("head"), lax.axis_index("blk")
    heads = jnp.array([h for h, _ in offsets], jnp.int32)
    blks = jnp.array([b for _, b in offsets], jnp.int32)
    return (head_index ^ heads) * lax.axis_size("blk") + (blk_index ^ blks)


def stack_heads(block):
    return jnp.concatenate(
        [block[:, i * HEAD_DIM : (i + 1) * HEAD_DIM] for i in range(GROUP)], axis=0
    )


def group_scores(query, keys, limit, key_pos):
    scores = lax.dot_general(
        query, keys, (((1,), (1,)), ((), ())), preferred_element_type=jnp.float32
    ) * (HEAD_DIM ** (-0.5))
    return jnp.where(key_pos <= limit, scores, masked_score)


def join(low_ref, high_ref, start):
    parts = [ref[:, :, start : start + HEAD_DIM].reshape(-1, HEAD_DIM) for ref in (low_ref, high_ref)]
    return jnp.concatenate(parts, axis=0)


def attend_kernel(q_ref, kv0_ref, kv1_ref, pos_ref, limit_ref, out_ref, low_ref, log_ref):
    stretch = q_ref.shape[0]
    query = stack_heads(q_ref[...])
    keys = join(kv0_ref, kv1_ref, 0)
    values = join(kv0_ref, kv1_ref, HEAD_DIM)
    limit = jnp.concatenate([limit_ref[...]] * GROUP, axis=0)
    scores = group_scores(query, keys, limit, pos_ref[...])
    top = jnp.max(scores, axis=1, keepdims=True)
    weights = jnp.exp(scores - top)
    total = jnp.sum(weights, axis=1, keepdims=True)
    out = jnp.dot(weights.astype(jnp.bfloat16), values, preferred_element_type=jnp.float32)
    out = out / total
    log_ref[0] = top + jnp.log(total)
    for i in range(GROUP):
        part = out[i * stretch : (i + 1) * stretch]
        columns = slice(i * HEAD_DIM, (i + 1) * HEAD_DIM)
        out_ref[:, columns] = part
        low_ref[:, columns] = part.astype(jnp.bfloat16)


def attend_back_kernel(
    q_ref,
    kv0_ref,
    kv1_ref,
    pos_ref,
    limit_ref,
    grad_ref,
    out_ref,
    log_ref,
    dq_ref,
    dkv0_ref,
    dkv1_ref,
):
    stretch = q_ref.shape[0]
    scale = HEAD_DIM ** (-0.5)
    low_type = jnp.bfloat16
    query = stack_heads(q_ref[...])
    keys = join(kv0_ref, kv1_ref, 0)
    values = join(kv0_ref, kv1_ref, HEAD_DIM)
    grad = stack_heads(grad_ref[...])
    row_dot = jnp.sum(
        grad.astype(jnp.float32) * stack_heads(out_ref[...]), axis=1, keepdims=True
    )
    limit = jnp.concatenate([limit_ref[...]] * GROUP, axis=0)
    scores = group_scores(query, keys, limit, pos_ref[...])
    weights = jnp.exp(scores - log_ref[0])
    grad_weights = lax.dot_general(
        grad, values, (((1,), (1,)), ((), ())), preferred_element_type=jnp.float32
    )
    grad_scores = (weights * (grad_weights - row_dot)).astype(low_type)
    weights_low = weights.astype(low_type)
    dq = jnp.dot(grad_scores, keys, preferred_element_type=jnp.float32) * scale
    dk = outer_dot(grad_scores, query) * scale
    dv = outer_dot(weights_low, grad)
    block = dkv0_ref.shape[:2] + (HEAD_DIM,)
    half = dk.shape[0] // 2
    for start, ref in ((0, dkv0_ref), (half, dkv1_ref)):
        ref[:, :, :HEAD_DIM] = dk[start : start + half].astype(low_type).reshape(block)
        ref[:, :, HEAD_DIM:] = dv[start : start + half].astype(low_type).reshape(block)
    for i in range(GROUP):
        part = dq[i * stretch : (i + 1) * stretch]
        dq_ref[:, i * HEAD_DIM : (i + 1) * HEAD_DIM] = part.astype(low_type)


def attention_specs(stretch, devices):
    wide = pl.BlockSpec((stretch, GROUP * HEAD_DIM), lambda g: (0, g))
    pair = pl.BlockSpec((devices // 2, stretch, 2 * HEAD_DIM), lambda g: (0, 0, g))
    pos = pl.BlockSpec((1, devices * stretch), lambda g: (0, 0))
    limit = pl.BlockSpec((stretch, 1), lambda g: (0, 0))
    log = pl.BlockSpec((1, GROUP * stretch, 1), lambda g: (g, 0, 0))
    return wide, pair, pos, limit, log


def attention_cost(groups, stretch, devices, matmuls):
    scores = groups * GROUP * stretch * devices * stretch
    return pl.CostEstimate(
        flops=2 * matmuls * scores * HEAD_DIM,
        bytes_accessed=devices * groups * stretch * 2 * HEAD_DIM * 2,
        transcendentals=scores,
    )


def attend(query, pair, key_pos, limit):
    stretch = query.shape[0]
    groups = query.shape[1] // (GROUP * HEAD_DIM)
    devices = 2 * pair[0].shape[0]
    wide, kv, pos, lim, log = attention_specs(stretch, devices)
    return pl.pallas_call(
        attend_kernel,
        grid=(groups,),
        in_specs=[wide, kv, kv, pos, lim],
        out_specs=[wide, wide, log],
        out_shape=[
            jax.ShapeDtypeStruct(query.shape, jnp.float32),
            jax.ShapeDtypeStruct(query.shape, jnp.bfloat16),
            jax.ShapeDtypeStruct((groups, GROUP * stretch, 1), jnp.float32),
        ],
        compiler_params=pltpu.CompilerParams(vmem_limit_bytes=48 << 20),
        cost_estimate=attention_cost(groups, stretch, devices, 2),
        name="attend",
    )(query, *pair, key_pos, limit)


def attend_back(query, pair, key_pos, limit, grad, out, log_total):
    stretch = query.shape[0]
    groups = query.shape[1] // (GROUP * HEAD_DIM)
    devices = 2 * pair[0].shape[0]
    wide, kv, pos, lim, log = attention_specs(stretch, devices)
    return pl.pallas_call(
        attend_back_kernel,
        grid=(groups,),
        in_specs=[wide, kv, kv, pos, lim, wide, wide, log],
        out_specs=[wide, kv, kv],
        out_shape=[
            jax.ShapeDtypeStruct(query.shape, jnp.bfloat16),
            jax.ShapeDtypeStruct(pair[0].shape, jnp.bfloat16),
            jax.ShapeDtypeStruct(pair[1].shape, jnp.bfloat16),
        ],
        compiler_params=pltpu.CompilerParams(vmem_limit_bytes=48 << 20),
        cost_estimate=attention_cost(groups, stretch, devices, 5),
        name="attend_back",
    )(query, *pair, key_pos, limit, grad, out, log_total)


def expert_kernel(blocks, place_ref, low_ref, high_ref, router_ref, own_ref, gu_ref, *refs):
    pulled_refs, named_refs = refs[:blocks], refs[blocks : 2 * blocks]
    out_low_ref, out_high_ref, act_ref, hid_ref = refs[2 * blocks :]
    low_type = jnp.bfloat16
    turn = pl.program_id(0)
    half = pl.num_programs(0) // 2
    first = jnp.where(turn < half, half + turn, turn - half) * blocks
    values = jnp.where(turn < half, high_ref[...], low_ref[...])
    width = values.shape[1]
    stretch = values.shape[0] // blocks
    chosen = jnp.concatenate([ref[...].reshape(stretch, -1) for ref in named_refs], axis=0) > 0
    pulled = jnp.concatenate([ref[...].reshape(stretch, -1) for ref in pulled_refs], axis=0)
    logits = jnp.dot(values, router_ref[...], preferred_element_type=jnp.float32)
    logits = jnp.where(chosen, logits, masked_score)
    raised = jnp.where(chosen, jnp.exp(logits - jnp.max(logits, axis=1, keepdims=True)), 0.0)
    own = own_ref[...]
    gate = jnp.sum(raised * own[:1], axis=1, keepdims=True) / jnp.sum(
        raised, axis=1, keepdims=True
    )
    hidden = jnp.dot(values, gu_ref[...], preferred_element_type=jnp.float32)
    shared = (hidden.shape[1] - 2 * EXPERT_FF) // 2

    def mixed(gate_part, up_part, grad_act, start):
        logistic = 1.0 / (1.0 + jnp.exp(-gate_part))
        smooth = gate_part * logistic
        slope = logistic * (1.0 + gate_part * (1.0 - logistic))
        size = gate_part.shape[1]
        hid_ref[:, start : start + size] = (grad_act * up_part * slope).astype(low_type)
        hid_ref[:, start + size : start + 2 * size] = (grad_act * smooth).astype(low_type)
        return (smooth * up_part).astype(low_type)

    start = 2 * EXPERT_FF
    act = mixed(
        hidden[:, :EXPERT_FF], hidden[:, EXPERT_FF:start], gate * pulled[:, :EXPERT_FF], 0
    ).astype(jnp.float32)
    grad_gate = jnp.sum(pulled[:, :EXPERT_FF] * act, axis=1, keepdims=True)
    shared_act = mixed(
        hidden[:, start : start + shared],
        hidden[:, start + shared :],
        pulled[:, EXPERT_FF : EXPERT_FF + shared],
        start,
    )
    rest = act_ref.shape[2] - EXPERT_FF - shared
    acts = jnp.concatenate(
        [
            (gate * act).astype(low_type),
            shared_act,
            jnp.zeros((values.shape[0], rest), low_type),
        ],
        axis=1,
    )
    for block in range(blocks):
        act_ref[place_ref[first + block]] = acts[block * stretch : (block + 1) * stretch]
    out = back_dot(hid_ref[...], gu_ref[...]).astype(low_type)
    high = grad_gate.astype(low_type).astype(jnp.float32)
    lanes = (high * own[:1] + (grad_gate - high) * own[1:]).astype(low_type)

    @pl.when(turn < half)
    def _():
        out_high_ref[:, :width] = out
        out_high_ref[:, width:] = lanes

    @pl.when(turn >= half)
    def _():
        out_low_ref[:, :width] = out
        out_low_ref[:, width:] = lanes


def run_expert(mid, pulled, early, router, own, gate_up, places, seq):
    rows, width = mid[0].shape
    devices, _, stretch, acts = pulled.shape
    block = min(rows, 256)
    blocks = block // stretch
    half = rows // block
    lanes = own.shape[1]
    hid = gate_up.shape[1]
    low_type = jnp.bfloat16

    def fixed(shape):
        return pl.BlockSpec(shape, lambda i, _: (0,) * len(shape))

    def first(i):
        return jnp.where(i < half, half + i, i - half) * blocks

    def scattered(piece, size, column):
        return pl.BlockSpec(
            (1, 1, stretch, size), lambda i, place: (place[first(i) + piece], seq, 0, column)
        )

    def low_rows(size):
        return pl.BlockSpec((block, size), lambda i, _: (jnp.maximum(i - half, 0), 0))

    def high_rows(size):
        return pl.BlockSpec((block, size), lambda i, _: (jnp.minimum(i, half - 1), 0))

    return pl.pallas_call(
        functools.partial(expert_kernel, blocks),
        grid_spec=pltpu.PrefetchScalarGridSpec(
            num_scalar_prefetch=1,
            grid=(2 * half,),
            in_specs=[
                low_rows(width),
                high_rows(width),
                fixed(router.shape),
                fixed(own.shape),
                fixed(gate_up.shape),
            ]
            + [scattered(piece, acts, 0) for piece in range(blocks)]
            + [scattered(piece, lanes, width // lanes) for piece in range(blocks)],
            out_specs=[
                low_rows(width + lanes),
                high_rows(width + lanes),
                fixed((devices, stretch, acts)),
                pl.BlockSpec((block, hid), lambda i, _: (first(i) // blocks, 0)),
            ],
        ),
        out_shape=[
            jax.ShapeDtypeStruct((rows, width + lanes), low_type),
            jax.ShapeDtypeStruct((rows, width + lanes), low_type),
            jax.ShapeDtypeStruct((devices, stretch, acts), low_type),
            jax.ShapeDtypeStruct((2 * rows, hid), low_type),
        ],
        compiler_params=pltpu.CompilerParams(vmem_limit_bytes=48 << 20),
        cost_estimate=pl.CostEstimate(
            flops=8 * rows * width * hid,
            bytes_accessed=4 * rows * (2 * width + 3 * acts + hid),
            transcendentals=2 * rows * acts,
        ),
        name="expert",
    )(places, mid[0], mid[1], router, own, gate_up, *[pulled] * blocks, *[early] * blocks)


def outer_experts_kernel(low0_ref, high0_ref, low1_ref, high1_ref, right0_ref, right1_ref, out_ref):
    total = None
    rows = low0_ref.shape[0]
    for refs, right in (((low0_ref, high0_ref), right0_ref), ((low1_ref, high1_ref), right1_ref)):
        for part, ref in enumerate(refs):
            term = outer_dot(ref[...], right[part * rows : (part + 1) * rows])
            total = term if total is None else total + term
    out_ref[...] = total.astype(out_ref.dtype)


def outer_experts(mid, hids):
    rows, width = mid[0][0].shape
    columns = hids[0].shape[1]
    block = 256
    lefts = pl.BlockSpec((rows, block), lambda i: (0, i))
    rights = pl.BlockSpec((2 * rows, columns), lambda i: (0, 0))
    return pl.pallas_call(
        outer_experts_kernel,
        grid=(width // block,),
        in_specs=[lefts] * 4 + [rights] * 2,
        out_specs=pl.BlockSpec((block, columns), lambda i: (i, 0)),
        out_shape=jax.ShapeDtypeStruct((width, columns), jnp.bfloat16),
        compiler_params=pltpu.CompilerParams(vmem_limit_bytes=48 << 20),
        cost_estimate=pl.CostEstimate(
            flops=8 * rows * width * columns,
            bytes_accessed=8 * rows * (width + columns) + 2 * width * columns,
            transcendentals=0,
        ),
        name="outer_experts",
    )(*mid[0], *mid[1], *hids)


def outer_acts_kernel(left0_ref, left1_ref, right_ref, out_ref):
    total = None
    for seq, ref in enumerate((left0_ref, left1_ref)):
        left = ref[...].reshape(-1, ref.shape[2])
        right = right_ref[:, seq].reshape(-1, right_ref.shape[3])
        term = outer_dot(left, right)
        total = term if total is None else total + term
    out_ref[...] = total.astype(out_ref.dtype)


def outer_acts(acts, early, width):
    devices, stretch, size = acts[0].shape
    block = 128
    lefts = pl.BlockSpec((devices, stretch, block), lambda i: (0, 0, i))
    rights = pl.BlockSpec((devices, 2, stretch, width), lambda i: (0, 0, 0, 0))
    return pl.pallas_call(
        outer_acts_kernel,
        grid=(size // block,),
        in_specs=[lefts] * 2 + [rights],
        out_specs=pl.BlockSpec((block, width), lambda i: (i, 0)),
        out_shape=jax.ShapeDtypeStruct((size, width), jnp.bfloat16),
        compiler_params=pltpu.CompilerParams(vmem_limit_bytes=48 << 20),
        cost_estimate=pl.CostEstimate(
            flops=4 * devices * stretch * size * width,
            bytes_accessed=4 * devices * stretch * (width + size) + 2 * size * width,
            transcendentals=0,
        ),
        name="outer_acts",
    )(*acts, early)


def local(
    tokens,
    cotangent,
    lengths,
    routes,
    w_qkv,
    m_qkv,
    v_qkv,
    w_out,
    m_out,
    v_out,
    w_shgu,
    m_shgu,
    v_shgu,
    w_shdown,
    m_shdown,
    v_shdown,
    w_router,
    m_router,
    v_router,
    w_gains,
    m_gains,
    v_gains,
    w_expgu,
    m_expgu,
    v_expgu,
    w_expdown,
    m_expdown,
    v_expdown,
):
    low_type = jnp.bfloat16
    full_type = jnp.float32
    heads_axis = lax.axis_size("head")
    blocks_axis = lax.axis_size("blk")
    head_index = lax.axis_index("head")
    blk_index = lax.axis_index("blk")
    seqs, stretch, width = tokens.shape
    rows = seqs * stretch
    experts = w_router.shape[1]
    capacity = min(rows, max(2, 2 * rows * TOP // experts))
    kv_local = KV_HEADS // heads_axis
    span = blocks_axis * stretch
    scale = HEAD_DIM ** (-0.5)
    queries_rows = heads_axis * stretch
    dense = (
        lax.all_gather(w_qkv.astype(low_type), ("head", "blk"), axis=0, tiled=True),
        lax.all_gather(w_out.astype(low_type), ("head", "blk"), axis=0, tiled=True),
        lax.all_gather(w_shgu.astype(low_type), ("head", "blk"), axis=0, tiled=True),
        lax.all_gather(w_shdown.astype(low_type), ("head", "blk"), axis=0, tiled=True),
        lax.all_gather(w_router.astype(low_type), ("head", "blk"), axis=0, tiled=True),
        lax.all_gather(w_gains.astype(low_type), ("head", "blk"), axis=1, tiled=True),
    )
    qkv_full, out_full, shgu_full, shdown_full, router_full, gains_full = dense
    expert_full = (
        lax.all_gather(w_expgu.astype(low_type), "head", axis=1, tiled=True),
        lax.all_gather(w_expdown.astype(low_type), "head", axis=1, tiled=True),
    )
    expgu_full = expert_full[0][0]
    expdown_full = expert_full[1][0]
    gain_in = gains_full[0].astype(full_type)
    gain_mid = gains_full[1].astype(full_type)
    inputs = tokens.astype(full_type).reshape(rows, width)
    inverse_in = lax.rsqrt(jnp.mean(inputs * inputs, axis=1, keepdims=True) + norm_eps)
    normed_in = (inputs * inverse_in * gain_in).astype(low_type)
    projected = jnp.dot(normed_in, qkv_full, preferred_element_type=full_type).astype(low_type)
    stacked = projected.reshape(1, rows, heads_axis, kv_local * (GROUP + 2) * HEAD_DIM)
    by_head = lax.all_to_all(stacked, "head", split_axis=2, concat_axis=0, tiled=True)
    by_head = by_head.reshape(heads_axis, seqs, stretch, kv_local, GROUP + 2, HEAD_DIM)
    queries = by_head[:, :, :, :, :GROUP, :]
    keys = by_head[:, :, :, :, GROUP, :]
    values = by_head[:, :, :, :, GROUP + 1, :]
    query_pos = (
        jnp.arange(heads_axis)[:, None] * span + blk_index * stretch + jnp.arange(stretch)[None, :]
    ).reshape(-1)

    def piece_scores(key_piece, start):
        count = key_piece.shape[0]
        raw = jnp.einsum(
            "astkgd,nbsukd->skgatnbu", queries, key_piece, preferred_element_type=full_type
        )
        raw = raw.reshape(seqs, kv_local, GROUP, queries_rows, count * heads_axis * stretch) * scale
        key_pos = (
            (start + jnp.arange(count))[:, None, None] * stretch
            + jnp.arange(heads_axis)[None, :, None] * span
            + jnp.arange(stretch)[None, None, :]
        ).reshape(-1)
        allowed = (key_pos[None, None, :] <= query_pos[None, :, None]) & (
            key_pos[None, None, :] < lengths[:, None, None]
        )
        allowed = allowed[:, None, None]
        return (jnp.where(allowed, raw, masked_score), allowed)

    kept = (
        lax.all_gather(keys[None], "blk", axis=0, tiled=True),
        lax.all_gather(values[None], "blk", axis=0, tiled=True),
    )

    def norm_fold(carry, piece, start):
        top, total = carry
        scores, allowed = piece_scores(piece[0], start)
        new_top = jnp.maximum(top, jnp.max(scores, axis=-1))
        shifted = jnp.where(allowed, jnp.exp(scores - new_top[..., None]), 0.0)
        return (new_top, total * jnp.exp(top - new_top) + jnp.sum(shifted, axis=-1))

    stat_shape = (seqs, kv_local, GROUP, queries_rows)
    top, total = local_fold(
        norm_fold,
        (jnp.full(stat_shape, masked_score, full_type), jnp.zeros(stat_shape, full_type)),
        kept,
    )
    log_total = top + jnp.log(total)

    def out_fold(carry, piece, start):
        keys_part, values_part = piece
        count = keys_part.shape[0]
        scores, allowed = piece_scores(keys_part, start)
        weights = jnp.where(allowed, jnp.exp(scores - log_total[..., None]), 0.0).astype(low_type)
        weights = weights.reshape(
            seqs, kv_local, GROUP, heads_axis, stretch, count, heads_axis, stretch
        )
        return carry + jnp.einsum(
            "skgatnbu,nbsukd->astkgd", weights, values_part, preferred_element_type=full_type
        )

    outputs = local_fold(out_fold, jnp.zeros(queries.shape, full_type), kept)
    attended = outputs.astype(low_type).reshape(heads_axis, rows, 1, kv_local * GROUP * HEAD_DIM)
    attended_tok = lax.all_to_all(
        attended, "head", split_axis=0, concat_axis=2, tiled=True
    ).reshape(rows, HEADS * HEAD_DIM)
    branch = jnp.dot(attended_tok, out_full, preferred_element_type=full_type)
    middle = inputs + branch
    inverse_mid = lax.rsqrt(jnp.mean(middle * middle, axis=1, keepdims=True) + norm_eps)
    normed_mid = (middle * inverse_mid * gain_mid).astype(low_type)
    expert_ids = jnp.arange(experts, dtype=jnp.int32)
    hits_ts = routes[..., None] == expert_ids
    named_ts = jnp.sum(hits_ts.astype(jnp.int32), axis=2).reshape(rows, experts)
    before_ts = (jnp.cumsum(named_ts, axis=0) - named_ts).reshape(stretch, seqs, experts)
    route_rows = jnp.transpose(routes, (1, 0, 2)).reshape(rows, TOP)
    hits = jnp.transpose(hits_ts, (1, 0, 2, 3)).reshape(rows, TOP, experts)
    before = jnp.transpose(before_ts, (1, 0, 2)).reshape(rows, experts)
    slots = jnp.sum(jnp.where(hits, before[:, None, :], 0), axis=2)
    flat_route = route_rows.reshape(-1)
    flat_slot = slots.reshape(-1)
    logits = jnp.dot(normed_mid, router_full, preferred_element_type=full_type)
    picked = jnp.sum(jnp.where(hits, logits[:, None, :], 0.0), axis=2)
    gates = jax.nn.softmax(picked, axis=1)
    outgoing = (
        jnp.zeros((experts, capacity, width), low_type)
        .at[flat_route, flat_slot]
        .set(jnp.repeat(normed_mid, TOP, axis=0))
    )
    arrived = to_experts(outgoing)
    flat_in = arrived.reshape(-1, width)
    hidden = jnp.dot(flat_in, expgu_full, preferred_element_type=full_type)
    gate_part = hidden[:, :EXPERT_FF]
    up_part = hidden[:, EXPERT_FF:]
    middle_act = (jax.nn.silu(gate_part) * up_part).astype(low_type)
    expert_out = jnp.dot(middle_act, expdown_full, preferred_element_type=full_type).astype(
        low_type
    )
    returned = from_experts(expert_out.reshape(arrived.shape))
    gathered_out = returned[flat_route, flat_slot].reshape(rows, TOP, width).astype(full_type)
    routed = jnp.sum(gates[:, :, None] * gathered_out, axis=1)
    shared_hidden = jnp.dot(normed_mid, shgu_full, preferred_element_type=full_type)
    shared_gate = shared_hidden[:, :SHARED]
    shared_up = shared_hidden[:, SHARED:]
    shared_mid = (jax.nn.silu(shared_gate) * shared_up).astype(low_type)
    shared_out = jnp.dot(shared_mid, shdown_full, preferred_element_type=full_type)
    final = middle + routed + shared_out
    block_out = final.astype(low_type).reshape(seqs, stretch, width)
    own_pos = (head_index * blocks_axis + blk_index) * stretch + jnp.arange(stretch)
    valid = (own_pos[None, :] < lengths[:, None]).astype(full_type).reshape(rows, 1)
    stat_sums = jnp.stack(
        [
            jnp.sum(branch * branch * valid),
            jnp.sum(middle * middle * valid),
            jnp.sum(final * final * valid),
        ]
    )
    grad_final = cotangent.astype(full_type).reshape(rows, width) * valid
    grad_low = grad_final.astype(low_type)
    grad_shdown = outer_dot(shared_mid, grad_low)
    grad_shared_mid = back_dot(grad_low, shdown_full)
    grad_shared_hidden = jnp.concatenate(
        [
            grad_shared_mid * shared_up * silu_grad(shared_gate),
            grad_shared_mid * jax.nn.silu(shared_gate),
        ],
        axis=1,
    ).astype(low_type)
    grad_shgu = outer_dot(normed_mid, grad_shared_hidden)
    grad_normed = back_dot(grad_shared_hidden, shgu_full)
    grad_gates = jnp.sum(grad_final[:, None, :] * gathered_out, axis=2)
    grad_picked = gates * (grad_gates - jnp.sum(gates * grad_gates, axis=1, keepdims=True))
    grad_logits = jnp.sum(jnp.where(hits, grad_picked[:, :, None], 0.0), axis=1).astype(low_type)
    grad_router = outer_dot(normed_mid, grad_logits)
    grad_normed = grad_normed + back_dot(grad_logits, router_full)
    grad_outputs = (
        (gates[:, :, None] * grad_final[:, None, :]).astype(low_type).reshape(rows * TOP, width)
    )
    outgoing_grad = (
        jnp.zeros((experts, capacity, width), low_type).at[flat_route, flat_slot].set(grad_outputs)
    )
    arrived_grad = to_experts(outgoing_grad).reshape(-1, width)
    grad_expdown = outer_dot(middle_act, arrived_grad)
    grad_middle_act = back_dot(arrived_grad, expdown_full)
    grad_hidden = jnp.concatenate(
        [
            grad_middle_act * up_part * silu_grad(gate_part),
            grad_middle_act * jax.nn.silu(gate_part),
        ],
        axis=1,
    ).astype(low_type)
    grad_expgu = outer_dot(flat_in, grad_hidden)
    grad_in = back_dot(grad_hidden, expgu_full).astype(low_type).reshape(arrived.shape)
    returned_grad = from_experts(grad_in)
    grad_normed = grad_normed + jnp.sum(
        returned_grad[flat_route, flat_slot].reshape(rows, TOP, width).astype(full_type), axis=1
    )
    scaled_mid = grad_normed * gain_mid
    grad_gain_mid = jnp.sum(grad_normed * middle * inverse_mid, axis=0)
    grad_mid_total = (
        grad_final
        + inverse_mid * scaled_mid
        - middle * inverse_mid**3 * jnp.mean(scaled_mid * middle, axis=1, keepdims=True)
    )
    grad_branch = grad_mid_total.astype(low_type)
    grad_out_w = outer_dot(attended_tok, grad_branch)
    grad_attended = back_dot(grad_branch, out_full).astype(low_type)
    grad_heads = lax.all_to_all(
        grad_attended.reshape(1, rows, heads_axis, kv_local * GROUP * HEAD_DIM),
        "head",
        split_axis=2,
        concat_axis=0,
        tiled=True,
    )
    grad_heads = grad_heads.reshape(queries.shape)
    row_dot = jnp.sum(grad_heads.astype(full_type) * outputs, axis=-1)
    row_dot = jnp.transpose(row_dot, (1, 3, 4, 0, 2)).reshape(stat_shape)

    def piece_grads(grad_q, keys_part, values_part, start):
        count = keys_part.shape[0]
        scores, allowed = piece_scores(keys_part, start)
        weights = jnp.where(allowed, jnp.exp(scores - log_total[..., None]), 0.0)
        full_shape = (seqs, kv_local, GROUP, heads_axis, stretch, count, heads_axis, stretch)
        weights_low = weights.astype(low_type).reshape(full_shape)
        grad_weights = jnp.einsum(
            "astkgd,nbsukd->skgatnbu", grad_heads, values_part, preferred_element_type=full_type
        )
        grad_weights = grad_weights.reshape(weights.shape)
        grad_scores = (
            (weights * (grad_weights - row_dot[..., None])).astype(low_type).reshape(full_shape)
        )
        grad_q = (
            grad_q
            + jnp.einsum(
                "skgatnbu,nbsukd->astkgd", grad_scores, keys_part, preferred_element_type=full_type
            )
            * scale
        )
        piece_k = (
            jnp.einsum(
                "skgatnbu,astkgd->nbsukd", grad_scores, queries, preferred_element_type=full_type
            )
            * scale
        )
        piece_v = jnp.einsum(
            "skgatnbu,astkgd->nbsukd", weights_low, grad_heads, preferred_element_type=full_type
        )
        return (grad_q, piece_k, piece_v)

    def back_fold(carry, piece, start):
        grad_q, grad_k_all, grad_v_all = carry
        grad_q, piece_k, piece_v = piece_grads(grad_q, piece[0], piece[1], start)
        grad_k_all = lax.dynamic_update_slice_in_dim(grad_k_all, piece_k, start, 0)
        grad_v_all = lax.dynamic_update_slice_in_dim(grad_v_all, piece_v, start, 0)
        return (grad_q, grad_k_all, grad_v_all)

    buffer_shape = (blocks_axis,) + keys.shape
    start_carry = (
        jnp.zeros(queries.shape, full_type),
        jnp.zeros(buffer_shape, full_type),
        jnp.zeros(buffer_shape, full_type),
    )
    grad_q, grad_k_all, grad_v_all = local_fold(back_fold, start_carry, kept)
    key_sums = (
        lax.psum_scatter(grad_k_all, "blk", scatter_dimension=0, tiled=True),
        lax.psum_scatter(grad_v_all, "blk", scatter_dimension=0, tiled=True),
    )
    key_grad_sum = key_sums[0][0]
    value_grad_sum = key_sums[1][0]
    grad_stack = jnp.concatenate(
        [grad_q, key_grad_sum[:, :, :, :, None, :], value_grad_sum[:, :, :, :, None, :]], axis=4
    )
    grad_stack = grad_stack.astype(low_type).reshape(
        heads_axis, rows, 1, kv_local * (GROUP + 2) * HEAD_DIM
    )
    grad_projected = lax.all_to_all(
        grad_stack, "head", split_axis=0, concat_axis=2, tiled=True
    ).reshape(rows, qkv_full.shape[1])
    grad_qkv = outer_dot(normed_in, grad_projected)
    grad_normed_in = back_dot(grad_projected, qkv_full)
    scaled_in = grad_normed_in * gain_in
    grad_gain_in = jnp.sum(grad_normed_in * inputs * inverse_in, axis=0)
    grad_inputs = (
        grad_mid_total
        + inverse_in * scaled_in
        - inputs * inverse_in**3 * jnp.mean(scaled_in * inputs, axis=1, keepdims=True)
    )
    token_grad = grad_inputs.reshape(seqs, stretch, width)
    shares = (
        lax.psum_scatter(grad_qkv, ("head", "blk"), scatter_dimension=0, tiled=True),
        lax.psum_scatter(grad_out_w, ("head", "blk"), scatter_dimension=0, tiled=True),
        lax.psum_scatter(grad_shgu, ("head", "blk"), scatter_dimension=0, tiled=True),
        lax.psum_scatter(grad_shdown, ("head", "blk"), scatter_dimension=0, tiled=True),
        lax.psum_scatter(grad_router, ("head", "blk"), scatter_dimension=0, tiled=True),
        lax.psum_scatter(
            jnp.stack([grad_gain_in, grad_gain_mid]),
            ("head", "blk"),
            scatter_dimension=1,
            tiled=True,
        ),
    )
    g_qkv, g_out, g_shgu, g_shdown, g_router, g_gains = shares
    expert_shares = (
        lax.psum_scatter(
            grad_expgu[None].astype(jnp.bfloat16), "head", scatter_dimension=1, tiled=True
        ).astype(jnp.float32),
        lax.psum_scatter(
            grad_expdown[None].astype(jnp.bfloat16), "head", scatter_dimension=1, tiled=True
        ).astype(jnp.float32),
    )
    g_expgu, g_expdown = expert_shares
    local_squares = (
        jnp.sum(g_qkv * g_qkv)
        + jnp.sum(g_out * g_out)
        + jnp.sum(g_shgu * g_shgu)
        + jnp.sum(g_shdown * g_shdown)
        + jnp.sum(g_router * g_router)
        + jnp.sum(g_gains * g_gains)
        + jnp.sum(g_expgu * g_expgu)
        + jnp.sum(g_expdown * g_expdown)
    )
    squares, stat_total = lax.psum((local_squares, stat_sums), ("head", "blk"))
    count = jnp.sum(lengths).astype(full_type) * width
    stats = jnp.sqrt(stat_total / count)
    grad_norm = jnp.sqrt(squares)
    factor = clip_norm / jnp.maximum(grad_norm, clip_norm)
    a_qkv, b_qkv, c_qkv = adam_update(w_qkv, m_qkv, v_qkv, g_qkv, factor)
    a_out, b_out, c_out = adam_update(w_out, m_out, v_out, g_out, factor)
    a_shgu, b_shgu, c_shgu = adam_update(w_shgu, m_shgu, v_shgu, g_shgu, factor)
    a_shdown, b_shdown, c_shdown = adam_update(w_shdown, m_shdown, v_shdown, g_shdown, factor)
    a_router, b_router, c_router = adam_update(w_router, m_router, v_router, g_router, factor)
    a_gains, b_gains, c_gains = adam_update(w_gains, m_gains, v_gains, g_gains, factor)
    a_expgu, b_expgu, c_expgu = adam_update(w_expgu, m_expgu, v_expgu, g_expgu, factor)
    a_expdown, b_expdown, c_expdown = adam_update(
        w_expdown, m_expdown, v_expdown, g_expdown, factor
    )
    return (
        block_out,
        token_grad,
        g_qkv,
        a_qkv,
        b_qkv,
        c_qkv,
        g_out,
        a_out,
        b_out,
        c_out,
        g_shgu,
        a_shgu,
        b_shgu,
        c_shgu,
        g_shdown,
        a_shdown,
        b_shdown,
        c_shdown,
        g_router,
        a_router,
        b_router,
        c_router,
        g_gains,
        a_gains,
        b_gains,
        c_gains,
        g_expgu,
        a_expgu,
        b_expgu,
        c_expgu,
        g_expdown,
        a_expdown,
        b_expdown,
        c_expdown,
        grad_norm,
        stats,
    )


def local_cube(
    tokens,
    cotangent,
    lengths,
    routes,
    w_qkv,
    m_qkv,
    v_qkv,
    w_out,
    m_out,
    v_out,
    w_shgu,
    m_shgu,
    v_shgu,
    w_shdown,
    m_shdown,
    v_shdown,
    w_router,
    m_router,
    v_router,
    w_gains,
    m_gains,
    v_gains,
    w_expgu,
    m_expgu,
    v_expgu,
    w_expdown,
    m_expdown,
    v_expdown,
):
    low_type = jnp.bfloat16
    full_type = jnp.float32
    heads_axis = lax.axis_size("head")
    blocks_axis = lax.axis_size("blk")
    head_index = lax.axis_index("head")
    blk_index = lax.axis_index("blk")
    devices = heads_axis * blocks_axis
    me = head_index * blocks_axis + blk_index
    seqs, stretch, width = tokens.shape
    rows = seqs * stretch
    experts = w_router.shape[1]
    shard = w_qkv.shape[0]
    group_cols = (GROUP + 2) * HEAD_DIM
    query_cols = GROUP * HEAD_DIM
    extra = -(-(experts + 2) // 128) * 128
    tail = -(-2 * experts // 128) * 128
    all_orders = both_orders()
    row_orders = blk_orders()
    head_bits = axis_bits("head")

    small = jnp.concatenate([w_router, w_gains.T], axis=1)
    small = jnp.pad(small, ((0, 0), (0, extra - experts - 2)))
    half_cols = w_qkv.shape[1] // 2
    first_half, second_half, small_full = gather_rows(
        [
            w_qkv[:, :half_cols].astype(low_type),
            w_qkv[:, half_cols:].astype(low_type),
            small.astype(low_type),
        ],
        (all_orders[0], all_orders[1], all_orders[0]),
    )
    router_full = small_full[:, :experts]
    gains_full = small_full[:, experts : experts + 2].astype(full_type)
    gain_in = gains_full[:, 0][None]
    gain_mid = gains_full[:, 1][None]
    out_low = w_out.astype(low_type)
    out_full = lax.all_gather(out_low, ("head", "blk"), axis=0, tiled=True)
    own_pos = me * stretch + jnp.arange(stretch, dtype=jnp.int32)
    valid = (own_pos[None, :] < lengths[:, None]).astype(full_type).reshape(rows, 1)
    limit = jnp.minimum(own_pos[None, :], lengths[:, None] - 1).reshape(rows, 1)
    grad_final = cotangent.astype(full_type).reshape(rows, width) * valid
    grad_low = grad_final.astype(low_type)

    inputs = tokens.astype(full_type).reshape(rows, width)
    inverse_in = lax.rsqrt(jnp.mean(inputs * inputs, axis=1, keepdims=True) + norm_eps)
    normed_in = (inputs * inverse_in * gain_in).astype(low_type)
    projected = [
        jnp.dot(normed_in, half, preferred_element_type=full_type).astype(low_type)
        for half in (first_half, second_half)
    ]
    per_half = KV_HEADS // 2
    by_group = [half.reshape(seqs, stretch, per_half, group_cols) for half in projected]
    queries = [
        [half[s, :, :, :query_cols].reshape(stretch, -1) for half in by_group]
        for s in range(seqs)
    ]
    pairs = gather_relative(
        [
            half[s, :, :, query_cols:].reshape(stretch, -1)
            for s in range(seqs)
            for half in by_group
        ],
        [order for s in range(seqs) for order in all_orders],
        WAVES_KV,
    )
    pairs = [pairs[2 * s : 2 * s + 2] for s in range(seqs)]
    limits = limit.reshape(seqs, stretch, 1)
    key_pos = [
        (block_devices(order)[:, None] * stretch + jnp.arange(stretch, dtype=jnp.int32)).reshape(
            1, -1
        )
        for order in all_orders
    ]

    route_rows = jnp.transpose(routes, (1, 0, 2)).reshape(rows, TOP)
    hits = route_rows[:, :, None] == jnp.arange(experts, dtype=jnp.int32)
    named = jnp.sum(hits.astype(full_type), axis=1)
    early = jnp.concatenate(
        [grad_low, jnp.pad(named, ((0, 0), (0, tail - experts))).astype(low_type)], axis=1
    )
    early_all = lax.all_gather(early, "blk", axis=0, tiled=True).reshape(
        blocks_axis, seqs, stretch, -1
    )

    def to_columns(values, beside):
        spread = gather_relative(values, row_orders, WAVES_COL, beside)
        return [[half.reshape(-1, half.shape[-1]) for half in pair] for pair in spread]

    def rows_of(values):
        return list(values.reshape(seqs, stretch, -1))


    def gather_head(values, *earlier):
        own = values.astype(low_type)[None]
        for step in reversed(head_bits):
            mine = jnp.arange(2).reshape(2, 1, 1, 1) == own_bit(step)
            own = jnp.where(mine, own[None], after(swap(own, step), *earlier)[None])
            own = own.reshape((-1,) + own.shape[2:])
        return own.reshape(-1, values.shape[1])

    def scatter_head(values, *earlier):
        for step in head_bits:
            half = values.shape[0] // 2
            bit = own_bit(step)
            mine = lax.dynamic_slice_in_dim(values, bit * half, half, 0)
            theirs = lax.dynamic_slice_in_dim(values, (1 - bit) * half, half, 0)
            others = after(swap(theirs.astype(low_type), step), *earlier)
            values = mine.astype(full_type) + others.astype(full_type)
        return values

    attended, attended_tok, branch, middle, inverse_mid, normed_mid = [], [], [], [], [], []
    for s in range(seqs):
        asked = queries[s] if s == 0 else after(queries[s], normed_mid[s - 1])
        attended.append(
            [
                attend(query, pair, pos, limits[s])
                for query, pair, pos in zip(asked, pairs[s], key_pos)
            ]
        )
        attended_tok.append(jnp.concatenate([item[1] for item in attended[s]], axis=1))
        branch.append(jnp.dot(attended_tok[s], out_full, preferred_element_type=full_type))
        middle.append(rows_of(inputs)[s] + branch[s])
        squares = jnp.mean(middle[s] * middle[s], axis=1, keepdims=True)
        inverse_mid.append(lax.rsqrt(squares + norm_eps))
        normed_mid.append((middle[s] * inverse_mid[s] * gain_mid).astype(low_type))

    unit = SHARED // devices
    w_shgu_late = after(w_shgu, projected)
    w_expgu_late = after(w_expgu, projected)
    units = 2 * heads_axis * unit
    sliced = jnp.transpose(
        w_shgu_late.astype(low_type).reshape(shard, 2 * heads_axis, blocks_axis, unit), (2, 0, 1, 3)
    ).reshape(blocks_axis, shard, units)
    sliced = gather_head(transpose_blk(sliced).reshape(blocks_axis * shard, units))
    gate_up_full = jnp.concatenate([gather_head(w_expgu_late[0], normed_mid), sliced], axis=1)
    down_full = jnp.concatenate([gather_head(w_expdown[0], projected), gather_head(w_shdown, projected)], axis=0)
    act_rows = -(-down_full.shape[0] // 128) * 128
    down_full = jnp.pad(down_full, ((0, act_rows - down_full.shape[0]), (0, 0)))

    def pull(_):
        flat = early_all.reshape(-1, early_all.shape[-1])[:, :width]
        return back_dot(flat, down_full).reshape(blocks_axis, seqs, stretch, -1)

    found = []
    mid_all = to_columns(normed_mid, ({1: pull}, found))
    pulled = found[0]

    lanes = jnp.arange(tail, dtype=jnp.int32)[None]
    own = jnp.concatenate([lanes == blk_index, lanes == experts + blk_index]).astype(full_type)
    router_wide = jnp.pad(router_full, ((0, 0), (0, tail - experts)))
    places = [blk_blocks(order) for order in row_orders]

    done, back_sums = [], []
    for s in range(seqs):
        mid = mid_all[s] if s == 0 else after(mid_all[s], done[s - 1][0])
        result = run_expert(
            mid, pulled, early_all, router_wide, own, gate_up_full, places[s], s
        )
        done.append(result)
        back_sums.append(
            tuple(item.reshape(blocks_axis // 2, stretch, -1) for item in result[:2])
        )
    acts = [item[2] for item in done]
    hids = [item[3] for item in done]

    def outer_gate_up(before):
        return outer_experts(mid_all, after(hids, before))

    def outer_down(before):
        return outer_acts(after(acts, before), early_all, width)

    def routed(before):
        terms = [
            jnp.dot(act.reshape(-1, act.shape[2]), down_full, preferred_element_type=full_type)
            .astype(low_type)
            .reshape(blocks_axis, stretch, width)
            for act in after(acts, before)
        ]
        return jnp.concatenate(terms, axis=1).reshape(-1, width)

    found = []
    back_sums = scatter_relative(
        back_sums,
        row_orders,
        beside=({1: outer_gate_up, 2: outer_down, 3: routed}, found),
    )
    back_sums = [item.astype(full_type) for item in back_sums]
    grad_gate_up, grad_down, routed_terms = found
    added = lax.psum_scatter(routed_terms, "blk", scatter_dimension=0, tiled=True)

    def sum_rows(values):
        return lax.psum_scatter(
            values.astype(low_type), ("head", "blk"), scatter_dimension=0, tiled=True
        ).astype(full_type)

    def all_gates(values, chosen):
        logits = jnp.dot(values, router_full, preferred_element_type=full_type)
        logits = jnp.where(chosen, logits, masked_score)
        raised = jnp.where(chosen, jnp.exp(logits - jnp.max(logits, axis=1, keepdims=True)), 0.0)
        return raised / jnp.sum(raised, axis=1, keepdims=True)

    chosen = rows_of(named > 0)
    finals = rows_of(grad_final)
    grad_router, grad_gain_mid, grad_mid_total, grad_branch, back = [], [], [], [], []
    for s in range(seqs):
        gates = all_gates(normed_mid[s], chosen[s])
        sums = back_sums[s]
        grad_gates = sums[:, width : width + experts] + (
            sums[:, width + experts : width + 2 * experts]
        )
        grad_logits = gates * (grad_gates - jnp.sum(gates * grad_gates, axis=1, keepdims=True))
        grad_logits = jnp.where(chosen[s], grad_logits, 0.0).astype(low_type)
        grad_router.append(outer_dot(normed_mid[s], grad_logits))
        grad_normed = back_dot(grad_logits, router_full) + sums[:, :width]
        scaled_mid = grad_normed * gain_mid
        grad_gain_mid.append(jnp.sum(grad_normed * middle[s] * inverse_mid[s], axis=0))
        grad_mid_total.append(
            finals[s]
            + inverse_mid[s] * scaled_mid
            - middle[s]
            * inverse_mid[s] ** 3
            * jnp.mean(scaled_mid * middle[s], axis=1, keepdims=True)
        )
        grad_branch.append(grad_mid_total[s].astype(low_type))
        grad_attended = back_dot(grad_branch[s], out_full).astype(low_type)
        cols = per_half * query_cols
        back.append(
            [
                attend_back(
                    queries[s][half],
                    pairs[s][half],
                    key_pos[half],
                    limits[s],
                    grad_attended[:, half * cols : (half + 1) * cols],
                    attended[s][half][0],
                    attended[s][half][2],
                )
                for half in range(2)
            ]
        )
    grad_router = sum(grad_router)
    grad_gain_mid = sum(grad_gain_mid)
    grad_mid_total = jnp.concatenate(grad_mid_total, axis=0)
    g_out = sum_rows(
        outer_dot(jnp.concatenate(attended_tok, axis=0), jnp.concatenate(grad_branch, axis=0))
    )
    g_shgu = scatter_head(grad_gate_up[:, 2 * EXPERT_FF :], grad_branch).astype(low_type)
    g_shgu = transpose_blk(g_shgu.reshape(blocks_axis, shard, units))
    g_shgu = (
        jnp.transpose(
            g_shgu.reshape(blocks_axis, shard, 2 * heads_axis, unit), (1, 2, 0, 3)
        )
        .reshape(w_shgu.shape)
        .astype(full_type)
    )

    pair_sums = scatter_relative(
        [item[1:] for part in back for item in part],
        [order for s in range(seqs) for order in all_orders],
        None,
    )
    grad_halves = [
        jnp.concatenate(
            [
                jnp.concatenate(
                    [
                        back[s][half][0].reshape(stretch, per_half, query_cols),
                        pair_sums[2 * s + half].reshape(stretch, per_half, 2 * HEAD_DIM),
                    ],
                    axis=2,
                ).reshape(stretch, -1)
                for s in range(seqs)
            ],
            axis=0,
        )
        for half in range(2)
    ]
    branch = jnp.concatenate(branch, axis=0)
    middle = jnp.concatenate(middle, axis=0)
    final = middle + added.astype(full_type)
    block_out = final.astype(low_type).reshape(seqs, stretch, width)
    stat_sums = jnp.stack(
        [
            jnp.sum(branch * branch * valid),
            jnp.sum(middle * middle * valid),
            jnp.sum(final * final * valid),
        ]
    )
    grad_halves = after(grad_halves, g_shgu)
    g_expgu = scatter_head(grad_gate_up[:, : 2 * EXPERT_FF], pair_sums[:2])[None]
    g_expdown = scatter_head(grad_down[:EXPERT_FF], pair_sums[:2])[None]
    g_shdown = scatter_head(grad_down[EXPERT_FF : EXPERT_FF + heads_axis * unit], pair_sums[:2])
    grad_normed_in = back_dot(grad_halves[0], first_half) + back_dot(grad_halves[1], second_half)
    scaled_in = grad_normed_in * gain_in
    grad_gain_in = jnp.sum(grad_normed_in * inputs * inverse_in, axis=0)
    grad_inputs = (
        grad_mid_total
        + inverse_in * scaled_in
        - inputs * inverse_in**3 * jnp.mean(scaled_in * inputs, axis=1, keepdims=True)
    )
    token_grad = grad_inputs.reshape(seqs, stretch, width)
    grad_small = jnp.concatenate(
        [grad_router, jnp.stack([grad_gain_in, grad_gain_mid], axis=1)], axis=1
    )
    grad_small = jnp.pad(grad_small, ((0, 0), (0, extra - experts - 2)))
    sums = scatter_rows(
        [outer_dot(normed_in, half).astype(low_type) for half in grad_halves]
        + [grad_small.astype(low_type)],
        (all_orders[0], all_orders[1], all_orders[0]),
    )
    g_qkv = jnp.concatenate(sums[:2], axis=1).astype(full_type)
    g_router = sums[2][:, :experts].astype(full_type)
    g_gains = sums[2][:, experts : experts + 2].astype(full_type).T

    local_squares = (
        jnp.sum(g_qkv * g_qkv)
        + jnp.sum(g_out * g_out)
        + jnp.sum(g_shgu * g_shgu)
        + jnp.sum(g_shdown * g_shdown)
        + jnp.sum(g_router * g_router)
        + jnp.sum(g_gains * g_gains)
        + jnp.sum(g_expgu * g_expgu)
        + jnp.sum(g_expdown * g_expdown)
    )
    scalars = jnp.concatenate([local_squares[None], stat_sums])
    totals = sum_everywhere(jnp.pad(scalars, (0, 124)).reshape(1, 128))[0]
    count = jnp.sum(lengths).astype(full_type) * width
    stats = jnp.sqrt(totals[1:4] / count)
    grad_norm = jnp.sqrt(totals[0])
    factor = clip_norm / jnp.maximum(grad_norm, clip_norm)
    outputs = [block_out, token_grad]
    for weight, first, second, grad in (
        (w_qkv, m_qkv, v_qkv, g_qkv),
        (w_out, m_out, v_out, g_out),
        (w_shgu, m_shgu, v_shgu, g_shgu),
        (w_shdown, m_shdown, v_shdown, g_shdown),
        (w_router, m_router, v_router, g_router),
        (w_gains, m_gains, v_gains, g_gains),
        (w_expgu, m_expgu, v_expgu, g_expgu),
        (w_expdown, m_expdown, v_expdown, g_expdown),
    ):
        outputs.append(grad)
        outputs.extend(adam_update(weight, first, second, grad, factor))
    return (*outputs, grad_norm, stats)


def solution(mesh):
    in_specs = (
        P(None, ("head", "blk"), None),
        P(None, ("head", "blk"), None),
        P(),
        P(("head", "blk"), None, None),
        P(("head", "blk"), None),
        P(("head", "blk"), None),
        P(("head", "blk"), None),
        P(("head", "blk"), None),
        P(("head", "blk"), None),
        P(("head", "blk"), None),
        P(("head", "blk"), None),
        P(("head", "blk"), None),
        P(("head", "blk"), None),
        P(("head", "blk"), None),
        P(("head", "blk"), None),
        P(("head", "blk"), None),
        P(("head", "blk"), None),
        P(("head", "blk"), None),
        P(("head", "blk"), None),
        P(None, ("head", "blk")),
        P(None, ("head", "blk")),
        P(None, ("head", "blk")),
        P("blk", "head", None),
        P("blk", "head", None),
        P("blk", "head", None),
        P("blk", "head", None),
        P("blk", "head", None),
        P("blk", "head", None),
    )
    out_specs = (
        P(None, ("head", "blk"), None),
        P(None, ("head", "blk"), None),
        P(("head", "blk"), None),
        P(("head", "blk"), None),
        P(("head", "blk"), None),
        P(("head", "blk"), None),
        P(("head", "blk"), None),
        P(("head", "blk"), None),
        P(("head", "blk"), None),
        P(("head", "blk"), None),
        P(("head", "blk"), None),
        P(("head", "blk"), None),
        P(("head", "blk"), None),
        P(("head", "blk"), None),
        P(("head", "blk"), None),
        P(("head", "blk"), None),
        P(("head", "blk"), None),
        P(("head", "blk"), None),
        P(("head", "blk"), None),
        P(("head", "blk"), None),
        P(("head", "blk"), None),
        P(("head", "blk"), None),
        P(None, ("head", "blk")),
        P(None, ("head", "blk")),
        P(None, ("head", "blk")),
        P(None, ("head", "blk")),
        P("blk", "head", None),
        P("blk", "head", None),
        P("blk", "head", None),
        P("blk", "head", None),
        P("blk", "head", None),
        P("blk", "head", None),
        P("blk", "head", None),
        P("blk", "head", None),
        P(),
        P(),
    )
    shards = mesh.size
    cubes = all(size & (size - 1) == 0 for size in mesh.shape.values())
    cubes = cubes and mesh.shape["head"] == 2
    step = local_cube if cubes and WIDTH_ROWS % (16 * shards) == 0 else local
    return jax.shard_map(step, mesh=mesh, in_specs=in_specs, out_specs=out_specs, check_vma=False)
```
